32 devices in a mesh: fsdp: 32 (over z, y, x, core).
Axes of the slice: x: 2, y: 2, z: 4, core: 2. Of those that a mesh axis runs over, the one named last changes fastest.
Arguments:
- tokens: bfloat16 [51712, 768], P('fsdp'), may hold values from -6 to 6
- lengths: int32 [256], P('fsdp'), may hold values from 67 to 202, as said below
- feature_directions: float32 [12, 64, 32], replicated, may hold values from -3 to 3
- first_gain: bfloat16 [768], P('fsdp'), may hold values from 0.5 to 1.5
- first_shift: bfloat16 [768], P('fsdp'), may hold values from -2 to 2
- query_weight: bfloat16 [768, 768], P('fsdp'), may hold values from -0.21875 to 0.21875
- key_weight: bfloat16 [768, 768], P('fsdp'), may hold values from -0.21875 to 0.21875
- value_weight: bfloat16 [768, 768], P('fsdp'), may hold values from -0.21875 to 0.21875
- out_weight: bfloat16 [768, 768], P('fsdp'), may hold values from -0.875 to 0.875
- second_gain: bfloat16 [768], P('fsdp'), may hold values from 0.5 to 1.5
- second_shift: bfloat16 [768], P('fsdp'), may hold values from -2 to 2
- up_weight: bfloat16 [768, 3072], P('fsdp'), may hold values from -0.21875 to 0.21875
- down_weight: bfloat16 [3072, 768], P('fsdp'), may hold values from -0.109375 to 0.109375
- out_cotangent: bfloat16 [51712, 768], P('fsdp'), may hold values from -6 to 6
Outputs:
- output: bfloat16 [51712, 768], P('fsdp')
- input_gradient: bfloat16 [51712, 768], P('fsdp')
- first_gain_gradient: float32 [768], P('fsdp')
- first_shift_gradient: float32 [768], P('fsdp')
- query_weight_gradient: float32 [768, 768], P('fsdp')
- key_weight_gradient: float32 [768, 768], P('fsdp')
- value_weight_gradient: float32 [768, 768], P('fsdp')
- out_weight_gradient: float32 [768, 768], P('fsdp')
- second_gain_gradient: float32 [768], P('fsdp')
- second_shift_gradient: float32 [768], P('fsdp')
- up_weight_gradient: float32 [768, 3072], P('fsdp')
- down_weight_gradient: float32 [3072, 768], P('fsdp')
The draws below stay inside these ranges and needn't reach their ends.
Inputs may be any that keep to these rules, and one draw needn't show every extreme that they name: `lengths`: tokens of each molecule; positions at or beyond it are padding; in every draw some molecule has 202 tokens and some has 67.
All inputs are finite; a program needn't handle non-finite values.
Results may differ from the reference program's by a relative error of at most 0.024.
Values may be sent and summed in bfloat16 or wider, within the bound.
A program may use at most 256 MiB of HBM per device.

```python
import jax
import jax.numpy as jnp
from jax import lax

D = 768
HEADS = 12
HEAD_DIM = 64
FEATS = 32
FF = 3072
LEN = 202
SEQS = 256
TOKENS = 51712
N_FSDP = 32


def draw_lengths(key, part):
    key = jax.random.fold_in(key, 7)
    first_key, second_key, third_key = jax.random.split(key, 3)
    counts = jax.random.randint(first_key, (SEQS,), LEN // 3, LEN + 1, dtype=jnp.int32)
    longest = jax.random.randint(second_key, (), 0, SEQS, dtype=jnp.int32)
    shortest = (longest + 1 + jax.random.randint(third_key, (), 0, SEQS - 1, dtype=jnp.int32)) % SEQS
    counts = counts.at[longest].set(LEN)
    counts = counts.at[shortest].set(LEN // 3)
    return counts


def shard_levels(rng, shape, shards, least, top_value):
    gain = 1.0
    for position, parts in shards:
        heights = jax.random.uniform(jax.random.fold_in(jax.random.fold_in(rng, 6), position), (parts,), jnp.float32, least / len(shards), top_value / len(shards))
        gain = gain * jnp.repeat(jnp.exp(heights), shape[position] // parts).reshape((-1,) + (1,) * (len(shape) - 1 - position))
    return gain


def scatter_about(key, shape, width, most, shards=(), kind=jnp.bfloat16):
    level = shard_levels(key, shape, shards, -0.22, 0.18) if shards else 1.0
    array = jax.random.normal(key, shape, jnp.float32) * width * level
    return jnp.minimum(jnp.maximum(array, -most), most).astype(kind)


def setup_inputs(seed: int = 0) -> dict:
    arg_keys = jax.random.split(jax.random.key(seed), 15)
    tokens = scatter_about(arg_keys[0], (TOKENS, D), 1.0, 6.0, ((0, 32),))
    lengths = draw_lengths(jax.random.fold_in(arg_keys[14], 71), 0)
    feature_directions = scatter_about(arg_keys[2], (HEADS, HEAD_DIM, FEATS), 0.5, 3.0, (), jnp.float32)
    first_gain = jnp.clip(1.0 + 0.1 * jax.random.normal(arg_keys[3], (D,), jnp.float32), 0.5, 1.5).astype(jnp.bfloat16)
    first_shift = scatter_about(arg_keys[4], (D,), 0.3, 2.0, ((0, 32),))
    query_weight = scatter_about(arg_keys[5], (D, D), D ** -0.5, 0.21875, ((0, 32),))
    key_weight = scatter_about(arg_keys[6], (D, D), D ** -0.5, 0.21875, ((0, 32),))
    value_weight = scatter_about(arg_keys[7], (D, D), D ** -0.5, 0.21875, ((0, 32),))
    out_weight = scatter_about(arg_keys[8], (D, D), (D // 16) ** -0.5, 0.875, ((0, 32),))
    second_gain = jnp.clip(1.0 + 0.1 * jax.random.normal(arg_keys[9], (D,), jnp.float32), 0.5, 1.5).astype(jnp.bfloat16)
    second_shift = scatter_about(arg_keys[10], (D,), 0.3, 2.0, ((0, 32),))
    up_weight = scatter_about(arg_keys[11], (D, FF), D ** -0.5, 0.21875, ((0, 32),))
    down_weight = scatter_about(arg_keys[12], (FF, D), FF ** -0.5, 0.109375, ((0, 32),))
    out_cotangent = scatter_about(arg_keys[13], (TOKENS, D), 1.0, 6.0, ((0, 32),))
    return {"tokens": tokens, "lengths": lengths, "feature_directions": feature_directions, "first_gain": first_gain, "first_shift": first_shift, "query_weight": query_weight, "key_weight": key_weight, "value_weight": value_weight, "out_weight": out_weight, "second_gain": second_gain, "second_shift": second_shift, "up_weight": up_weight, "down_weight": down_weight, "out_cotangent": out_cotangent}


@jax.custom_vjp
def low(v):
    return lax.optimization_barrier(v.astype(jnp.bfloat16)).astype(jnp.float32)

@jax.custom_vjp
def low_back(v):
    return v

def low_keep(v):
    return (low(v), None)

def low_pass(kept, grad):
    return (grad,)

def back_keep(v):
    return (v, None)

def back_low(kept, grad):
    return (low(grad),)
low.defvjp(low_keep, low_pass)
low_back.defvjp(back_keep, back_low)

def matmul(left_rows, right_rows):
    return jnp.dot(left_rows, right_rows, precision=lax.Precision.HIGHEST)

def rotate_scale(vectors):
    half_size = vectors.shape[-1] // 2
    positions = jnp.arange(vectors.shape[1], dtype=jnp.float32)
    frequency = 10000.0 ** (-jnp.arange(half_size, dtype=jnp.float32) * 2.0 / vectors.shape[-1])
    angles = positions[:, None] * frequency[None, :]
    cosine_table = jnp.cos(angles)[None, :, None, :]
    sine_table = jnp.sin(angles)[None, :, None, :]
    first_half = vectors[..., :half_size]
    second_half = vectors[..., half_size:]
    turned = jnp.concatenate([first_half * cosine_table - second_half * sine_table, first_half * sine_table + second_half * cosine_table], -1)
    return turned * vectors.shape[-1] ** (-0.25)

def feature_map(vectors, directions):
    turned = rotate_scale(vectors)
    logits = jnp.einsum('slhd,hdm->slhm', turned, directions, precision=lax.Precision.HIGHEST)
    logits = logits - 0.5 * lax.optimization_barrier(jnp.sum(turned * turned, -1, keepdims=True))
    return jnp.exp(logits) * directions.shape[-1] ** (-0.5)

def layer_norm(inputs, gain_row, shift_row):
    row_mean = lax.optimization_barrier(jnp.mean(inputs, -1, keepdims=True))
    centered = inputs - row_mean
    inverse = lax.rsqrt(lax.optimization_barrier(jnp.mean(centered * centered, -1, keepdims=True)) + 1e-05)
    return centered * inverse * gain_row + shift_row

def smooth_gelu(values):
    return jax.nn.gelu(values, approximate=True)

def layer_block(parameters, inputs, group_lengths, directions):
    first_gain, first_shift, query_weight, key_weight, value_weight, out_weight, second_gain, second_shift, up_weight, down_weight = parameters
    head_count = directions.shape[0]
    model_width = inputs.shape[1]
    seqs_here = group_lengths.shape[0]

    def split_heads(row_block):
        return row_block.reshape(seqs_here, -1, head_count, model_width // head_count)
    normed = low(layer_norm(inputs, first_gain, first_shift))
    query_rows = low_back(matmul(normed, query_weight))
    key_rows = low_back(matmul(normed, key_weight))
    value_rows = low(low_back(matmul(normed, value_weight)))
    query_feats = low(feature_map(split_heads(query_rows), directions))
    key_feats = low(feature_map(split_heads(key_rows), directions))
    positions = jnp.arange(key_feats.shape[1], dtype=jnp.int32)
    key_live = (positions[None, :] < group_lengths[:, None]).astype(jnp.float32)
    masked = key_feats * key_live[:, :, None, None]
    state_sum = low(low_back(jnp.einsum('slhm,slhd->shmd', masked, split_heads(value_rows), precision=lax.Precision.HIGHEST)))
    totals = lax.optimization_barrier(jnp.sum(masked, 1))
    numerator = low_back(jnp.einsum('slhm,shmd->slhd', query_feats, state_sum, precision=lax.Precision.HIGHEST))
    denominator = jnp.einsum('slhm,shm->slh', query_feats, totals, precision=lax.Precision.HIGHEST)
    mixed_rows = low((numerator / denominator[..., None]).reshape(-1, model_width))
    branch = low_back(matmul(mixed_rows, out_weight))
    middle = inputs + branch
    second = low(layer_norm(middle, second_gain, second_shift))
    hidden = low(smooth_gelu(low_back(matmul(second, up_weight))))
    return middle + matmul(hidden, down_weight)

def reference(tokens, lengths, feature_directions, first_gain, first_shift, query_weight, key_weight, value_weight, out_weight, second_gain, second_shift, up_weight, down_weight, out_cotangent):
    parameters = tuple((weight_arg.astype(jnp.float32) for weight_arg in (first_gain, first_shift, query_weight, key_weight, value_weight, out_weight, second_gain, second_shift, up_weight, down_weight)))
    inputs = tokens.astype(jnp.float32)
    directions = feature_directions.astype(jnp.float32)
    model_width = inputs.shape[1]
    group_lengths = lengths.reshape(N_FSDP, -1)

    def forward(weights_all, layer_input):
        grouped = layer_input.reshape(N_FSDP, -1, model_width)

        def one_group(pair):
            return layer_block(weights_all, pair[0], pair[1], directions)
        results = lax.map(jax.checkpoint(one_group), (grouped, group_lengths))
        return results.reshape(-1, model_width)
    output, pullback = jax.vjp(forward, parameters, inputs)
    weight_grads, input_grad = pullback(out_cotangent.astype(jnp.float32))
    return (output.astype(jnp.bfloat16), input_grad.astype(jnp.bfloat16), weight_grads[0], weight_grads[1], weight_grads[2], weight_grads[3], weight_grads[4], weight_grads[5], weight_grads[6], weight_grads[7], weight_grads[8], weight_grads[9])
```

```python
import functools

import jax
import jax.numpy as jnp
import numpy as np
from jax import lax
from jax.experimental import pallas as pl
from jax.experimental.pallas import tpu as pltpu
from jax.sharding import PartitionSpec as P

F32 = jnp.float32
BF16 = jnp.bfloat16


def rotate_scale(vectors):
    half_size = vectors.shape[-1] // 2
    positions = jnp.arange(vectors.shape[1], dtype=jnp.float32)
    frequency = 10000.0 ** (-jnp.arange(half_size, dtype=jnp.float32) * 2.0 / vectors.shape[-1])
    angles = positions[:, None] * frequency[None, :]
    cosine_table = jnp.cos(angles)[None, :, None, :]
    sine_table = jnp.sin(angles)[None, :, None, :]
    first_half = vectors[..., :half_size]
    second_half = vectors[..., half_size:]
    turned = jnp.concatenate(
        [
            first_half * cosine_table - second_half * sine_table,
            first_half * sine_table + second_half * cosine_table,
        ],
        -1,
    )
    return turned * vectors.shape[-1] ** (-0.25)


def feature_map(vectors, directions):
    turned = rotate_scale(vectors)
    logits = jnp.einsum("slhd,hdm->slhm", turned, directions, precision=lax.Precision.HIGHEST)
    logits = logits - 0.5 * jnp.sum(turned * turned, -1, keepdims=True)
    return jnp.exp(logits) * directions.shape[-1] ** (-0.5)


def smooth_gelu(values):
    return jax.nn.gelu(values, approximate=True)


def norm_parts(inputs, gain_row, shift_row):
    row_mean = jnp.mean(inputs, -1, keepdims=True)
    centered = inputs - row_mean
    inverse = lax.rsqrt(jnp.mean(centered * centered, -1, keepdims=True) + 1e-05)
    hat_rows = centered * inverse
    return (
        hat_rows * gain_row.astype(jnp.float32) + shift_row.astype(jnp.float32),
        hat_rows,
        inverse,
    )


def norm_back(grad_rows, hat_rows, inverse, gain_row):
    scaled = grad_rows * gain_row.astype(jnp.float32)
    return inverse * (
        scaled
        - jnp.mean(scaled, -1, keepdims=True)
        - hat_rows * jnp.mean(scaled * hat_rows, -1, keepdims=True)
    )


def per_device(
    tokens,
    lengths,
    feature_directions,
    first_gain,
    first_shift,
    query_weight,
    key_weight,
    value_weight,
    out_weight,
    second_gain,
    second_shift,
    up_weight,
    down_weight,
    out_cotangent,
):
    model_width = tokens.shape[1]
    head_count = feature_directions.shape[0]
    head_size = model_width // head_count
    seqs_here = lengths.shape[0]
    length = tokens.shape[0] // seqs_here
    inputs = tokens.astype(jnp.float32)

    def feature_of(row_block):
        return feature_map(
            row_block.reshape(seqs_here, length, head_count, head_size), feature_directions
        )

    gain_one, shift_one, query_full, key_full, value_full, out_full = (
        lax.all_gather(first_gain, "fsdp", axis=0, tiled=True),
        lax.all_gather(first_shift, "fsdp", axis=0, tiled=True),
        lax.all_gather(query_weight, "fsdp", axis=0, tiled=True),
        lax.all_gather(key_weight, "fsdp", axis=0, tiled=True),
        lax.all_gather(value_weight, "fsdp", axis=0, tiled=True),
        lax.all_gather(out_weight, "fsdp", axis=0, tiled=True),
    )
    normed_wide, hat_one, inverse_one = norm_parts(inputs, gain_one, shift_one)
    normed = normed_wide.astype(jnp.bfloat16)
    query_rows = jnp.dot(normed, query_full, preferred_element_type=jnp.float32)
    key_rows = jnp.dot(normed, key_full, preferred_element_type=jnp.float32)
    value_rows = jnp.dot(normed, value_full, preferred_element_type=jnp.float32)
    value_low = value_rows.astype(jnp.bfloat16).reshape(seqs_here, length, head_count, head_size)
    query_raw, query_back = jax.vjp(feature_of, query_rows)
    key_raw, key_back = jax.vjp(feature_of, key_rows)
    query_low = query_raw.astype(jnp.bfloat16)
    key_low = key_raw.astype(jnp.bfloat16)
    positions = jnp.arange(length, dtype=jnp.int32)
    key_live = positions[None, :] < lengths[:, None]
    masked = key_low * key_live.astype(jnp.bfloat16)[:, :, None, None]
    state_sum = jnp.einsum("slhm,slhd->shmd", masked, value_low, preferred_element_type=jnp.float32)
    state_low = state_sum.astype(jnp.bfloat16)
    totals = jnp.sum(masked.astype(jnp.float32), 1)
    numerator = jnp.einsum(
        "slhm,shmd->slhd", query_low, state_low, preferred_element_type=jnp.float32
    )
    query_wide = query_low.astype(jnp.float32)
    denominator = jnp.einsum("slhm,shm->slh", query_wide, totals, precision=lax.Precision.HIGHEST)
    mixed_rows = (numerator / denominator[..., None]).reshape(-1, model_width).astype(jnp.bfloat16)
    branch = jnp.dot(mixed_rows, out_full, preferred_element_type=jnp.float32)
    middle = inputs + branch
    gain_two, shift_two, up_full, down_full = (
        lax.all_gather(second_gain, "fsdp", axis=0, tiled=True),
        lax.all_gather(second_shift, "fsdp", axis=0, tiled=True),
        lax.all_gather(up_weight, "fsdp", axis=0, tiled=True),
        lax.all_gather(down_weight, "fsdp", axis=0, tiled=True),
    )
    second_wide, hat_two, inverse_two = norm_parts(middle, gain_two, shift_two)
    second = second_wide.astype(jnp.bfloat16)
    up_rows = jnp.dot(second, up_full, preferred_element_type=jnp.float32)
    gelu_rows, gelu_back = jax.vjp(smooth_gelu, up_rows)
    hidden = gelu_rows.astype(jnp.bfloat16)
    output = (middle + jnp.dot(hidden, down_full, preferred_element_type=jnp.float32)).astype(
        jnp.bfloat16
    )
    gain_two, shift_two, up_full, down_full = (
        lax.all_gather(second_gain, "fsdp", axis=0, tiled=True),
        lax.all_gather(second_shift, "fsdp", axis=0, tiled=True),
        lax.all_gather(up_weight, "fsdp", axis=0, tiled=True),
        lax.all_gather(down_weight, "fsdp", axis=0, tiled=True),
    )
    gain_one, shift_one, query_full, key_full, value_full, out_full = (
        lax.all_gather(first_gain, "fsdp", axis=0, tiled=True),
        lax.all_gather(first_shift, "fsdp", axis=0, tiled=True),
        lax.all_gather(query_weight, "fsdp", axis=0, tiled=True),
        lax.all_gather(key_weight, "fsdp", axis=0, tiled=True),
        lax.all_gather(value_weight, "fsdp", axis=0, tiled=True),
        lax.all_gather(out_weight, "fsdp", axis=0, tiled=True),
    )
    down_grad = jnp.einsum("tf,td->fd", hidden, out_cotangent, preferred_element_type=jnp.float32)
    hidden_grad = jnp.einsum(
        "td,fd->tf", out_cotangent, down_full, preferred_element_type=jnp.float32
    )
    pre_grad = gelu_back(hidden_grad)[0].astype(jnp.bfloat16)
    up_grad = jnp.einsum("td,tf->df", second, pre_grad, preferred_element_type=jnp.float32)
    second_grad = jnp.einsum("tf,df->td", pre_grad, up_full, preferred_element_type=jnp.float32)
    gain_two_grad = jnp.sum(second_grad * hat_two, 0)
    shift_two_grad = jnp.sum(second_grad, 0)
    middle_grad = out_cotangent.astype(jnp.float32) + norm_back(
        second_grad, hat_two, inverse_two, gain_two
    )
    ffn_shards = (
        lax.psum_scatter(gain_two_grad, "fsdp", scatter_dimension=0, tiled=True),
        lax.psum_scatter(shift_two_grad, "fsdp", scatter_dimension=0, tiled=True),
        lax.psum_scatter(up_grad, "fsdp", scatter_dimension=0, tiled=True),
        lax.psum_scatter(down_grad, "fsdp", scatter_dimension=0, tiled=True),
    )
    branch_grad = middle_grad.astype(jnp.bfloat16)
    out_grad = jnp.einsum("td,te->de", mixed_rows, branch_grad, preferred_element_type=jnp.float32)
    mixed_grad = jnp.einsum("te,de->td", branch_grad, out_full, preferred_element_type=jnp.float32)
    mixed_grad = mixed_grad.reshape(seqs_here, length, head_count, head_size)
    numer_grad = (mixed_grad / denominator[..., None]).astype(jnp.bfloat16)
    denom_grad = -jnp.sum(mixed_grad * numerator, -1) / (denominator * denominator)
    query_feat_grad = jnp.einsum(
        "slhd,shmd->slhm", numer_grad, state_low, preferred_element_type=jnp.float32
    )
    query_feat_grad = query_feat_grad + denom_grad[..., None] * totals[:, None]
    state_grad = jnp.einsum(
        "slhm,slhd->shmd", query_low, numer_grad, preferred_element_type=jnp.float32
    ).astype(jnp.bfloat16)
    totals_grad = jnp.einsum(
        "slh,slhm->shm", denom_grad, query_wide, precision=lax.Precision.HIGHEST
    )
    key_feat_grad = jnp.einsum(
        "slhd,shmd->slhm", value_low, state_grad, preferred_element_type=jnp.float32
    )
    key_feat_grad = (key_feat_grad + totals_grad[:, None]) * key_live.astype(jnp.float32)[
        :, :, None, None
    ]
    value_grad = jnp.einsum(
        "slhm,shmd->slhd", masked, state_grad, preferred_element_type=jnp.float32
    )
    value_grad = value_grad.reshape(-1, model_width).astype(jnp.bfloat16)
    query_grad = query_back(query_feat_grad)[0].astype(jnp.bfloat16)
    key_grad = key_back(key_feat_grad)[0].astype(jnp.bfloat16)
    normed_grad = jnp.einsum(
        "te,de->td", query_grad, query_full, preferred_element_type=jnp.float32
    )
    normed_grad = normed_grad + jnp.einsum(
        "te,de->td", key_grad, key_full, preferred_element_type=jnp.float32
    )
    normed_grad = normed_grad + jnp.einsum(
        "te,de->td", value_grad, value_full, preferred_element_type=jnp.float32
    )
    query_weight_grad = jnp.einsum(
        "td,te->de", normed, query_grad, preferred_element_type=jnp.float32
    )
    key_weight_grad = jnp.einsum("td,te->de", normed, key_grad, preferred_element_type=jnp.float32)
    value_weight_grad = jnp.einsum(
        "td,te->de", normed, value_grad, preferred_element_type=jnp.float32
    )
    gain_one_grad = jnp.sum(normed_grad * hat_one, 0)
    shift_one_grad = jnp.sum(normed_grad, 0)
    input_grad = middle_grad + norm_back(normed_grad, hat_one, inverse_one, gain_one)
    attn_shards = (
        lax.psum_scatter(gain_one_grad, "fsdp", scatter_dimension=0, tiled=True),
        lax.psum_scatter(shift_one_grad, "fsdp", scatter_dimension=0, tiled=True),
        lax.psum_scatter(query_weight_grad, "fsdp", scatter_dimension=0, tiled=True),
        lax.psum_scatter(key_weight_grad, "fsdp", scatter_dimension=0, tiled=True),
        lax.psum_scatter(value_weight_grad, "fsdp", scatter_dimension=0, tiled=True),
        lax.psum_scatter(out_grad, "fsdp", scatter_dimension=0, tiled=True),
    )
    shards = tuple(attn_shards) + tuple(ffn_shards)
    return (output, input_grad.astype(jnp.bfloat16)) + shards


def dot_nn(a, b):
    return lax.dot_general(a, b, (((1,), (0,)), ((), ())), preferred_element_type=F32)


def dot_nt(a, b):
    return lax.dot_general(a, b, (((1,), (1,)), ((), ())), preferred_element_type=F32)


def dot_tn(a, b):
    return lax.dot_general(a, b, (((0,), (0,)), ((), ())), preferred_element_type=F32)


def split_low(v):
    high = v.astype(BF16)
    return high, (v - high.astype(F32)).astype(BF16)


def remote(src, dst, send, recv, device):
    return pltpu.make_async_remote_copy(
        src_ref=src,
        dst_ref=dst,
        send_sem=send,
        recv_sem=recv,
        device_id=(device,),
        device_id_type=pl.DeviceIdType.MESH,
    )


class Place:
    def __init__(self):
        me = lax.axis_index("fsdp")
        self.c = lax.rem(me, 2)
        self.x = lax.rem(lax.div(me, 2), 2)
        self.y = lax.rem(lax.div(me, 4), 2)
        self.z = lax.div(me, 8)
        self.sib = me + 1 - 2 * self.c
        self.px = me + 2 - 4 * self.x
        self.py = me + 4 - 8 * self.y
        self.zs = [lax.rem(self.z + d, 4) for d in (1, 2, 3)]
        self.pz = [me + (zp - self.z) * 8 for zp in self.zs]

    def enter(self):
        barrier = pltpu.get_barrier_semaphore()
        peers = [self.sib, self.px, self.py] + self.pz
        for peer in peers:
            pl.semaphore_signal(
                barrier, inc=1, device_id=(peer,), device_id_type=pl.DeviceIdType.MESH
            )
        pl.semaphore_wait(barrier, len(peers))


class Gather:
    def __init__(self, at, buf, send, recv, y_first):
        self.buf, self.send, self.recv = buf, send, recv
        c, z, y, x = at.c, at.z, at.y, at.x
        mine = buf.at[c, z, y, x]
        line = buf.at[c, :, y, x]
        plane = buf.at[c, :, :, x] if y_first else buf.at[c, :, y]
        first, second = (at.py, at.px) if y_first else (at.px, at.py)
        self.copies = [
            [remote(mine, mine, send.at[d], recv.at[d], at.pz[d]) for d in range(3)],
            [remote(line, line, send.at[3], recv.at[3], first)],
            [remote(plane, plane, send.at[4], recv.at[4], second)],
            [remote(buf.at[c], buf.at[c], send.at[5], recv.at[5], at.sib)],
        ]

    def start(self, phase):
        for copy in self.copies[phase]:
            copy.start()

    def arrived(self, phase):
        for copy in self.copies[phase]:
            copy.wait_recv()

    def sent(self):
        for phase in self.copies:
            for copy in phase:
                copy.wait_send()


class Reduce:
    def __init__(self, at, refs, send, recv, kind, y_first, posted=None):
        self.posted = posted
        self.at, self.kind, self.y_first = at, kind, y_first
        self.R, self.B1, self.S, self.B2, self.S2, self.B3, self.S3, self.B4 = refs[:8]
        self.extra = refs[8:]
        self.send, self.recv = send, recv

    def copies(self, phase, par, y_first):
        at, s, r = self.at, self.send.at[par], self.recv.at[par]
        if phase == 0:
            return [remote(self.R.at[1 - at.c], self.B1.at[par], s.at[0], r.at[0], at.sib)]
        if phase == 1:
            src = self.S.at[:, 1 - at.y] if y_first else self.S.at[:, :, 1 - at.x]
            return [remote(src, self.B2.at[par], s.at[1], r.at[1], at.py if y_first else at.px)]
        if phase == 2:
            src = self.S2.at[:, 1 - (at.x if y_first else at.y)]
            return [remote(src, self.B3.at[par], s.at[2], r.at[2], at.px if y_first else at.py)]
        if phase == 3:
            return [
                remote(self.S3.at[at.zs[d]], self.B4.at[par, d], s.at[3 + d], r.at[3 + d], at.pz[d])
                for d in range(3)
            ]
        return []

    def post(self, par, unit):
        flat, out = self.extra
        at = self.at
        return remote(
            flat.at[par, 1 - at.c],
            out.at[unit, at.c],
            self.posted[0].at[unit],
            self.posted[1].at[unit],
            at.sib,
        )

    def start(self, phase, par, y_first=None):
        y_first = self.y_first if y_first is None else y_first
        for copy in self.copies(phase, par, y_first):
            copy.start()

    def wait_sent(self, phase, par, y_first=None):
        y_first = self.y_first if y_first is None else y_first
        for copy in self.copies(phase, par, y_first):
            copy.wait_send()

    def step(self, phase, unit, par, y_first=None, before=True):
        y_first = self.y_first if y_first is None else y_first
        at = self.at
        for copy in self.copies(phase - 1, par, y_first):
            copy.wait_recv()
        if phase < 4:
            if before is True:
                self.wait_sent(phase, 1 - par, y_first)
            elif before is not False:

                @pl.when(before)
                def _():
                    self.wait_sent(phase, 1 - par, y_first)

        kind = self.S.dtype
        if phase == 1:

            def add1(i, _):
                own = self.R[at.c, i].astype(F32) + self.B1[par, i].astype(F32)
                self.S[i] = own.astype(kind)
                return 0

            lax.fori_loop(0, 4, add1, 0)
        elif phase == 2:

            def add2(i, _):
                own = self.S[i, at.y] if y_first else self.S[i, :, at.x]
                self.S2[i] = (own.astype(F32) + self.B2[par, i].astype(F32)).astype(kind)
                return 0

            lax.fori_loop(0, 4, add2, 0)
        elif phase == 3:
            keep = at.x if y_first else at.y

            def add3(i, _):
                own = self.S2[i, keep].astype(F32) + self.B3[par, i].astype(F32)
                self.S3[i] = own.astype(kind)
                return 0

            lax.fori_loop(0, 4, add3, 0)
        else:
            total = self.S3[at.z].astype(F32)
            for d in range(3):
                total = total + self.B4[par, d].astype(F32)
            if self.kind == "pair":
                flat, out = self.extra
                flat[par] = total.reshape(flat.shape[1:])
                out[unit, at.c] = flat[par, at.c]
                self.post(par, unit).start()
            else:
                self.extra[0][unit] = total
            return
        self.start(phase, par, y_first)


def layer_kernel(
    sizes,
    x_hbm,
    dy_hbm,
    lengths,
    params_here,
    wide_here,
    down_here,
    cosine,
    sine,
    feats,
    ones_rot,
    ones_val,
    diagonal,
    out_hbm,
    dx_hbm,
    wide_out,
    down_out,
    params_out,
    wu,
    wd,
    pb,
    px32,
    xb,
    normed,
    rotq,
    rotk,
    vv,
    pq,
    pk,
    mixed,
    second,
    hat2,
    inv2,
    acc,
    dsec,
    hid,
    dpre,
    tb,
    prm,
    lng,
    ru,
    b1u,
    su,
    b2u,
    s2u,
    b3u,
    s3u,
    b4u,
    flu,
    rd,
    b1d,
    sd,
    b2d,
    s2d,
    b3d,
    s3d,
    b4d,
    rp,
    b1p,
    sp,
    b2p,
    s2p,
    b3p,
    s3p,
    b4p,
    res_u,
    res_d,
    res_p,
    ag_send,
    ag_recv,
    pre_send,
    pre_recv,
    us,
    ur,
    ds_,
    dr,
    ps,
    pr,
    qs,
    qr,
    local,
):
    tokens_here, padded, length, mols = sizes
    spare = padded - tokens_here
    at = Place()
    load_x = pltpu.make_async_copy(x_hbm, xb.at[pl.ds(0, tokens_here)], local.at[0])
    load_dy = pltpu.make_async_copy(dy_hbm, xb.at[pl.ds(0, tokens_here)], local.at[0])
    load_wide = pltpu.make_async_copy(wide_here, res_u, local.at[1])
    load_wide.start()
    load_x.start()
    at.enter()
    load_wide.wait()

    swap = remote(res_u.at[:, 1 - at.c], px32, pre_send, pre_recv, at.sib)
    swap.start()
    pb[at.c, at.z, at.y, at.x] = params_here[...]
    for ch in range(6):
        wd[ch, at.c, at.z, at.y, at.x] = down_here[16 * ch : 16 * ch + 16, :]
    tail = pl.ds(tokens_here, spare)
    xb[tail, :] = jnp.zeros((spare, xb.shape[1]), BF16)
    mixed[tail, :] = jnp.zeros((spare, xb.shape[1]), BF16)
    lng[...] = jnp.zeros(lng.shape, F32)
    swap.wait()
    even = at.c == 0

    def build(u, _):
        mine = res_u[u, at.c]
        other = px32[u]
        top = jnp.where(even, mine, other)
        low = jnp.where(even, other, mine)
        wu[u, at.c, at.z, at.y, at.x] = jnp.concatenate([top, low], 0).astype(BF16)
        return 0

    lax.fori_loop(0, 12, build, 0)

    def gather_unit(u):
        if u < 6:
            buf = wu.at[u]
        else:
            buf = wu.at[6 + (u - 6) // 2] if u % 2 == 0 else wd.at[(u - 6) // 2]
        return Gather(at, buf, ag_send.at[u], ag_recv.at[u], u % 2 == 0)

    units = [gather_unit(u) for u in range(18)]
    params = Gather(at, pb, ag_send.at[18], ag_recv.at[18], True)
    state = {"tick": 0, "needed": set()}

    def tick(count=1):
        for _ in range(count):
            t = state["tick"]
            state["tick"] += 1
            if t == 0:
                params.start(0)
            if t < 18:
                units[t].start(0)
            for k in (1, 2, 3):
                u = t - k
                if u == 0:
                    params.arrived(k - 1)
                    params.start(k)
                if 0 <= u < 18:
                    units[u].arrived(k - 1)
                    units[u].start(k)

    def need(u):
        while state["tick"] <= u + 3:
            tick()
        if u not in state["needed"]:
            state["needed"].add(u)
            units[u].arrived(3)

    tick(4)
    params.arrived(3)
    parts = [jnp.zeros((8, 128), F32) for _ in range(7)]
    for i in range(32):
        block = pb[i % 2, i // 8, (i // 4) % 2, (i // 2) % 2]
        k, shift = (24 * i) // 128, (24 * i) % 128
        pair = jnp.concatenate([block, jnp.zeros((8, 128), F32)], 1)
        if shift:
            pair = pltpu.roll(pair, shift, 1)
        parts[k] = parts[k] + pair[:, :128]
        parts[k + 1] = parts[k + 1] + pair[:, 128:]
    prm[...] = jnp.concatenate(parts[:6], 1)

    def rows(i, count):
        return pl.ds(pl.multiple_of(i * count, 16), count)

    def norm(v):
        centered = v - jnp.mean(v, -1, keepdims=True)
        inverse = lax.rsqrt(jnp.mean(centered * centered, -1, keepdims=True) + 1e-05)
        return centered * inverse, inverse

    load_x.wait()

    def first_norm(i, _):
        r = rows(i, 208)
        hat, _ = norm(xb[r, :].astype(F32))
        normed[r, :] = (hat * prm[0:1, :] + prm[1:2, :]).astype(BF16)
        return 0

    lax.fori_loop(0, padded // 208, first_norm, 0)

    def block(b):
        return wu[b // 2, b % 2].reshape(768, 256)

    def features(base, rot_ref, feat_ref):
        def body(i, _):
            r = rows(i, 416)
            lines = normed[r, :]
            ct, st = cosine[r, :], sine[r, :]
            for g in range(3):
                u = dot_nn(lines, block(base + g))
                a, b = u[:, :128], u[:, 128:]
                rot = jnp.concatenate([a * ct - b * st, a * st + b * ct], 1)
                high, low = split_low(rot)
                sq_high, sq_low = split_low(rot * rot)
                two = dot_nn(high, feats[g])
                logits = two[:, :128] + two[:, 128:] + dot_nn(low, feats[g, :, :128])
                norms = dot_nn(sq_high, ones_rot[...]) + dot_nn(sq_low, ones_rot[...])
                p = jnp.exp(logits - 0.5 * norms) * (32**-0.5)
                rot_ref[r, 256 * g : 256 * g + 256] = high
                feat_ref[r, 128 * g : 128 * g + 128] = p.astype(BF16)
            return 0

        lax.fori_loop(0, padded // 416, body, 0)

    need(0)
    need(1)
    features(0, rotk, pk)
    need(2)

    def values(i, _):
        r = rows(i, 416)
        for g in range(3):
            vv[r, 256 * g : 256 * g + 256] = dot_nn(normed[r, :], block(3 + g)).astype(BF16)
        return 0

    lax.fori_loop(0, padded // 416, values, 0)
    need(3)
    need(4)
    features(6, rotq, pq)
    tick(2)

    window = 224

    def places(s):
        begin = lax.div(s * length, 16) * 16
        pos = lax.broadcasted_iota(jnp.int32, (window, 1), 0) - (s * length - begin)
        valid = (pos >= 0) & (pos < length)
        live = valid & (pos < lengths[s])
        return pl.ds(pl.multiple_of(begin, 16), window), pos, valid, live

    def state_of(g, w, live, pkm):
        ones = jnp.ones((window, 256), BF16)
        diag = diagonal[...]
        st = (dot_tn(pkm, vv[w, 256 * g : 256 * g + 256]) * diag).astype(BF16)
        tot = dot_tn(pkm, ones) * diag
        tot_high, tot_low = split_low(tot)
        return st, tot_high, tot_low

    def masked_keys(g, w, live):
        keys = pk[w, 128 * g : 128 * g + 128].astype(F32)
        return jnp.where(live, keys, 0.0)

    def attend(s, _):
        w, pos, valid, live = places(s)
        for g in range(3):
            pkm = masked_keys(g, w, live).astype(BF16)
            st, tot_high, tot_low = state_of(g, w, live, pkm)
            pqg = pq[w, 128 * g : 128 * g + 128]
            num = dot_nn(pqg, st)
            den = dot_nn(pqg, tot_high) + dot_nn(pqg, tot_low)
            mix = jnp.where(valid, num / den, 0.0)
            col = slice(256 * g, 256 * g + 256)
            old = mixed[w, col].astype(F32)
            mixed[w, col] = jnp.where(pos < 0, old, mix).astype(BF16)
        return 0

    lax.fori_loop(0, mols // 2, attend, 0)
    tick(3)
    lax.fori_loop(mols // 2, mols, attend, 0)
    need(5)
    tick(2)

    def project(i, _):
        r = rows(i, 208)
        lines = mixed[r, :]
        branch = jnp.concatenate([dot_nn(lines, block(9 + g)) for g in range(3)], 1)
        middle = xb[r, :].astype(F32) + branch
        acc[r, :] = middle
        hat, inverse = norm(middle)
        hat2[r, :] = hat.astype(BF16)
        inv2[r, :] = jnp.broadcast_to(inverse, (208, 128))
        second[r, :] = (hat * prm[2:3, :] + prm[3:4, :]).astype(BF16)
        dsec[r, :] = jnp.zeros((208, 768), F32)
        return 0

    lax.fori_loop(0, padded // 208, project, 0)

    def turn(src):
        for j in range(6):
            tb[128 * j : 128 * j + 128, :] = src[:, 128 * j : 128 * j + 128].T

    load_dy.start()
    turn(second)
    load_dy.wait()
    for u in range(18):
        need(u)

    lane_u = Reduce(at, (ru, b1u, su, b2u, s2u, b3u, s3u, b4u, flu, res_u), us, ur, "pair", True, (qs, qr))
    lane_d = Reduce(at, (rd, b1d, sd, b2d, s2d, b3d, s3d, b4d, res_d), ds_, dr, "own", False)

    slope = 0.7978845608028654
    bend = 0.044715

    def chunk(ch, _):
        def inner(i, _):
            r = rows(i, 416)
            lines, cot = second[r, :], xb[r, :]
            for h in range(2):
                pre = dot_nn(lines, wu[6 + ch, h].reshape(768, 256))
                dh = dot_nt(cot, wd[ch, h].reshape(256, 768))
                square = pre * pre
                t = jnp.tanh(pre * (slope + slope * bend * square))
                half = 0.5 + 0.5 * t
                col = slice(256 * h, 256 * h + 256)
                hid[r, col] = (pre * half).astype(BF16)
                bent = slope + 3.0 * slope * bend * square
                grad = half + 0.5 * pre * (1.0 - t * t) * bent
                dpre[r, col] = (dh * grad).astype(BF16)
            return 0

        lax.fori_loop(0, padded // 416, inner, 0)
        par = lax.rem(ch, 2)
        for phase in (4, 3, 2, 1):
            j = ch - phase

            @pl.when(j >= 0)
            def _():
                old = lax.rem(j + 8, 2)
                if phase == 4:

                    @pl.when(j >= 2)
                    def _():
                        lane_u.post(old, j - 2).wait_send()

                lane_u.step(phase, j, old, before=j >= 1)
                lane_d.step(phase, j, old, before=j >= 1)

        @pl.when(ch >= 1)
        def _():
            lane_u.wait_sent(0, 1 - par)
            lane_d.wait_sent(0, 1 - par)

        for h in range(2):
            col = slice(256 * h, 256 * h + 256)
            ru[h] = dot_nn(tb[...], dpre[:, col]).astype(BF16).reshape(4, 2, 2, 48, 256)
            rd[h] = dot_tn(hid[:, col], xb[...]).astype(BF16).reshape(4, 2, 2, 16, 768)
        lane_u.start(0, par)
        lane_d.start(0, par)

        def outer(i, _):
            r = rows(i, 416)
            acc[r, :] += dot_nn(hid[r, :], wd[ch].reshape(512, 768))
            dp = dpre[r, :]
            dsec[r, :] += dot_nt(dp[:, :256], wu[6 + ch, 0].reshape(768, 256)) + dot_nt(
                dp[:, 256:], wu[6 + ch, 1].reshape(768, 256)
            )
            return 0

        lax.fori_loop(0, padded // 416, outer, 0)
        return 0

    lax.fori_loop(0, 6, chunk, 0)

    def drain(t, lanes):
        for phase in (4, 3, 2, 1):
            j = t - phase
            for lane, count in lanes:
                if 0 <= j < count:
                    if phase == 4 and lane is lane_u and j >= 2:
                        lane.post(j % 2, j - 2).wait_send()
                    lane.step(phase, j, j % 2, before=j >= 1)

    drain(6, ((lane_u, 12), (lane_d, 6)))

    def second_back(i, _):
        r = rows(i, 208)
        e = dsec[r, :]
        hat = hat2[r, :].astype(F32)
        inverse = inv2[r, :][:, :1]
        lng[2:3, :] += jnp.sum(e * hat, 0, keepdims=True)
        lng[3:4, :] += jnp.sum(e, 0, keepdims=True)
        eg = e * prm[2:3, :]
        m1 = jnp.mean(eg, -1, keepdims=True)
        m2 = jnp.mean(eg * hat, -1, keepdims=True)
        dmid = xb[r, :].astype(F32) + inverse * (eg - m1 - hat * m2)
        dsec[r, :] = dmid
        low = dmid.astype(BF16)
        second[r, :] = low
        hat2[r, :] = acc[r, :].astype(BF16)
        grad = dot_nt(low[:, :256], block(9))
        grad = grad + dot_nt(low[:, 256:512], block(10))
        acc[r, :] = grad + dot_nt(low[:, 512:], block(11))
        return 0

    lax.fori_loop(0, padded // 208, second_back, 0)
    store_out = pltpu.make_async_copy(hat2.at[pl.ds(0, tokens_here)], out_hbm, local.at[0])
    store_out.start()
    load_x = pltpu.make_async_copy(x_hbm, xb.at[pl.ds(0, tokens_here)], local.at[2])
    load_x.start()

    def weight_grad(unit, parts):
        lane_u.wait_sent(0, 1 - unit % 2)
        for h, (ref, col) in enumerate(parts):
            grad = dot_nn(tb[...], ref[:, 256 * col : 256 * col + 256])
            ru[h] = grad.astype(BF16).reshape(4, 2, 2, 48, 256)
        lane_u.start(0, unit % 2)

    turn(mixed)
    weight_grad(6, ((second, 0), (second, 1)))
    drain(7, ((lane_u, 7), (lane_d, 6)))
    drain(8, ((lane_u, 7), (lane_d, 6)))

    def attend_back(s, _):
        w, pos, valid, live = places(s)
        for g in range(3):
            wide = slice(256 * g, 256 * g + 256)
            thin = slice(128 * g, 128 * g + 128)
            diag = diagonal[...]
            pk32 = masked_keys(g, w, live)
            pkm = pk32.astype(BF16)
            st, tot_high, tot_low = state_of(g, w, live, pkm)
            tot = jnp.sum(pk32, 0, keepdims=True)
            pqg = pq[w, thin]
            pq32 = jnp.where(valid, pqg.astype(F32), 0.0)
            num = dot_nn(pqg, st)
            den = dot_nn(pqg, tot_high) + dot_nn(pqg, tot_low)
            share = 1.0 / den
            part = acc[w, wide] * share
            dnum = jnp.where(valid, part, 0.0).astype(BF16)
            e_high, e_low = split_low(jnp.where(valid, -part * (num * share), 0.0))
            dden = dot_nn(e_high, ones_val[...]) + dot_nn(e_low, ones_val[...])
            dpq = dot_nt(dnum, st) + dden * tot
            dst = (dot_tn(pqg, dnum) * diag).astype(BF16)
            dtot = jnp.sum(dden * pq32, 0, keepdims=True)
            vals = vv[w, wide]
            dpk = dot_nt(vals, dst) + dtot
            dvv = dot_nn(pkm, dst)
            vv[w, wide] = jnp.where(valid, dvv, vals.astype(F32)).astype(BF16)
            for rot_ref, grad in ((rotq, dpq * pq32), (rotk, dpk * pk32)):
                high, low = split_low(grad)
                rot = rot_ref[w, wide].astype(F32)
                total = dot_nt(high, ones_rot[...]) + dot_nt(low, ones_rot[...])
                back = dot_nt(jnp.concatenate([high, high], 1), feats[g])
                back = back + dot_nt(low, feats[g, :, :128]) - rot * total
                a, b = back[:, :128], back[:, 128:]
                ct, sn = cosine[w, :], sine[w, :]
                turned = jnp.concatenate([a * ct + b * sn, b * ct - a * sn], 1)
                rot_ref[w, wide] = jnp.where(valid, turned, rot).astype(BF16)
        return 0

    lax.fori_loop(0, mols // 2, attend_back, 0)
    drain(9, ((lane_u, 7), (lane_d, 6)))
    lax.fori_loop(mols // 2, mols, attend_back, 0)
    nothing = jnp.zeros((spare, 768), BF16)
    rotq[tail, :] = nothing
    rotk[tail, :] = nothing
    vv[tail, :] = nothing
    drain(10, ((lane_u, 7), (lane_d, 6)))

    lane_u.wait_sent(0, 0)
    grad = dot_nn(tb[...], second[:, 512:768])
    ru[0] = grad.astype(BF16).reshape(4, 2, 2, 48, 256)
    turn(normed)
    grad = dot_nn(tb[...], vv[:, 0:256])
    ru[1] = grad.astype(BF16).reshape(4, 2, 2, 48, 256)
    lane_u.start(0, 1)

    def step_unit(unit, phase):
        if phase == 4:
            lane_u.post(unit % 2, unit - 2).wait_send()
        lane_u.step(phase, unit, unit % 2, before=True)

    weight_list = {
        8: ((vv, 1), (vv, 2)),
        9: ((rotk, 0), (rotk, 1)),
        10: ((rotk, 2), (rotq, 0)),
        11: ((rotq, 1), (rotq, 2)),
    }
    for unit in (8, 9, 10, 11):
        for phase in (4, 3, 2, 1):
            j = unit - phase
            if j >= 7:
                step_unit(j, phase)
        weight_grad(unit, weight_list[unit])

    def first_back(i, _):
        r = rows(i, 208)
        dn = jnp.zeros((208, 768), F32)
        for base, ref in ((0, rotk), (3, vv), (6, rotq)):
            lines = ref[r, :]
            for g in range(3):
                dn = dn + dot_nt(lines[:, 256 * g : 256 * g + 256], block(base + g))
        hat, inverse = norm(xb[r, :].astype(F32))
        lng[0:1, :] += jnp.sum(dn * hat, 0, keepdims=True)
        lng[1:2, :] += jnp.sum(dn, 0, keepdims=True)
        eg = dn * prm[0:1, :]
        m1 = jnp.mean(eg, -1, keepdims=True)
        m2 = jnp.mean(eg * hat, -1, keepdims=True)
        normed[r, :] = (dsec[r, :] + inverse * (eg - m1 - hat * m2)).astype(BF16)
        return 0

    load_x.wait()
    tiles = padded // 208
    done = 0
    for t in range(12, 15):
        upto = done + tiles // 4
        lax.fori_loop(done, upto, first_back, 0)
        done = upto
        for phase in (4, 3, 2, 1):
            j = t - phase
            if 7 <= j < 12:
                step_unit(j, phase)
    lax.fori_loop(done, tiles, first_back, 0)
    store_dx = pltpu.make_async_copy(normed.at[pl.ds(0, tokens_here)], dx_hbm, local.at[1])
    store_dx.start()

    ends = lng[...]
    ends = jnp.concatenate([ends, jnp.zeros((8, 128), F32)], 1)
    for i in range(32):
        k, shift = (24 * i) // 128, (24 * i) % 128
        pair = ends[:, 128 * k : 128 * k + 256]
        if shift:
            pair = pltpu.roll(pair, 256 - shift, 1)
        rp[i % 2, i // 8, (i // 4) % 2, (i // 2) % 2] = pair[:, :128]
    store_down = pltpu.make_async_copy(res_d, down_out, local.at[3])
    store_down.start()
    lane_p = Reduce(at, (rp, b1p, sp, b2p, s2p, b3p, s3p, b4p, res_p), ps, pr, "own", True)
    lane_p.start(0, 0)
    step_unit(11, 4)
    for phase in (1, 2, 3, 4):
        lane_p.step(phase, 0, 0, before=False)
    params_out[...] = res_p[0]
    for phase in range(4):
        lane_p.wait_sent(phase, 0)
        lane_u.wait_sent(phase, 1)
        lane_d.wait_sent(phase, 1)
    lane_u.post(0, 10).wait_send()
    lane_u.post(1, 11).wait_send()
    for unit in range(12):
        lane_u.post(unit % 2, unit).wait_recv()
    for unit in units:
        unit.sent()
    params.sent()
    store_wide = pltpu.make_async_copy(res_u, wide_out, local.at[2])
    store_wide.start()
    store_wide.wait()
    store_down.wait()
    store_out.wait()
    store_dx.wait()


def fused_device(
    tokens,
    lengths,
    feature_directions,
    first_gain,
    first_shift,
    query_weight,
    key_weight,
    value_weight,
    out_weight,
    second_gain,
    second_shift,
    up_weight,
    down_weight,
    out_cotangent,
):
    tokens_here, width = tokens.shape
    mols = lengths.shape[0]
    length = tokens_here // mols
    padded = -(-tokens_here // 416) * 416
    share = first_gain.shape[0]

    def halves_first(w):
        return w.reshape(share, 3, 4, 2, 32).transpose(0, 1, 3, 2, 4).reshape(share, width)

    wide = jnp.concatenate(
        [halves_first(key_weight), value_weight, halves_first(query_weight), out_weight], 1
    )
    wide = wide.reshape(share, 6, 2, 256).transpose(1, 2, 0, 3)
    up = up_weight.reshape(share, 16, 2, 6, 16).transpose(3, 2, 0, 1, 4).reshape(6, 2, share, 256)
    wide = jnp.concatenate([wide, up], 0).astype(F32)
    vectors = jnp.stack([first_gain, first_shift, second_gain, second_shift]).astype(F32)
    params = jnp.pad(vectors, ((0, 4), (0, 128 - share)))

    frequency = np.float32(10000.0) ** (-np.arange(32, dtype=np.float32) * np.float32(2.0 / 64))
    angles = (np.arange(padded) % length).astype(np.float32)[:, None] * frequency[None, :]
    scale = 64.0**-0.25
    cosine = jnp.asarray(np.tile(np.cos(angles) * scale, (1, 4)), F32)
    sine = jnp.asarray(np.tile(np.sin(angles) * scale, (1, 4)), F32)
    split = feature_directions.reshape(3, 4, 2, 32, 32)
    eye = jnp.eye(4, dtype=F32)
    packed = split.transpose(0, 2, 1, 3, 4)[:, :, :, :, None, :] * eye[None, None, :, None, :, None]
    packed = packed.reshape(3, 256, 128)
    high = packed.astype(BF16)
    feats = jnp.concatenate([high, (packed - high.astype(F32)).astype(BF16)], 2)
    lane_head = np.arange(128) // 32
    ones_rot = jnp.asarray(np.tile(lane_head, 2)[:, None] == lane_head[None, :], BF16)
    value_head = np.arange(256) // 64
    ones_val = jnp.asarray(value_head[:, None] == lane_head[None, :], BF16)
    diagonal = jnp.asarray(lane_head[:, None] == value_head[None, :], F32)

    def vm(shape, kind):
        return pltpu.VMEM(shape, kind)

    def lane(block, kind, tail):
        return [
            vm((2, 4, 2, 2) + block, kind),
            vm((2, 4, 2, 2) + block, kind),
            vm((4, 2, 2) + block, kind),
            vm((2, 4, 2) + block, kind),
            vm((4, 2) + block, kind),
            vm((2, 4) + block, kind),
            vm((4,) + block, kind),
            vm((2, 3) + block, kind),
        ] + tail

    rows16 = (padded, width)
    scratch = [
        vm((12, 2, 4, 2, 2, 48, 256), BF16),
        vm((6, 2, 4, 2, 2, 16, 768), BF16),
        vm((2, 4, 2, 2, 8, 128), F32),
        vm((12, 24, 256), F32),
        vm(rows16, BF16),
        vm(rows16, BF16),
        vm(rows16, BF16),
        vm(rows16, BF16),
        vm(rows16, BF16),
        vm((padded, 384), BF16),
        vm((padded, 384), BF16),
        vm(rows16, BF16),
        vm(rows16, BF16),
        vm(rows16, BF16),
        vm((padded, 128), F32),
        vm(rows16, F32),
        vm(rows16, F32),
        vm((padded, 512), BF16),
        vm((padded, 512), BF16),
        vm((width, padded), BF16),
        vm((8, width), F32),
        vm((8, width), F32),
    ]
    scratch += lane((48, 256), BF16, [vm((2, 2, 24, 256), F32)])
    scratch += lane((16, 768), BF16, [])
    scratch += lane((8, 128), F32, [])
    scratch += [
        vm((12, 2, 24, 256), F32),
        vm((6, 16, 768), F32),
        vm((1, 8, 128), F32),
        pltpu.SemaphoreType.DMA((19, 6)),
        pltpu.SemaphoreType.DMA((19, 6)),
        pltpu.SemaphoreType.DMA,
        pltpu.SemaphoreType.DMA,
    ]
    scratch += [pltpu.SemaphoreType.DMA((2, 6))] * 6 + [pltpu.SemaphoreType.DMA((12,))] * 2
    scratch += [pltpu.SemaphoreType.DMA((4,))]
    spaces = [pl.ANY, pl.ANY, pltpu.SMEM, pltpu.VMEM, pl.ANY] + [pltpu.VMEM] * 7
    kernel = functools.partial(layer_kernel, (tokens_here, padded, length, mols))
    outs = pl.pallas_call(
        kernel,
        out_shape=[
            jax.ShapeDtypeStruct(tokens.shape, BF16),
            jax.ShapeDtypeStruct(tokens.shape, BF16),
            jax.ShapeDtypeStruct((12, 2, share, 256), F32),
            jax.ShapeDtypeStruct((6, 16, width), F32),
            jax.ShapeDtypeStruct((8, 128), F32),
        ],
        in_specs=[pl.BlockSpec(memory_space=s) for s in spaces],
        out_specs=[pl.BlockSpec(memory_space=s) for s in [pl.ANY] * 4 + [pltpu.VMEM]],
        scratch_shapes=scratch,
        compiler_params=pltpu.CompilerParams(
            collective_id=0, has_side_effects=True, vmem_limit_bytes=VMEM_BYTES
        ),
        name="encoder_layer",
    )(
        tokens,
        out_cotangent,
        lengths,
        params,
        wide,
        down_weight,
        cosine,
        sine,
        feats,
        ones_rot,
        ones_val,
        diagonal,
    )
    output, input_grad, wide_grad, down_grad, vector_grad = outs

    def natural(w):
        return w.reshape(share, 3, 2, 4, 32).transpose(0, 1, 3, 2, 4).reshape(share, width)

    attn = wide_grad[6:].transpose(2, 0, 1, 3).reshape(share, 12, 256)

    def columns(first):
        return attn[:, first : first + 3].reshape(share, width)

    up_grad = wide_grad[:6].reshape(6, 2, share, 16, 16).transpose(2, 3, 1, 0, 4)
    return (
        output,
        input_grad,
        vector_grad[0, :share],
        vector_grad[1, :share],
        natural(columns(9)),
        natural(columns(6)),
        columns(3),
        columns(0),
        vector_grad[2, :share],
        vector_grad[3, :share],
        up_grad.reshape(share, up_weight.shape[1]),
        down_grad.reshape(down_weight.shape),
    )


VMEM_BYTES = 64 * 1024 * 1024


def solution(mesh):
    placed = (
        P("fsdp", None),
        P("fsdp"),
        P(),
        P("fsdp"),
        P("fsdp"),
        P("fsdp", None),
        P("fsdp", None),
        P("fsdp", None),
        P("fsdp", None),
        P("fsdp"),
        P("fsdp"),
        P("fsdp", None),
        P("fsdp", None),
        P("fsdp", None),
    )
    fused = mesh.shape["fsdp"] == 32
    return jax.shard_map(
        fused_device if fused else per_device,
        mesh=mesh,
        in_specs=placed,
        out_specs=(
            P("fsdp", None),
            P("fsdp", None),
            P("fsdp"),
            P("fsdp"),
            P("fsdp", None),
            P("fsdp", None),
            P("fsdp", None),
            P("fsdp", None),
            P("fsdp"),
            P("fsdp"),
            P("fsdp", None),
            P("fsdp", None),
        ),
        check_vma=False,
    )
```

```python
import functools

import jax
import jax.numpy as jnp
import numpy as np
from jax import lax
from jax.experimental import pallas as pl
from jax.experimental.pallas import tpu as pltpu
from jax.sharding import PartitionSpec as P

F32 = jnp.float32
BF16 = jnp.bfloat16


def rotate_scale(vectors):
    half_size = vectors.shape[-1] // 2
    positions = jnp.arange(vectors.shape[1], dtype=jnp.float32)
    frequency = 10000.0 ** (-jnp.arange(half_size, dtype=jnp.float32) * 2.0 / vectors.shape[-1])
    angles = positions[:, None] * frequency[None, :]
    cosine_table = jnp.cos(angles)[None, :, None, :]
    sine_table = jnp.sin(angles)[None, :, None, :]
    first_half = vectors[..., :half_size]
    second_half = vectors[..., half_size:]
    turned = jnp.concatenate(
        [
            first_half * cosine_table - second_half * sine_table,
            first_half * sine_table + second_half * cosine_table,
        ],
        -1,
    )
    return turned * vectors.shape[-1] ** (-0.25)


def feature_map(vectors, directions):
    turned = rotate_scale(vectors)
    logits = jnp.einsum("slhd,hdm->slhm", turned, directions, precision=lax.Precision.HIGHEST)
    logits = logits - 0.5 * jnp.sum(turned * turned, -1, keepdims=True)
    return jnp.exp(logits) * directions.shape[-1] ** (-0.5)


def smooth_gelu(values):
    return jax.nn.gelu(values, approximate=True)


def norm_parts(inputs, gain_row, shift_row):
    row_mean = jnp.mean(inputs, -1, keepdims=True)
    centered = inputs - row_mean
    inverse = lax.rsqrt(jnp.mean(centered * centered, -1, keepdims=True) + 1e-05)
    hat_rows = centered * inverse
    return (
        hat_rows * gain_row.astype(jnp.float32) + shift_row.astype(jnp.float32),
        hat_rows,
        inverse,
    )


def norm_back(grad_rows, hat_rows, inverse, gain_row):
    scaled = grad_rows * gain_row.astype(jnp.float32)
    return inverse * (
        scaled
        - jnp.mean(scaled, -1, keepdims=True)
        - hat_rows * jnp.mean(scaled * hat_rows, -1, keepdims=True)
    )


def per_device(
    tokens,
    lengths,
    feature_directions,
    first_gain,
    first_shift,
    query_weight,
    key_weight,
    value_weight,
    out_weight,
    second_gain,
    second_shift,
    up_weight,
    down_weight,
    out_cotangent,
):
    model_width = tokens.shape[1]
    head_count = feature_directions.shape[0]
    head_size = model_width // head_count
    seqs_here = lengths.shape[0]
    length = tokens.shape[0] // seqs_here
    inputs = tokens.astype(jnp.float32)

    def feature_of(row_block):
        return feature_map(
            row_block.reshape(seqs_here, length, head_count, head_size), feature_directions
        )

    gain_one, shift_one, query_full, key_full, value_full, out_full = (
        lax.all_gather(first_gain, "fsdp", axis=0, tiled=True),
        lax.all_gather(first_shift, "fsdp", axis=0, tiled=True),
        lax.all_gather(query_weight, "fsdp", axis=0, tiled=True),
        lax.all_gather(key_weight, "fsdp", axis=0, tiled=True),
        lax.all_gather(value_weight, "fsdp", axis=0, tiled=True),
        lax.all_gather(out_weight, "fsdp", axis=0, tiled=True),
    )
    normed_wide, hat_one, inverse_one = norm_parts(inputs, gain_one, shift_one)
    normed = normed_wide.astype(jnp.bfloat16)
    query_rows = jnp.dot(normed, query_full, preferred_element_type=jnp.float32)
    key_rows = jnp.dot(normed, key_full, preferred_element_type=jnp.float32)
    value_rows = jnp.dot(normed, value_full, preferred_element_type=jnp.float32)
    value_low = value_rows.astype(jnp.bfloat16).reshape(seqs_here, length, head_count, head_size)
    query_raw, query_back = jax.vjp(feature_of, query_rows)
    key_raw, key_back = jax.vjp(feature_of, key_rows)
    query_low = query_raw.astype(jnp.bfloat16)
    key_low = key_raw.astype(jnp.bfloat16)
    positions = jnp.arange(length, dtype=jnp.int32)
    key_live = positions[None, :] < lengths[:, None]
    masked = key_low * key_live.astype(jnp.bfloat16)[:, :, None, None]
    state_sum = jnp.einsum("slhm,slhd->shmd", masked, value_low, preferred_element_type=jnp.float32)
    state_low = state_sum.astype(jnp.bfloat16)
    totals = jnp.sum(masked.astype(jnp.float32), 1)
    numerator = jnp.einsum(
        "slhm,shmd->slhd", query_low, state_low, preferred_element_type=jnp.float32
    )
    query_wide = query_low.astype(jnp.float32)
    denominator = jnp.einsum("slhm,shm->slh", query_wide, totals, precision=lax.Precision.HIGHEST)
    mixed_rows = (numerator / denominator[..., None]).reshape(-1, model_width).astype(jnp.bfloat16)
    branch = jnp.dot(mixed_rows, out_full, preferred_element_type=jnp.float32)
    middle = inputs + branch
    gain_two, shift_two, up_full, down_full = (
        lax.all_gather(second_gain, "fsdp", axis=0, tiled=True),
        lax.all_gather(second_shift, "fsdp", axis=0, tiled=True),
        lax.all_gather(up_weight, "fsdp", axis=0, tiled=True),
        lax.all_gather(down_weight, "fsdp", axis=0, tiled=True),
    )
    second_wide, hat_two, inverse_two = norm_parts(middle, gain_two, shift_two)
    second = second_wide.astype(jnp.bfloat16)
    up_rows = jnp.dot(second, up_full, preferred_element_type=jnp.float32)
    gelu_rows, gelu_back = jax.vjp(smooth_gelu, up_rows)
    hidden = gelu_rows.astype(jnp.bfloat16)
    output = (middle + jnp.dot(hidden, down_full, preferred_element_type=jnp.float32)).astype(
        jnp.bfloat16
    )
    gain_two, shift_two, up_full, down_full = (
        lax.all_gather(second_gain, "fsdp", axis=0, tiled=True),
        lax.all_gather(second_shift, "fsdp", axis=0, tiled=True),
        lax.all_gather(up_weight, "fsdp", axis=0, tiled=True),
        lax.all_gather(down_weight, "fsdp", axis=0, tiled=True),
    )
    gain_one, shift_one, query_full, key_full, value_full, out_full = (
        lax.all_gather(first_gain, "fsdp", axis=0, tiled=True),
        lax.all_gather(first_shift, "fsdp", axis=0, tiled=True),
        lax.all_gather(query_weight, "fsdp", axis=0, tiled=True),
        lax.all_gather(key_weight, "fsdp", axis=0, tiled=True),
        lax.all_gather(value_weight, "fsdp", axis=0, tiled=True),
        lax.all_gather(out_weight, "fsdp", axis=0, tiled=True),
    )
    down_grad = jnp.einsum("tf,td->fd", hidden, out_cotangent, preferred_element_type=jnp.float32)
    hidden_grad = jnp.einsum(
        "td,fd->tf", out_cotangent, down_full, preferred_element_type=jnp.float32
    )
    pre_grad = gelu_back(hidden_grad)[0].astype(jnp.bfloat16)
    up_grad = jnp.einsum("td,tf->df", second, pre_grad, preferred_element_type=jnp.float32)
    second_grad = jnp.einsum("tf,df->td", pre_grad, up_full, preferred_element_type=jnp.float32)
    gain_two_grad = jnp.sum(second_grad * hat_two, 0)
    shift_two_grad = jnp.sum(second_grad, 0)
    middle_grad = out_cotangent.astype(jnp.float32) + norm_back(
        second_grad, hat_two, inverse_two, gain_two
    )
    ffn_shards = (
        lax.psum_scatter(gain_two_grad, "fsdp", scatter_dimension=0, tiled=True),
        lax.psum_scatter(shift_two_grad, "fsdp", scatter_dimension=0, tiled=True),
        lax.psum_scatter(up_grad, "fsdp", scatter_dimension=0, tiled=True),
        lax.psum_scatter(down_grad, "fsdp", scatter_dimension=0, tiled=True),
    )
    branch_grad = middle_grad.astype(jnp.bfloat16)
    out_grad = jnp.einsum("td,te->de", mixed_rows, branch_grad, preferred_element_type=jnp.float32)
    mixed_grad = jnp.einsum("te,de->td", branch_grad, out_full, preferred_element_type=jnp.float32)
    mixed_grad = mixed_grad.reshape(seqs_here, length, head_count, head_size)
    numer_grad = (mixed_grad / denominator[..., None]).astype(jnp.bfloat16)
    denom_grad = -jnp.sum(mixed_grad * numerator, -1) / (denominator * denominator)
    query_feat_grad = jnp.einsum(
        "slhd,shmd->slhm", numer_grad, state_low, preferred_element_type=jnp.float32
    )
    query_feat_grad = query_feat_grad + denom_grad[..., None] * totals[:, None]
    state_grad = jnp.einsum(
        "slhm,slhd->shmd", query_low, numer_grad, preferred_element_type=jnp.float32
    ).astype(jnp.bfloat16)
    totals_grad = jnp.einsum(
        "slh,slhm->shm", denom_grad, query_wide, precision=lax.Precision.HIGHEST
    )
    key_feat_grad = jnp.einsum(
        "slhd,shmd->slhm", value_low, state_grad, preferred_element_type=jnp.float32
    )
    key_feat_grad = (key_feat_grad + totals_grad[:, None]) * key_live.astype(jnp.float32)[
        :, :, None, None
    ]
    value_grad = jnp.einsum(
        "slhm,shmd->slhd", masked, state_grad, preferred_element_type=jnp.float32
    )
    value_grad = value_grad.reshape(-1, model_width).astype(jnp.bfloat16)
    query_grad = query_back(query_feat_grad)[0].astype(jnp.bfloat16)
    key_grad = key_back(key_feat_grad)[0].astype(jnp.bfloat16)
    normed_grad = jnp.einsum(
        "te,de->td", query_grad, query_full, preferred_element_type=jnp.float32
    )
    normed_grad = normed_grad + jnp.einsum(
        "te,de->td", key_grad, key_full, preferred_element_type=jnp.float32
    )
    normed_grad = normed_grad + jnp.einsum(
        "te,de->td", value_grad, value_full, preferred_element_type=jnp.float32
    )
    query_weight_grad = jnp.einsum(
        "td,te->de", normed, query_grad, preferred_element_type=jnp.float32
    )
    key_weight_grad = jnp.einsum("td,te->de", normed, key_grad, preferred_element_type=jnp.float32)
    value_weight_grad = jnp.einsum(
        "td,te->de", normed, value_grad, preferred_element_type=jnp.float32
    )
    gain_one_grad = jnp.sum(normed_grad * hat_one, 0)
    shift_one_grad = jnp.sum(normed_grad, 0)
    input_grad = middle_grad + norm_back(normed_grad, hat_one, inverse_one, gain_one)
    attn_shards = (
        lax.psum_scatter(gain_one_grad, "fsdp", scatter_dimension=0, tiled=True),
        lax.psum_scatter(shift_one_grad, "fsdp", scatter_dimension=0, tiled=True),
        lax.psum_scatter(query_weight_grad, "fsdp", scatter_dimension=0, tiled=True),
        lax.psum_scatter(key_weight_grad, "fsdp", scatter_dimension=0, tiled=True),
        lax.psum_scatter(value_weight_grad, "fsdp", scatter_dimension=0, tiled=True),
        lax.psum_scatter(out_grad, "fsdp", scatter_dimension=0, tiled=True),
    )
    shards = tuple(attn_shards) + tuple(ffn_shards)
    return (output, input_grad.astype(jnp.bfloat16)) + shards


def dot_nn(a, b):
    return lax.dot_general(a, b, (((1,), (0,)), ((), ())), preferred_element_type=F32)


def dot_nt(a, b):
    return lax.dot_general(a, b, (((1,), (1,)), ((), ())), preferred_element_type=F32)


def dot_tn(a, b):
    return lax.dot_general(a, b, (((0,), (0,)), ((), ())), preferred_element_type=F32)


def split_low(v):
    high = v.astype(BF16)
    return high, (v - high.astype(F32)).astype(BF16)


def remote(src, dst, send, recv, device):
    return pltpu.make_async_remote_copy(
        src_ref=src,
        dst_ref=dst,
        send_sem=send,
        recv_sem=recv,
        device_id=(device,),
        device_id_type=pl.DeviceIdType.MESH,
    )


class Place:
    def __init__(self):
        me = lax.axis_index("fsdp")
        self.c = lax.rem(me, 2)
        self.x = lax.rem(lax.div(me, 2), 2)
        self.y = lax.rem(lax.div(me, 4), 2)
        self.z = lax.div(me, 8)
        self.sib = me + 1 - 2 * self.c
        self.px = me + 2 - 4 * self.x
        self.py = me + 4 - 8 * self.y
        self.zs = [lax.rem(self.z + d, 4) for d in (1, 2, 3)]
        self.pz = [me + (zp - self.z) * 8 for zp in self.zs]

    def enter(self):
        barrier = pltpu.get_barrier_semaphore()
        peers = [self.sib, self.px, self.py] + self.pz
        for peer in peers:
            pl.semaphore_signal(
                barrier, inc=1, device_id=(peer,), device_id_type=pl.DeviceIdType.MESH
            )
        pl.semaphore_wait(barrier, len(peers))


class Gather:
    def __init__(self, at, buf, send, recv, y_first):
        self.buf, self.send, self.recv = buf, send, recv
        c, z, y, x = at.c, at.z, at.y, at.x
        mine = buf.at[c, z, y, x]
        line = buf.at[c, :, y, x]
        plane = buf.at[c, :, :, x] if y_first else buf.at[c, :, y]
        first, second = (at.py, at.px) if y_first else (at.px, at.py)
        self.copies = [
            [remote(mine, mine, send.at[d], recv.at[d], at.pz[d]) for d in range(3)],
            [remote(line, line, send.at[3], recv.at[3], first)],
            [remote(plane, plane, send.at[4], recv.at[4], second)],
            [remote(buf.at[c], buf.at[c], send.at[5], recv.at[5], at.sib)],
        ]

    def start(self, phase):
        for copy in self.copies[phase]:
            copy.start()

    def arrived(self, phase):
        for copy in self.copies[phase]:
            copy.wait_recv()

    def sent(self):
        for phase in self.copies:
            for copy in phase:
                copy.wait_send()


class Reduce:
    def __init__(self, at, refs, send, recv, y_first):
        self.at, self.y_first = at, y_first
        self.R, self.B1, self.S, self.B2, self.S2, self.B3, self.S3, self.B4 = refs
        self.send, self.recv = send, recv

    def copies(self, phase, par):
        at, s, r = self.at, self.send.at[par], self.recv.at[par]
        first, second = (at.py, at.px) if self.y_first else (at.px, at.py)
        if phase == 0:
            return [remote(self.R.at[1 - at.c], self.B1.at[par], s.at[0], r.at[0], at.sib)]
        if phase == 1:
            src = self.S.at[:, 1 - at.y] if self.y_first else self.S.at[:, :, 1 - at.x]
            return [remote(src, self.B2.at[par], s.at[1], r.at[1], first)]
        if phase == 2:
            src = self.S2.at[:, 1 - (at.x if self.y_first else at.y)]
            return [remote(src, self.B3.at[par], s.at[2], r.at[2], second)]
        return [
            remote(self.S3.at[at.zs[d]], self.B4.at[par, d], s.at[3 + d], r.at[3 + d], at.pz[d])
            for d in range(3)
        ]

    def start(self, phase, par):
        for copy in self.copies(phase, par):
            copy.start()

    def wait_sent(self, phase, par):
        for copy in self.copies(phase, par):
            copy.wait_send()

    def step(self, phase, par, before=True):
        at = self.at
        for copy in self.copies(phase - 1, par):
            copy.wait_recv()
        if phase == 4:
            total = self.S3[at.z].astype(F32)
            for d in range(3):
                total = total + self.B4[par, d].astype(F32)
            return total
        if before is True:
            self.wait_sent(phase, 1 - par)
        elif before is not False:

            @pl.when(before)
            def _():
                self.wait_sent(phase, 1 - par)

        kind = self.S.dtype

        def add(i, _):
            if phase == 1:
                own, other, out = self.R[at.c, i], self.B1[par, i], self.S
            elif phase == 2:
                own = self.S[i, at.y] if self.y_first else self.S[i, :, at.x]
                other, out = self.B2[par, i], self.S2
            else:
                own = self.S2[i, at.x if self.y_first else at.y]
                other, out = self.B3[par, i], self.S3
            out[i] = (own.astype(F32) + other.astype(F32)).astype(kind)
            return 0

        lax.fori_loop(0, 4, add, 0)
        self.start(phase, par)
        return None


def layer_kernel(
    sizes,
    x_hbm,
    dy_hbm,
    lengths,
    params_here,
    wide_here,
    down_here,
    cosine_hbm,
    sine_hbm,
    feats,
    ones_rot,
    ones_val,
    diagonal,
    out_hbm,
    dx_hbm,
    wide_out,
    down_out,
    params_out,
    wu,
    wd,
    pb,
    px32,
    xb,
    normed,
    rotq,
    rotk,
    vv,
    pq,
    pk,
    mixed,
    second,
    inv2,
    acc,
    dsec,
    hid,
    dpre,
    tb,
    prm,
    lng,
    ru,
    b1u,
    su,
    b2u,
    s2u,
    b3u,
    s3u,
    b4u,
    flu,
    fld,
    rd,
    b1d,
    sd,
    b2d,
    s2d,
    b3d,
    s3d,
    b4d,
    rp,
    b1p,
    sp,
    b2p,
    s2p,
    b3p,
    s3p,
    b4p,
    res_u,
    res_d,
    ag_send,
    ag_recv,
    pre_send,
    pre_recv,
    us,
    ur,
    ds_,
    dr,
    ps,
    pr,
    qs,
    qr,
    cosine,
    sine,
    local,
):
    tokens_here, padded, length, mols = sizes
    spare = padded - tokens_here
    at = Place()
    load_x = pltpu.make_async_copy(x_hbm, xb.at[pl.ds(0, tokens_here)], local.at[0])
    load_dy = pltpu.make_async_copy(dy_hbm, xb.at[pl.ds(0, tokens_here)], local.at[0])
    load_wide = pltpu.make_async_copy(wide_here, res_u, local.at[1])
    load_wide.start()
    load_x.start()
    load_cos = pltpu.make_async_copy(cosine_hbm, cosine, local.at[2])
    load_sin = pltpu.make_async_copy(sine_hbm, sine, local.at[3])
    load_cos.start()
    load_sin.start()
    at.enter()
    load_wide.wait()

    swap = remote(res_u.at[:, 1 - at.c], px32, pre_send, pre_recv, at.sib)
    swap.start()
    pb[at.c, at.z, at.y, at.x] = params_here[...]
    for ch in range(6):
        wd[ch, at.c, at.z, at.y, at.x] = down_here[16 * ch : 16 * ch + 16, :]
    tail = pl.ds(tokens_here, spare)
    xb[tail, :] = jnp.zeros((spare, xb.shape[1]), BF16)
    mixed[tail, :] = jnp.zeros((spare, xb.shape[1]), BF16)
    lng[...] = jnp.zeros(lng.shape, F32)
    swap.wait()
    even = at.c == 0

    def build(u, _):
        mine = res_u[u, at.c]
        other = px32[u]
        top = jnp.where(even, mine, other)
        low = jnp.where(even, other, mine)
        wu[u, at.c, at.z, at.y, at.x] = jnp.concatenate([top, low], 0).astype(BF16)
        return 0

    lax.fori_loop(0, 12, build, 0)

    def gather_unit(u):
        if u < 6:
            buf = wu.at[u]
        else:
            buf = wu.at[6 + (u - 6) // 2] if u % 2 == 0 else wd.at[(u - 6) // 2]
        return Gather(at, buf, ag_send.at[u], ag_recv.at[u], u % 2 == 0)

    units = [gather_unit(u) for u in range(18)]
    params = Gather(at, pb, ag_send.at[18], ag_recv.at[18], True)
    state = {"tick": 0, "needed": set()}
    lags, last = LAGS, (13, 11, 9, 7)

    def tick(count=1):
        for _ in range(count):
            t = state["tick"]
            state["tick"] += 1
            if t == 0:
                params.start(0)
            for k in range(4):
                u = t - lags[k]
                if 0 <= u <= last[k]:
                    if k:
                        if u == 0:
                            params.arrived(k - 1)
                            params.start(k)
                        units[u].arrived(k - 1)
                    units[u].start(k)

    def need(u):
        while state["tick"] <= u + lags[3]:
            tick()
        if u not in state["needed"]:
            state["needed"].add(u)
            units[u].arrived(3)

    tick(lags[3] + 1)
    params.arrived(3)
    parts = [jnp.zeros((8, 128), F32) for _ in range(7)]
    for i in range(32):
        block = pb[i % 2, i // 8, (i // 4) % 2, (i // 2) % 2]
        k, shift = (24 * i) // 128, (24 * i) % 128
        pair = jnp.concatenate([block, jnp.zeros((8, 128), F32)], 1)
        if shift:
            pair = pltpu.roll(pair, shift, 1)
        parts[k] = parts[k] + pair[:, :128]
        parts[k + 1] = parts[k + 1] + pair[:, 128:]
    prm[...] = jnp.concatenate(parts[:6], 1)

    def rows(i, count):
        return pl.ds(pl.multiple_of(i * count, 16), count)

    def norm(v):
        centered = v - jnp.mean(v, -1, keepdims=True)
        inverse = lax.rsqrt(jnp.mean(centered * centered, -1, keepdims=True) + 1e-05)
        return centered * inverse, inverse

    load_x.wait()
    load_cos.wait()
    load_sin.wait()

    def first_norm(i, _):
        r = rows(i, 208)
        hat, _ = norm(xb[r, :].astype(F32))
        normed[r, :] = (hat * prm[0:1, :] + prm[1:2, :]).astype(BF16)
        return 0

    lax.fori_loop(0, padded // 208, first_norm, 0)

    def block(b):
        return wu[b // 2, b % 2].reshape(768, 256)

    def features(base, rot_ref, feat_ref, part):
        def body(i, _):
            r = rows(i, 416)
            lines = normed[r, :]
            ct, st = cosine[r, :], sine[r, :]
            for g in range(3):
                u = dot_nn(lines, block(base + g))
                a, b = u[:, :128], u[:, 128:]
                rot = jnp.concatenate([a * ct - b * st, a * st + b * ct], 1)
                high, low = split_low(rot)
                sq_high, sq_low = split_low(rot * rot)
                two = dot_nn(high, feats[g])
                logits = two[:, :128] + two[:, 128:] + dot_nn(low, feats[g, :, :128])
                norms = dot_nn(sq_high, ones_rot[...]) + dot_nn(sq_low, ones_rot[...])
                p = jnp.exp(logits - 0.5 * norms) * (32**-0.5)
                rot_ref[r, 256 * g : 256 * g + 256] = high
                feat_ref[r, 128 * g : 128 * g + 128] = p.astype(BF16)
            return 0

        half = padded // 832
        lax.fori_loop(part * half, part * half + half, body, 0)

    need(0)
    need(1)
    features(0, rotk, pk, 0)
    tick()
    features(0, rotk, pk, 1)
    tick()
    need(2)

    def values(i, _):
        r = rows(i, 416)
        for g in range(3):
            vv[r, 256 * g : 256 * g + 256] = dot_nn(normed[r, :], block(3 + g)).astype(BF16)
        return 0

    lax.fori_loop(0, padded // 416, values, 0)
    tick()
    need(3)
    need(4)
    features(6, rotq, pq, 0)
    tick()
    features(6, rotq, pq, 1)
    tick()
    here = pl.ds(0, tokens_here)
    spill = pltpu.make_async_copy(normed.at[here], dx_hbm, local.at[1])
    spill.start()
    hat2 = normed

    window = 224

    def places(s):
        begin = lax.div(s * length, 16) * 16
        pos = lax.broadcasted_iota(jnp.int32, (window, 1), 0) - (s * length - begin)
        valid = (pos >= 0) & (pos < length)
        live = valid & (pos < lengths[s])
        return pl.ds(pl.multiple_of(begin, 16), window), pos, valid, live

    def state_of(g, w, live, pkm):
        ones = jnp.ones((window, 256), BF16)
        diag = diagonal[...]
        st = (dot_tn(pkm, vv[w, 256 * g : 256 * g + 256]) * diag).astype(BF16)
        tot = dot_tn(pkm, ones) * diag
        tot_high, tot_low = split_low(tot)
        return st, tot_high, tot_low

    def masked_keys(g, w, live):
        keys = pk[w, 128 * g : 128 * g + 128].astype(F32)
        return jnp.where(live, keys, 0.0)

    def attend(s, _):
        w, pos, valid, live = places(s)
        mixes = []
        for g in range(3):
            pkm = masked_keys(g, w, live).astype(BF16)
            st, tot_high, tot_low = state_of(g, w, live, pkm)
            pqg = pq[w, 128 * g : 128 * g + 128]
            num = dot_nn(pqg, st)
            den = dot_nn(pqg, tot_high) + dot_nn(pqg, tot_low)
            mixes.append(jnp.where(valid, num / den, 0.0))
        mix = jnp.where(pos < 0, mixed[w, :].astype(F32), jnp.concatenate(mixes, 1))
        mixed[w, :] = mix.astype(BF16)
        return 0

    lax.fori_loop(0, mols // 2, attend, 0)
    tick()
    lax.fori_loop(mols // 2, mols, attend, 0)
    need(5)
    tick()
    spill.wait()

    def project(i, _):
        r = rows(i, 208)
        lines = mixed[r, :]
        branch = jnp.concatenate([dot_nn(lines, block(9 + g)) for g in range(3)], 1)
        middle = xb[r, :].astype(F32) + branch
        acc[r, :] = middle
        hat, inverse = norm(middle)
        hat2[r, :] = hat.astype(BF16)
        inv2[r, :] = jnp.broadcast_to(inverse, (208, 128))
        second[r, :] = (hat * prm[2:3, :] + prm[3:4, :]).astype(BF16)
        dsec[r, :] = jnp.zeros((208, 768), F32)
        return 0

    lax.fori_loop(0, padded // 416, project, 0)
    tick()
    lax.fori_loop(padded // 416, padded // 208, project, 0)

    def turn(src):
        for j in range(6):
            tb[128 * j : 128 * j + 128, :] = src[:, 128 * j : 128 * j + 128].T

    load_dy.start()
    turn(second)
    load_dy.wait()
    while state["tick"] <= last[0] + lags[0]:
        tick()
    need(6)
    need(7)

    def pair_of(q):
        up, down = 6 + 2 * q, 7 + 2 * q
        return (
            Gather(at, wu.at[6 + q], ag_send.at[up], ag_recv.at[up], True),
            Gather(at, wd.at[q], ag_send.at[down], ag_recv.at[down], False),
        )

    def gather_on(q, phase):
        @pl.when(q < 6)
        def _():
            for unit in pair_of(q):
                if phase:
                    unit.arrived(phase - 1)
                unit.start(phase)

    lane_u = Reduce(at, (ru, b1u, su, b2u, s2u, b3u, s3u, b4u), us, ur, True)
    lane_d = Reduce(at, (rd, b1d, sd, b2d, s2d, b3d, s3d, b4d), ds_, dr, False)

    def post(flat, par, unit):
        return remote(
            flat.at[par, 1 - at.c], res_u.at[unit, at.c], qs.at[unit], qr.at[unit], at.sib
        )

    def emit_pair(flat, total, par, unit):
        flat[par] = total.reshape(flat.shape[1:])
        res_u[unit, at.c] = flat[par, at.c]
        post(flat, par, unit).start()

    def emit_own(total, unit):
        for b in range(3):
            res_d[unit, :, 256 * b : 256 * b + 256] = total[16 * b : 16 * b + 16]

    def keep(lane, half, grad):
        lane.R[half] = grad.astype(BF16).reshape(4, 2, 2, 48, 256)

    slope = 0.7978845608028654
    bend = 0.044715

    def chunk(ch, _):
        def inner(i, _):
            r = rows(i, 416)
            lines, cot = second[r, :], xb[r, :]
            for h in range(2):
                pre = dot_nn(lines, wu[6 + ch, h].reshape(768, 256))
                dh = dot_nt(cot, wd[ch, h].reshape(256, 768))
                square = pre * pre
                t = jnp.tanh(pre * (slope + slope * bend * square))
                half = 0.5 + 0.5 * t
                col = slice(256 * h, 256 * h + 256)
                hid[r, col] = (pre * half).astype(BF16)
                bent = slope + 3.0 * slope * bend * square
                grad = half + 0.5 * pre * (1.0 - t * t) * bent
                dpre[r, col] = (dh * grad).astype(BF16)
            return 0

        @pl.when(ch >= 1)
        def _():
            for unit in pair_of(ch):
                unit.arrived(3)

        lax.fori_loop(0, padded // 416, inner, 0)
        gather_on(ch + 1, 3)
        gather_on(ch + 2, 2)
        gather_on(ch + 3, 1)
        gather_on(ch + 4, 0)
        par = lax.rem(ch, 2)
        for phase in (4, 3, 2, 1):
            j = ch - phase

            @pl.when(j >= 0)
            def _():
                old = lax.rem(j + 8, 2)
                if phase == 4:

                    @pl.when(j >= 2)
                    def _():
                        post(flu, old, j - 2).wait_send()

                up_total = lane_u.step(phase, old, before=j >= 1)
                down_total = lane_d.step(phase, old, before=j >= 1)
                if phase == 4:
                    emit_pair(flu, up_total, old, j)
                    emit_own(down_total, j)

        @pl.when(ch >= 1)
        def _():
            lane_u.wait_sent(0, 1 - par)
            lane_d.wait_sent(0, 1 - par)

        for h in range(2):
            col = slice(256 * h, 256 * h + 256)
            keep(lane_u, h, dot_nn(tb[...], dpre[:, col]))
            grad = dot_tn(hid[:, col], xb[...]).astype(BF16)
            for b in range(3):
                part = grad[:, 256 * b : 256 * b + 256].reshape(4, 2, 2, 16, 256)
                rd[h, :, :, :, 16 * b : 16 * b + 16, :] = part
        lane_u.start(0, par)
        lane_d.start(0, par)

        def outer(i, _):
            r = rows(i, 416)
            acc[r, :] += dot_nn(hid[r, :], wd[ch].reshape(512, 768))
            dp = dpre[r, :]
            dsec[r, :] += dot_nt(dp[:, :256], wu[6 + ch, 0].reshape(768, 256)) + dot_nt(
                dp[:, 256:], wu[6 + ch, 1].reshape(768, 256)
            )
            return 0

        lax.fori_loop(0, padded // 416, outer, 0)
        return 0

    lax.fori_loop(0, 6, chunk, 0)

    def drain(lane, phase, j):
        par = j % 2
        pairs = lane is lane_u or j >= 6
        flat = flu if lane is lane_u else fld
        unit = j if lane is lane_u else j + 3
        if phase == 4 and pairs and (lane is lane_u or j >= 8):
            post(flat, par, unit - 2).wait_send()
        total = lane.step(phase, par)
        if phase == 4:
            if pairs:
                emit_pair(flat, total, par, unit)
            else:
                emit_own(total, j)

    def both(*steps):
        for phase, j in steps:
            drain(lane_u, phase, j)
            drain(lane_d, phase, j)

    both((4, 2), (3, 3), (2, 4), (1, 5))

    def second_back(i, _):
        r = rows(i, 208)
        e = dsec[r, :]
        hat = hat2[r, :].astype(F32)
        inverse = inv2[r, :][:, :1]
        lng[2:3, :] += jnp.sum(e * hat, 0, keepdims=True)
        lng[3:4, :] += jnp.sum(e, 0, keepdims=True)
        eg = e * prm[2:3, :]
        m1 = jnp.mean(eg, -1, keepdims=True)
        m2 = jnp.mean(eg * hat, -1, keepdims=True)
        dmid = xb[r, :].astype(F32) + inverse * (eg - m1 - hat * m2)
        dsec[r, :] = dmid
        low = dmid.astype(BF16)
        second[r, :] = low
        hat2[r, :] = acc[r, :].astype(BF16)
        grad = dot_nt(low[:, :256], block(9))
        grad = grad + dot_nt(low[:, 256:512], block(10))
        acc[r, :] = grad + dot_nt(low[:, 512:], block(11))
        return 0

    lax.fori_loop(0, padded // 416, second_back, 0)
    both((4, 3), (3, 4), (2, 5))
    lax.fori_loop(padded // 416, padded // 208, second_back, 0)
    store_out = pltpu.make_async_copy(hat2.at[pl.ds(0, tokens_here)], out_hbm, local.at[0])
    store_out.start()
    load_x = pltpu.make_async_copy(x_hbm, xb.at[pl.ds(0, tokens_here)], local.at[2])
    load_x.start()

    def weight_grad(lane, j, parts):
        lane.wait_sent(0, 1 - j % 2)
        for h, (ref, col) in enumerate(parts):
            keep(lane, h, dot_nn(tb[...], ref[:, 256 * col : 256 * col + 256]))
        lane.start(0, j % 2)

    turn(mixed)
    fetch = pltpu.make_async_copy(dx_hbm, mixed.at[here], local.at[1])
    fetch.start()
    both((4, 4), (3, 5))
    weight_grad(lane_u, 6, ((second, 0), (second, 1)))

    def attend_back(s, _):
        w, pos, valid, live = places(s)
        olds = [acc[w, 128 * j : 128 * j + 128] for j in range(6)]
        vals = [vv[w, 256 * g : 256 * g + 256] for g in range(3)]
        dq_parts, dk_parts, dv_parts = [], [], []
        for g in range(3):
            thin = slice(128 * g, 128 * g + 128)
            diag = diagonal[...]
            pk32 = masked_keys(g, w, live)
            pkm = pk32.astype(BF16)
            st, tot_high, tot_low = state_of(g, w, live, pkm)
            tot = jnp.sum(pk32, 0, keepdims=True)
            pqg = pq[w, thin]
            pq32 = jnp.where(valid, pqg.astype(F32), 0.0)
            num = dot_nn(pqg, st)
            den = dot_nn(pqg, tot_high) + dot_nn(pqg, tot_low)
            share = 1.0 / den
            part = jnp.concatenate([olds[2 * g], olds[2 * g + 1]], 1) * share
            dnum = jnp.where(valid, part, 0.0).astype(BF16)
            e_high, e_low = split_low(jnp.where(valid, -part * (num * share), 0.0))
            dden = dot_nn(e_high, ones_val[...]) + dot_nn(e_low, ones_val[...])
            dpq = dot_nt(dnum, st) + dden * tot
            dst = (dot_tn(pqg, dnum) * diag).astype(BF16)
            dtot = jnp.sum(dden * pq32, 0, keepdims=True)
            dpk = dot_nt(vals[g], dst) + dtot
            dv_parts.append(dot_nn(pkm, dst))
            dq_parts.append(dpq * pq32)
            dk_parts.append(dpk * pk32)
        for j, new in enumerate(dq_parts + dk_parts):
            acc[w, 128 * j : 128 * j + 128] = jnp.where(valid, new, olds[j])
        for g in range(3):
            new = jnp.where(valid, dv_parts[g], vals[g].astype(F32))
            vv[w, 256 * g : 256 * g + 256] = new.astype(BF16)
        return 0

    lax.fori_loop(0, mols // 2, attend_back, 0)
    both((4, 5))
    drain(lane_u, 1, 6)
    lax.fori_loop(mols // 2, mols, attend_back, 0)
    vv[tail, :] = jnp.zeros((spare, 768), BF16)
    drain(lane_u, 2, 6)
    lane_d.wait_sent(0, 1)
    keep(lane_d, 0, dot_nn(tb[...], second[:, 512:768]))
    fetch.wait()
    turn(mixed)
    keep(lane_d, 1, dot_nn(tb[...], vv[:, 0:256]))
    lane_d.start(0, 0)
    weight_grad(lane_u, 7, ((vv, 1), (vv, 2)))
    drain(lane_u, 3, 6)

    def features_back(i, _):
        r = rows(i, 416)
        ct, sn = cosine[r, :], sine[r, :]
        for rot_ref, base in ((rotk, 384), (rotq, 0)):
            for g in range(3):
                wide = slice(256 * g, 256 * g + 256)
                high, low = split_low(acc[r, base + 128 * g : base + 128 * g + 128])
                rot = rot_ref[r, wide].astype(F32)
                total = dot_nt(high, ones_rot[...]) + dot_nt(low, ones_rot[...])
                back = dot_nt(jnp.concatenate([high, high], 1), feats[g])
                back = back + dot_nt(low, feats[g, :, :128]) - rot * total
                a, b = back[:, :128], back[:, 128:]
                turned = jnp.concatenate([a * ct + b * sn, b * ct - a * sn], 1)
                rot_ref[r, wide] = turned.astype(BF16)
        return 0

    lax.fori_loop(0, padded // 832, features_back, 0)
    drain(lane_d, 1, 6)
    drain(lane_u, 4, 6)
    drain(lane_u, 1, 7)
    lax.fori_loop(padded // 832, padded // 416, features_back, 0)
    drain(lane_d, 2, 6)
    drain(lane_u, 2, 7)
    weight_grad(lane_d, 7, ((rotk, 0), (rotk, 1)))
    drain(lane_d, 3, 6)
    drain(lane_u, 3, 7)
    weight_grad(lane_u, 8, ((rotk, 2), (rotq, 0)))
    drain(lane_d, 4, 6)
    drain(lane_u, 4, 7)
    drain(lane_d, 1, 7)
    weight_grad(lane_d, 8, ((rotq, 1), (rotq, 2)))
    drain(lane_d, 2, 7)
    drain(lane_u, 1, 8)

    def first_back(i, _):
        r = rows(i, 208)
        dn = jnp.zeros((208, 768), F32)
        for base, ref in ((0, rotk), (3, vv), (6, rotq)):
            lines = ref[r, :]
            for g in range(3):
                dn = dn + dot_nt(lines[:, 256 * g : 256 * g + 256], block(base + g))
        hat, inverse = norm(xb[r, :].astype(F32))
        lng[0:1, :] += jnp.sum(dn * hat, 0, keepdims=True)
        lng[1:2, :] += jnp.sum(dn, 0, keepdims=True)
        eg = dn * prm[0:1, :]
        m1 = jnp.mean(eg, -1, keepdims=True)
        m2 = jnp.mean(eg * hat, -1, keepdims=True)
        mixed[r, :] = (dsec[r, :] + inverse * (eg - m1 - hat * m2)).astype(BF16)
        return 0

    load_x.wait()
    tiles = padded // 208
    quarter = tiles // 4
    lax.fori_loop(0, quarter, first_back, 0)
    drain(lane_d, 3, 7)
    drain(lane_u, 2, 8)
    drain(lane_d, 1, 8)
    lax.fori_loop(quarter, 2 * quarter, first_back, 0)
    drain(lane_d, 4, 7)
    drain(lane_u, 3, 8)
    drain(lane_d, 2, 8)
    lax.fori_loop(2 * quarter, 3 * quarter, first_back, 0)
    drain(lane_u, 4, 8)
    drain(lane_d, 3, 8)
    lax.fori_loop(3 * quarter, tiles, first_back, 0)
    store_dx = pltpu.make_async_copy(mixed.at[here], dx_hbm, local.at[1])
    store_dx.start()

    ends = lng[...]
    ends = jnp.concatenate([ends, jnp.zeros((8, 128), F32)], 1)
    for i in range(32):
        k, shift = (24 * i) // 128, (24 * i) % 128
        pair = ends[:, 128 * k : 128 * k + 256]
        if shift:
            pair = pltpu.roll(pair, 256 - shift, 1)
        rp[i % 2, i // 8, (i // 4) % 2, (i // 2) % 2] = pair[:, :128]
    store_down = pltpu.make_async_copy(res_d, down_out, local.at[3])
    store_down.start()
    lane_p = Reduce(at, (rp, b1p, sp, b2p, s2p, b3p, s3p, b4p), ps, pr, True)
    lane_p.start(0, 0)
    drain(lane_d, 4, 8)
    for phase in (1, 2, 3):
        lane_p.step(phase, 0, before=False)
    params_out[...] = lane_p.step(4, 0)
    for phase in range(4):
        lane_p.wait_sent(phase, 0)
        lane_u.wait_sent(phase, 0)
        lane_d.wait_sent(phase, 0)
    for flat, par, unit in ((flu, 1, 7), (flu, 0, 8), (fld, 1, 10), (fld, 0, 11)):
        post(flat, par, unit).wait_send()
    for unit in range(12):
        post(flu, 0, unit).wait_recv()
    for unit in units:
        unit.sent()
    params.sent()
    store_wide = pltpu.make_async_copy(res_u, wide_out, local.at[2])
    store_wide.start()
    store_wide.wait()
    store_down.wait()
    store_out.wait()
    store_dx.wait()


def fused_device(
    tokens,
    lengths,
    feature_directions,
    first_gain,
    first_shift,
    query_weight,
    key_weight,
    value_weight,
    out_weight,
    second_gain,
    second_shift,
    up_weight,
    down_weight,
    out_cotangent,
):
    tokens_here, width = tokens.shape
    mols = lengths.shape[0]
    length = tokens_here // mols
    padded = -(-tokens_here // 416) * 416
    share = first_gain.shape[0]

    def halves_first(w):
        return w.reshape(share, 3, 4, 2, 32).transpose(0, 1, 3, 2, 4).reshape(share, width)

    wide = jnp.concatenate(
        [halves_first(key_weight), value_weight, halves_first(query_weight), out_weight], 1
    )
    wide = wide.reshape(share, 6, 2, 256).transpose(1, 2, 0, 3)
    up = up_weight.reshape(share, 16, 2, 6, 16).transpose(3, 2, 0, 1, 4).reshape(6, 2, share, 256)
    wide = jnp.concatenate([wide, up], 0).astype(F32)
    vectors = jnp.stack([first_gain, first_shift, second_gain, second_shift]).astype(F32)
    params = jnp.pad(vectors, ((0, 4), (0, 128 - share)))

    frequency = np.float32(10000.0) ** (-np.arange(32, dtype=np.float32) * np.float32(2.0 / 64))
    angles = (np.arange(padded) % length).astype(np.float32)[:, None] * frequency[None, :]
    scale = 64.0**-0.25
    cosine = jnp.asarray(np.tile(np.cos(angles) * scale, (1, 4)), F32)
    sine = jnp.asarray(np.tile(np.sin(angles) * scale, (1, 4)), F32)
    split = feature_directions.reshape(3, 4, 2, 32, 32)
    eye = jnp.eye(4, dtype=F32)
    packed = split.transpose(0, 2, 1, 3, 4)[:, :, :, :, None, :] * eye[None, None, :, None, :, None]
    packed = packed.reshape(3, 256, 128)
    high = packed.astype(BF16)
    feats = jnp.concatenate([high, (packed - high.astype(F32)).astype(BF16)], 2)
    lane_head = np.arange(128) // 32
    ones_rot = jnp.asarray(np.tile(lane_head, 2)[:, None] == lane_head[None, :], BF16)
    value_head = np.arange(256) // 64
    ones_val = jnp.asarray(value_head[:, None] == lane_head[None, :], BF16)
    diagonal = jnp.asarray(lane_head[:, None] == value_head[None, :], F32)

    def vm(shape, kind):
        return pltpu.VMEM(shape, kind)

    def lane(block, kind, tail):
        return [
            vm((2, 4, 2, 2) + block, kind),
            vm((2, 4, 2, 2) + block, kind),
            vm((4, 2, 2) + block, kind),
            vm((2, 4, 2) + block, kind),
            vm((4, 2) + block, kind),
            vm((2, 4) + block, kind),
            vm((4,) + block, kind),
            vm((2, 3) + block, kind),
        ] + tail

    rows16 = (padded, width)
    scratch = [
        vm((12, 2, 4, 2, 2, 48, 256), BF16),
        vm((6, 2, 4, 2, 2, 16, 768), BF16),
        vm((2, 4, 2, 2, 8, 128), F32),
        vm((12, 24, 256), F32),
        vm(rows16, BF16),
        vm(rows16, BF16),
        vm(rows16, BF16),
        vm(rows16, BF16),
        vm(rows16, BF16),
        vm((padded, 384), BF16),
        vm((padded, 384), BF16),
        vm(rows16, BF16),
        vm(rows16, BF16),
        vm((padded, 128), F32),
        vm(rows16, F32),
        vm(rows16, F32),
        vm((padded, 512), BF16),
        vm((padded, 512), BF16),
        vm((width, padded), BF16),
        vm((8, width), F32),
        vm((8, width), F32),
    ]
    scratch += lane((48, 256), BF16, [vm((2, 2, 24, 256), F32)] * 2)
    scratch += lane((48, 256), BF16, [])
    scratch += lane((8, 128), F32, [])
    scratch += [
        vm((12, 2, 24, 256), F32),
        vm((6, 16, 768), F32),
        pltpu.SemaphoreType.DMA((19, 6)),
        pltpu.SemaphoreType.DMA((19, 6)),
        pltpu.SemaphoreType.DMA,
        pltpu.SemaphoreType.DMA,
    ]
    scratch += [pltpu.SemaphoreType.DMA((2, 6))] * 6 + [pltpu.SemaphoreType.DMA((12,))] * 2
    scratch += [vm((padded, 128), F32), vm((padded, 128), F32), pltpu.SemaphoreType.DMA((4,))]
    spaces = [pl.ANY, pl.ANY, pltpu.SMEM, pltpu.VMEM, pl.ANY, pltpu.VMEM, pl.ANY, pl.ANY] + [pltpu.VMEM] * 4
    kernel = functools.partial(layer_kernel, (tokens_here, padded, length, mols))
    outs = pl.pallas_call(
        kernel,
        out_shape=[
            jax.ShapeDtypeStruct(tokens.shape, BF16),
            jax.ShapeDtypeStruct(tokens.shape, BF16),
            jax.ShapeDtypeStruct((12, 2, share, 256), F32),
            jax.ShapeDtypeStruct((6, 16, width), F32),
            jax.ShapeDtypeStruct((8, 128), F32),
        ],
        in_specs=[pl.BlockSpec(memory_space=s) for s in spaces],
        out_specs=[pl.BlockSpec(memory_space=s) for s in [pl.ANY] * 4 + [pltpu.VMEM]],
        scratch_shapes=scratch,
        compiler_params=pltpu.CompilerParams(
            collective_id=0, has_side_effects=True, vmem_limit_bytes=VMEM_BYTES
        ),
        name="encoder_layer",
    )(
        tokens,
        out_cotangent,
        lengths,
        params,
        wide,
        down_weight,
        cosine,
        sine,
        feats,
        ones_rot,
        ones_val,
        diagonal,
    )
    output, input_grad, wide_grad, down_grad, vector_grad = outs

    def natural(w):
        return w.reshape(share, 3, 2, 4, 32).transpose(0, 1, 3, 2, 4).reshape(share, width)

    def columns(*places):
        return jnp.concatenate([wide_grad[u, h] for u, h in places], 1)

    up_grad = wide_grad[:6].reshape(6, 2, share, 16, 16).transpose(2, 3, 1, 0, 4)
    return (
        output,
        input_grad,
        vector_grad[0, :share],
        vector_grad[1, :share],
        natural(columns((8, 1), (11, 0), (11, 1))),
        natural(columns((10, 0), (10, 1), (8, 0))),
        columns((9, 1), (7, 0), (7, 1)),
        columns((6, 0), (6, 1), (9, 0)),
        vector_grad[2, :share],
        vector_grad[3, :share],
        up_grad.reshape(share, up_weight.shape[1]),
        down_grad.reshape(down_weight.shape),
    )


LAGS = (0, 1, 2, 4)
VMEM_BYTES = 64 * 1024 * 1024


def solution(mesh):
    placed = (
        P("fsdp", None),
        P("fsdp"),
        P(),
        P("fsdp"),
        P("fsdp"),
        P("fsdp", None),
        P("fsdp", None),
        P("fsdp", None),
        P("fsdp", None),
        P("fsdp"),
        P("fsdp"),
        P("fsdp", None),
        P("fsdp", None),
        P("fsdp", None),
    )
    fused = mesh.shape["fsdp"] == 32
    return jax.shard_map(
        fused_device if fused else per_device,
        mesh=mesh,
        in_specs=placed,
        out_specs=(
            P("fsdp", None),
            P("fsdp", None),
            P("fsdp"),
            P("fsdp"),
            P("fsdp", None),
            P("fsdp", None),
            P("fsdp", None),
            P("fsdp", None),
            P("fsdp"),
            P("fsdp"),
            P("fsdp", None),
            P("fsdp", None),
        ),
        check_vma=False,
    )
```

```python
import functools

import jax
import jax.numpy as jnp
import numpy as np
from jax import lax
from jax.experimental import pallas as pl
from jax.experimental.pallas import tpu as pltpu
from jax.sharding import PartitionSpec as P

F32 = jnp.float32
BF16 = jnp.bfloat16


def rotate_scale(vectors):
    half_size = vectors.shape[-1] // 2
    positions = jnp.arange(vectors.shape[1], dtype=jnp.float32)
    frequency = 10000.0 ** (-jnp.arange(half_size, dtype=jnp.float32) * 2.0 / vectors.shape[-1])
    angles = positions[:, None] * frequency[None, :]
    cosine_table = jnp.cos(angles)[None, :, None, :]
    sine_table = jnp.sin(angles)[None, :, None, :]
    first_half = vectors[..., :half_size]
    second_half = vectors[..., half_size:]
    turned = jnp.concatenate(
        [
            first_half * cosine_table - second_half * sine_table,
            first_half * sine_table + second_half * cosine_table,
        ],
        -1,
    )
    return turned * vectors.shape[-1] ** (-0.25)


def feature_map(vectors, directions):
    turned = rotate_scale(vectors)
    logits = jnp.einsum("slhd,hdm->slhm", turned, directions, precision=lax.Precision.HIGHEST)
    logits = logits - 0.5 * jnp.sum(turned * turned, -1, keepdims=True)
    return jnp.exp(logits) * directions.shape[-1] ** (-0.5)


def smooth_gelu(values):
    return jax.nn.gelu(values, approximate=True)


def norm_parts(inputs, gain_row, shift_row):
    row_mean = jnp.mean(inputs, -1, keepdims=True)
    centered = inputs - row_mean
    inverse = lax.rsqrt(jnp.mean(centered * centered, -1, keepdims=True) + 1e-05)
    hat_rows = centered * inverse
    return (
        hat_rows * gain_row.astype(jnp.float32) + shift_row.astype(jnp.float32),
        hat_rows,
        inverse,
    )


def norm_back(grad_rows, hat_rows, inverse, gain_row):
    scaled = grad_rows * gain_row.astype(jnp.float32)
    return inverse * (
        scaled
        - jnp.mean(scaled, -1, keepdims=True)
        - hat_rows * jnp.mean(scaled * hat_rows, -1, keepdims=True)
    )


def per_device(
    tokens,
    lengths,
    feature_directions,
    first_gain,
    first_shift,
    query_weight,
    key_weight,
    value_weight,
    out_weight,
    second_gain,
    second_shift,
    up_weight,
    down_weight,
    out_cotangent,
):
    model_width = tokens.shape[1]
    head_count = feature_directions.shape[0]
    head_size = model_width // head_count
    seqs_here = lengths.shape[0]
    length = tokens.shape[0] // seqs_here
    inputs = tokens.astype(jnp.float32)

    def feature_of(row_block):
        return feature_map(
            row_block.reshape(seqs_here, length, head_count, head_size), feature_directions
        )

    gain_one, shift_one, query_full, key_full, value_full, out_full = (
        lax.all_gather(first_gain, "fsdp", axis=0, tiled=True),
        lax.all_gather(first_shift, "fsdp", axis=0, tiled=True),
        lax.all_gather(query_weight, "fsdp", axis=0, tiled=True),
        lax.all_gather(key_weight, "fsdp", axis=0, tiled=True),
        lax.all_gather(value_weight, "fsdp", axis=0, tiled=True),
        lax.all_gather(out_weight, "fsdp", axis=0, tiled=True),
    )
    normed_wide, hat_one, inverse_one = norm_parts(inputs, gain_one, shift_one)
    normed = normed_wide.astype(jnp.bfloat16)
    query_rows = jnp.dot(normed, query_full, preferred_element_type=jnp.float32)
    key_rows = jnp.dot(normed, key_full, preferred_element_type=jnp.float32)
    value_rows = jnp.dot(normed, value_full, preferred_element_type=jnp.float32)
    value_low = value_rows.astype(jnp.bfloat16).reshape(seqs_here, length, head_count, head_size)
    query_raw, query_back = jax.vjp(feature_of, query_rows)
    key_raw, key_back = jax.vjp(feature_of, key_rows)
    query_low = query_raw.astype(jnp.bfloat16)
    key_low = key_raw.astype(jnp.bfloat16)
    positions = jnp.arange(length, dtype=jnp.int32)
    key_live = positions[None, :] < lengths[:, None]
    masked = key_low * key_live.astype(jnp.bfloat16)[:, :, None, None]
    state_sum = jnp.einsum("slhm,slhd->shmd", masked, value_low, preferred_element_type=jnp.float32)
    state_low = state_sum.astype(jnp.bfloat16)
    totals = jnp.sum(masked.astype(jnp.float32), 1)
    numerator = jnp.einsum(
        "slhm,shmd->slhd", query_low, state_low, preferred_element_type=jnp.float32
    )
    query_wide = query_low.astype(jnp.float32)
    denominator = jnp.einsum("slhm,shm->slh", query_wide, totals, precision=lax.Precision.HIGHEST)
    mixed_rows = (numerator / denominator[..., None]).reshape(-1, model_width).astype(jnp.bfloat16)
    branch = jnp.dot(mixed_rows, out_full, preferred_element_type=jnp.float32)
    middle = inputs + branch
    gain_two, shift_two, up_full, down_full = (
        lax.all_gather(second_gain, "fsdp", axis=0, tiled=True),
        lax.all_gather(second_shift, "fsdp", axis=0, tiled=True),
        lax.all_gather(up_weight, "fsdp", axis=0, tiled=True),
        lax.all_gather(down_weight, "fsdp", axis=0, tiled=True),
    )
    second_wide, hat_two, inverse_two = norm_parts(middle, gain_two, shift_two)
    second = second_wide.astype(jnp.bfloat16)
    up_rows = jnp.dot(second, up_full, preferred_element_type=jnp.float32)
    gelu_rows, gelu_back = jax.vjp(smooth_gelu, up_rows)
    hidden = gelu_rows.astype(jnp.bfloat16)
    output = (middle + jnp.dot(hidden, down_full, preferred_element_type=jnp.float32)).astype(
        jnp.bfloat16
    )
    gain_two, shift_two, up_full, down_full = (
        lax.all_gather(second_gain, "fsdp", axis=0, tiled=True),
        lax.all_gather(second_shift, "fsdp", axis=0, tiled=True),
        lax.all_gather(up_weight, "fsdp", axis=0, tiled=True),
        lax.all_gather(down_weight, "fsdp", axis=0, tiled=True),
    )
    gain_one, shift_one, query_full, key_full, value_full, out_full = (
        lax.all_gather(first_gain, "fsdp", axis=0, tiled=True),
        lax.all_gather(first_shift, "fsdp", axis=0, tiled=True),
        lax.all_gather(query_weight, "fsdp", axis=0, tiled=True),
        lax.all_gather(key_weight, "fsdp", axis=0, tiled=True),
        lax.all_gather(value_weight, "fsdp", axis=0, tiled=True),
        lax.all_gather(out_weight, "fsdp", axis=0, tiled=True),
    )
    down_grad = jnp.einsum("tf,td->fd", hidden, out_cotangent, preferred_element_type=jnp.float32)
    hidden_grad = jnp.einsum(
        "td,fd->tf", out_cotangent, down_full, preferred_element_type=jnp.float32
    )
    pre_grad = gelu_back(hidden_grad)[0].astype(jnp.bfloat16)
    up_grad = jnp.einsum("td,tf->df", second, pre_grad, preferred_element_type=jnp.float32)
    second_grad = jnp.einsum("tf,df->td", pre_grad, up_full, preferred_element_type=jnp.float32)
    gain_two_grad = jnp.sum(second_grad * hat_two, 0)
    shift_two_grad = jnp.sum(second_grad, 0)
    middle_grad = out_cotangent.astype(jnp.float32) + norm_back(
        second_grad, hat_two, inverse_two, gain_two
    )
    ffn_shards = (
        lax.psum_scatter(gain_two_grad, "fsdp", scatter_dimension=0, tiled=True),
        lax.psum_scatter(shift_two_grad, "fsdp", scatter_dimension=0, tiled=True),
        lax.psum_scatter(up_grad, "fsdp", scatter_dimension=0, tiled=True),
        lax.psum_scatter(down_grad, "fsdp", scatter_dimension=0, tiled=True),
    )
    branch_grad = middle_grad.astype(jnp.bfloat16)
    out_grad = jnp.einsum("td,te->de", mixed_rows, branch_grad, preferred_element_type=jnp.float32)
    mixed_grad = jnp.einsum("te,de->td", branch_grad, out_full, preferred_element_type=jnp.float32)
    mixed_grad = mixed_grad.reshape(seqs_here, length, head_count, head_size)
    numer_grad = (mixed_grad / denominator[..., None]).astype(jnp.bfloat16)
    denom_grad = -jnp.sum(mixed_grad * numerator, -1) / (denominator * denominator)
    query_feat_grad = jnp.einsum(
        "slhd,shmd->slhm", numer_grad, state_low, preferred_element_type=jnp.float32
    )
    query_feat_grad = query_feat_grad + denom_grad[..., None] * totals[:, None]
    state_grad = jnp.einsum(
        "slhm,slhd->shmd", query_low, numer_grad, preferred_element_type=jnp.float32
    ).astype(jnp.bfloat16)
    totals_grad = jnp.einsum(
        "slh,slhm->shm", denom_grad, query_wide, precision=lax.Precision.HIGHEST
    )
    key_feat_grad = jnp.einsum(
        "slhd,shmd->slhm", value_low, state_grad, preferred_element_type=jnp.float32
    )
    key_feat_grad = (key_feat_grad + totals_grad[:, None]) * key_live.astype(jnp.float32)[
        :, :, None, None
    ]
    value_grad = jnp.einsum(
        "slhm,shmd->slhd", masked, state_grad, preferred_element_type=jnp.float32
    )
    value_grad = value_grad.reshape(-1, model_width).astype(jnp.bfloat16)
    query_grad = query_back(query_feat_grad)[0].astype(jnp.bfloat16)
    key_grad = key_back(key_feat_grad)[0].astype(jnp.bfloat16)
    normed_grad = jnp.einsum(
        "te,de->td", query_grad, query_full, preferred_element_type=jnp.float32
    )
    normed_grad = normed_grad + jnp.einsum(
        "te,de->td", key_grad, key_full, preferred_element_type=jnp.float32
    )
    normed_grad = normed_grad + jnp.einsum(
        "te,de->td", value_grad, value_full, preferred_element_type=jnp.float32
    )
    query_weight_grad = jnp.einsum(
        "td,te->de", normed, query_grad, preferred_element_type=jnp.float32
    )
    key_weight_grad = jnp.einsum("td,te->de", normed, key_grad, preferred_element_type=jnp.float32)
    value_weight_grad = jnp.einsum(
        "td,te->de", normed, value_grad, preferred_element_type=jnp.float32
    )
    gain_one_grad = jnp.sum(normed_grad * hat_one, 0)
    shift_one_grad = jnp.sum(normed_grad, 0)
    input_grad = middle_grad + norm_back(normed_grad, hat_one, inverse_one, gain_one)
    attn_shards = (
        lax.psum_scatter(gain_one_grad, "fsdp", scatter_dimension=0, tiled=True),
        lax.psum_scatter(shift_one_grad, "fsdp", scatter_dimension=0, tiled=True),
        lax.psum_scatter(query_weight_grad, "fsdp", scatter_dimension=0, tiled=True),
        lax.psum_scatter(key_weight_grad, "fsdp", scatter_dimension=0, tiled=True),
        lax.psum_scatter(value_weight_grad, "fsdp", scatter_dimension=0, tiled=True),
        lax.psum_scatter(out_grad, "fsdp", scatter_dimension=0, tiled=True),
    )
    shards = tuple(attn_shards) + tuple(ffn_shards)
    return (output, input_grad.astype(jnp.bfloat16)) + shards


def dot_nn(a, b):
    return lax.dot_general(a, b, (((1,), (0,)), ((), ())), preferred_element_type=F32)


def dot_nt(a, b):
    return lax.dot_general(a, b, (((1,), (1,)), ((), ())), preferred_element_type=F32)


def dot_tn(a, b):
    return lax.dot_general(a, b, (((0,), (0,)), ((), ())), preferred_element_type=F32)


def split_low(v):
    high = v.astype(BF16)
    return high, (v - high.astype(F32)).astype(BF16)


def remote(src, dst, send, recv, device):
    return pltpu.make_async_remote_copy(
        src_ref=src,
        dst_ref=dst,
        send_sem=send,
        recv_sem=recv,
        device_id=(device,),
        device_id_type=pl.DeviceIdType.MESH,
    )


class Place:
    def __init__(self):
        me = lax.axis_index("fsdp")
        self.c = lax.rem(me, 2)
        self.x = lax.rem(lax.div(me, 2), 2)
        self.y = lax.rem(lax.div(me, 4), 2)
        self.z = lax.div(me, 8)
        self.sib = me + 1 - 2 * self.c
        self.px = me + 2 - 4 * self.x
        self.py = me + 4 - 8 * self.y
        self.zs = [lax.rem(self.z + d, 4) for d in (1, 2, 3)]
        self.pz = [me + (zp - self.z) * 8 for zp in self.zs]

    def greet(self):
        barrier = pltpu.get_barrier_semaphore()
        for peer in [self.sib, self.px, self.py] + self.pz:
            pl.semaphore_signal(
                barrier, inc=1, device_id=(peer,), device_id_type=pl.DeviceIdType.MESH
            )

    def enter(self):
        pl.semaphore_wait(pltpu.get_barrier_semaphore(), 6)


class Gather:
    def __init__(self, at, buf, send, recv, y_first):
        self.buf, self.send, self.recv = buf, send, recv
        c, z, y, x = at.c, at.z, at.y, at.x
        mine = buf.at[c, z, y, x]
        line = buf.at[c, :, y, x]
        plane = buf.at[c, :, :, x] if y_first else buf.at[c, :, y]
        first, second = (at.py, at.px) if y_first else (at.px, at.py)
        self.copies = [
            [remote(mine, mine, send.at[d], recv.at[d], at.pz[d]) for d in range(3)],
            [remote(line, line, send.at[3], recv.at[3], first)],
            [remote(plane, plane, send.at[4], recv.at[4], second)],
            [remote(buf.at[c], buf.at[c], send.at[5], recv.at[5], at.sib)],
        ]

    def start(self, phase):
        for copy in self.copies[phase]:
            copy.start()

    def arrived(self, phase):
        for copy in self.copies[phase]:
            copy.wait_recv()

    def sent(self):
        for phase in self.copies:
            for copy in phase:
                copy.wait_send()


class Reduce:
    def __init__(self, at, refs, send, recv, y_first):
        self.at, self.y_first = at, y_first
        self.R, self.B1, self.S, self.B2, self.S2, self.B3, self.S3, self.B4 = refs
        self.send, self.recv = send, recv

    def copies(self, phase, par):
        at, s, r = self.at, self.send.at[par], self.recv.at[par]
        first, second = (at.py, at.px) if self.y_first else (at.px, at.py)
        if phase == 0:
            return [remote(self.R.at[1 - at.c], self.B1.at[par], s.at[0], r.at[0], at.sib)]
        if phase == 1:
            src = self.S.at[:, 1 - at.y] if self.y_first else self.S.at[:, :, 1 - at.x]
            return [remote(src, self.B2.at[par], s.at[1], r.at[1], first)]
        if phase == 2:
            src = self.S2.at[:, 1 - (at.x if self.y_first else at.y)]
            return [remote(src, self.B3.at[par], s.at[2], r.at[2], second)]
        return [
            remote(self.S3.at[at.zs[d]], self.B4.at[par, d], s.at[3 + d], r.at[3 + d], at.pz[d])
            for d in range(3)
        ]

    def start(self, phase, par):
        for copy in self.copies(phase, par):
            copy.start()

    def wait_sent(self, phase, par):
        for copy in self.copies(phase, par):
            copy.wait_send()

    def step(self, phase, par, before=True):
        at = self.at
        for copy in self.copies(phase - 1, par):
            copy.wait_recv()
        if phase == 4:
            total = self.S3[at.z].astype(F32)
            for d in range(3):
                total = total + self.B4[par, d].astype(F32)
            return total
        if before is True:
            self.wait_sent(phase, 1 - par)
        elif before is not False:

            @pl.when(before)
            def _():
                self.wait_sent(phase, 1 - par)

        kind = self.S.dtype

        def add(i, _):
            if phase == 1:
                own, other, out = self.R[at.c, i], self.B1[par, i], self.S
            elif phase == 2:
                own = self.S[i, at.y] if self.y_first else self.S[i, :, at.x]
                other, out = self.B2[par, i], self.S2
            else:
                own = self.S2[i, at.x if self.y_first else at.y]
                other, out = self.B3[par, i], self.S3
            out[i] = (own.astype(F32) + other.astype(F32)).astype(kind)
            return 0

        lax.fori_loop(0, 4, add, 0)
        self.start(phase, par)
        return None


def layer_kernel(
    sizes,
    x_hbm,
    dy_hbm,
    lengths,
    params_here,
    key_here,
    value_here,
    query_here,
    mix_here,
    up_here,
    down_here,
    directions,
    cosine_hbm,
    sine_hbm,
    ones_rot,
    ones_val,
    diagonal,
    out_hbm,
    dx_hbm,
    key_out,
    value_out,
    query_out,
    mix_out,
    up_out,
    down_out,
    params_out,
    wu,
    wd,
    pb,
    px32,
    xb,
    normed,
    rotq,
    rotk,
    vv,
    pq,
    pk,
    mixed,
    second,
    inv2,
    acc,
    dsec,
    dpre,
    tb,
    prm,
    lng,
    ru,
    b1u,
    b2u,
    b3u,
    b4u,
    flu,
    fld,
    rd,
    b1d,
    b2d,
    b3d,
    b4d,
    rp,
    b1p,
    sp,
    b2p,
    s2p,
    b3p,
    s3p,
    b4p,
    res_u,
    ag_send,
    ag_recv,
    pre_send,
    pre_recv,
    us,
    ur,
    ds_,
    dr,
    ps,
    pr,
    qs,
    qr,
    cosine,
    sine,
    feats,
    local,
):
    tokens_here, padded, length, mols = sizes
    spare = padded - tokens_here
    at = Place()
    at.greet()
    hid = mixed
    load_x = pltpu.make_async_copy(x_hbm, xb.at[pl.ds(0, tokens_here)], local.at[0])
    load_dy = pltpu.make_async_copy(dy_hbm, xb.at[pl.ds(0, tokens_here)], local.at[0])
    load_x.start()
    load_cos = pltpu.make_async_copy(cosine_hbm, cosine, local.at[2])
    load_sin = pltpu.make_async_copy(sine_hbm, sine, local.at[3])
    load_cos.start()
    load_sin.start()

    def halves_pick():
        t = lax.broadcasted_iota(jnp.int32, (1, 256), 1)
        source = ((t & 127) >> 5) * 64 + (t >> 7) * 32 + (t & 31)
        row = lax.broadcasted_iota(jnp.int32, (256, 256), 0)
        return jnp.where(row == source, 1.0, 0.0).astype(BF16)

    picks = [hid.at[0:768, 0:256], hid.at[0:768, 256:512], dpre.at[0:768, 0:256]]

    def hidden_pick():
        for b in range(3):
            t = lax.broadcasted_iota(jnp.int32, (1, 256), 1) + 256 * b
            owner = 2 * ((t & 63) >> 4) + ((t & 127) >> 6)
            source = 96 * owner + 16 * (t >> 7) + (t & 15)

            def fill(i, _):
                row = lax.broadcasted_iota(jnp.int32, (128, 256), 0) + 128 * i
                r = pl.ds(pl.multiple_of(128 * i, 128), 128)
                picks[b][r, :] = jnp.where(row == source, 1.0, 0.0).astype(BF16)
                return 0

            lax.fori_loop(0, 6, fill, 0)

    halves = halves_pick()
    for g in range(3):
        col = slice(256 * g, 256 * g + 256)
        for base, ref in ((0, key_here), (6, query_here)):
            res_u[(base + g) // 2, (base + g) % 2] = dot_nn(ref[:, col], halves)
        for base, ref in ((3, value_here), (9, mix_here)):
            res_u[(base + g) // 2, (base + g) % 2] = ref[:, col].astype(F32)
    pb[at.c, at.z, at.y, at.x] = params_here[...]
    for ch in range(6):
        wd[ch, at.c, at.z, at.y, at.x] = down_here[16 * ch : 16 * ch + 16, :]
    at.enter()

    def swap_of(k):
        half = pl.ds(6 * k, 6)
        src = res_u.at[half, 1 - at.c]
        return remote(src, px32.at[half], pre_send.at[k], pre_recv.at[k], at.sib)

    swaps = [swap_of(k) for k in range(2)]
    swaps[0].start()
    up32 = up_here[...].astype(F32)
    stacked = jnp.concatenate([up32[:, 768 * i : 768 * i + 768] for i in range(4)], 0)
    hidden_pick()
    stacked = stacked.astype(BF16)
    order = jnp.concatenate([dot_nn(stacked, pick[...]) for pick in picks], 1)
    for ch in range(6):
        for h in range(2):
            at_col = 128 * ch + 64 * h
            res_u[6 + ch, h] = jnp.concatenate(
                [order[24 * i : 24 * i + 24, at_col : at_col + 64] for i in range(4)], 1
            )
    swaps[1].start()
    swaps[0].wait()
    even = at.c == 0

    def build(u, _):
        mine = res_u[u, at.c]
        other = px32[u]
        top = jnp.where(even, mine, other)
        low = jnp.where(even, other, mine)
        wu[u, at.c, at.z, at.y, at.x] = jnp.concatenate([top, low], 0).astype(BF16)
        return 0

    lax.fori_loop(0, 6, build, 0)
    tail = pl.ds(tokens_here, spare)
    xb[tail, :] = jnp.zeros((spare, xb.shape[1]), BF16)
    mixed[tail, :] = jnp.zeros((spare, xb.shape[1]), BF16)
    lng[...] = jnp.zeros(lng.shape, F32)
    tb[768:784, :] = jnp.ones((16, padded), BF16)

    def gather_unit(u):
        if u < 6:
            buf = wu.at[u]
        else:
            buf = wu.at[6 + (u - 6) // 2] if u % 2 == 0 else wd.at[(u - 6) // 2]
        return Gather(at, buf, ag_send.at[u], ag_recv.at[u], u % 2 == 0)

    units = [gather_unit(u) for u in range(18)]
    params = Gather(at, pb, ag_send.at[18], ag_recv.at[18], True)
    state = {"tick": 0, "needed": set()}
    lags, last = LAGS, (13, 11, 9, 7)

    def tick(count=1):
        for _ in range(count):
            t = state["tick"]
            state["tick"] += 1
            if t == 0:
                params.start(0)
            for k in range(4):
                u = t - lags[k]
                if 0 <= u <= last[k]:
                    if k:
                        if u == 0:
                            params.arrived(k - 1)
                            params.start(k)
                        units[u].arrived(k - 1)
                    units[u].start(k)

    def need(u):
        while state["tick"] <= u + lags[3]:
            tick()
        if u not in state["needed"]:
            state["needed"].add(u)
            units[u].arrived(3)

    tick(1)
    swaps[1].wait()
    lax.fori_loop(6, 12, build, 0)
    tick(1)
    for g in range(3):
        for half in range(2):
            lines = []
            for hh in range(4):
                at_row = 64 * (4 * g + hh) + 32 * half
                piece = directions[at_row : at_row + 32, :]
                gap = jnp.zeros((32, 32), F32)
                lines.append(jnp.concatenate([gap] * hh + [piece] + [gap] * (3 - hh), 1))
            high, low = split_low(jnp.concatenate(lines, 0))
            feats[g, 128 * half : 128 * half + 128, :] = jnp.concatenate([high, low], 1)

    def rows(i, count):
        return pl.ds(pl.multiple_of(i * count, 16), count)

    def norm(v):
        centered = v - jnp.mean(v, -1, keepdims=True)
        inverse = lax.rsqrt(jnp.mean(centered * centered, -1, keepdims=True) + 1e-05)
        return centered * inverse, inverse

    load_x.wait()
    load_cos.wait()
    load_sin.wait()

    def first_hat(i, _):
        r = rows(i, 208)
        acc[r, :] = norm(xb[r, :].astype(F32))[0]
        return 0

    lax.fori_loop(0, padded // 208, first_hat, 0)
    tick(lags[3] - 1)
    params.arrived(3)
    parts = [jnp.zeros((8, 128), F32) for _ in range(7)]
    for i in range(32):
        block = pb[i % 2, i // 8, (i // 4) % 2, (i // 2) % 2]
        k, shift = (24 * i) // 128, (24 * i) % 128
        pair = jnp.concatenate([block, jnp.zeros((8, 128), F32)], 1)
        if shift:
            pair = pltpu.roll(pair, shift, 1)
        parts[k] = parts[k] + pair[:, :128]
        parts[k + 1] = parts[k + 1] + pair[:, 128:]
    prm[...] = jnp.concatenate(parts[:6], 1)

    def first_norm(i, _):
        r = rows(i, 208)
        normed[r, :] = (acc[r, :] * prm[0:1, :] + prm[1:2, :]).astype(BF16)
        return 0

    lax.fori_loop(0, padded // 208, first_norm, 0)

    def block(b):
        return wu[b // 2, b % 2].reshape(768, 256)

    def features(base, rot_ref, feat_ref, part):
        def body(i, _):
            r = rows(i, 416)
            lines = normed[r, :]
            ct, st = cosine[r, :], sine[r, :]
            for g in range(3):
                u = dot_nn(lines, block(base + g))
                a, b = u[:, :128], u[:, 128:]
                rot = jnp.concatenate([a * ct - b * st, a * st + b * ct], 1)
                high, low = split_low(rot)
                sq_high, sq_low = split_low(rot * rot)
                two = dot_nn(high, feats[g])
                logits = two[:, :128] + two[:, 128:] + dot_nn(low, feats[g, :, :128])
                norms = dot_nn(sq_high, ones_rot[...]) + dot_nn(sq_low, ones_rot[...])
                p = jnp.exp(logits - 0.5 * norms) * (32**-0.5)
                rot_ref[r, 256 * g : 256 * g + 256] = high
                feat_ref[r, 128 * g : 128 * g + 128] = p.astype(BF16)
            return 0

        half = padded // 832
        lax.fori_loop(part * half, part * half + half, body, 0)

    need(0)
    need(1)
    features(0, rotk, pk, 0)
    tick()
    features(0, rotk, pk, 1)
    tick()
    need(2)

    def values(i, _):
        r = rows(i, 416)
        for g in range(3):
            vv[r, 256 * g : 256 * g + 256] = dot_nn(normed[r, :], block(3 + g)).astype(BF16)
        return 0

    lax.fori_loop(0, padded // 416, values, 0)
    tick()
    need(3)
    need(4)
    features(6, rotq, pq, 0)
    tick()
    features(6, rotq, pq, 1)
    tick()
    here = pl.ds(0, tokens_here)
    spill = pltpu.make_async_copy(normed.at[here], dx_hbm, local.at[1])
    spill.start()
    hat2 = normed

    window = 224

    def places(s):
        begin = lax.div(s * length, 16) * 16
        pos = lax.broadcasted_iota(jnp.int32, (window, 1), 0) - (s * length - begin)
        valid = (pos >= 0) & (pos < length)
        live = valid & (pos < lengths[s])
        return pl.ds(pl.multiple_of(begin, 16), window), pos, valid, live

    def state_of(g, w, live, pkm):
        ones = jnp.ones((window, 256), BF16)
        diag = diagonal[...]
        st = (dot_tn(pkm, vv[w, 256 * g : 256 * g + 256]) * diag).astype(BF16)
        tot = dot_tn(pkm, ones) * diag
        tot_high, tot_low = split_low(tot)
        return st, tot_high, tot_low

    def masked_keys(g, w, live):
        keys = pk[w, 128 * g : 128 * g + 128].astype(F32)
        return jnp.where(live, keys, 0.0)

    def attend(s, _):
        w, pos, valid, live = places(s)
        mixes = []
        for g in range(3):
            pkm = masked_keys(g, w, live).astype(BF16)
            st, tot_high, tot_low = state_of(g, w, live, pkm)
            pqg = pq[w, 128 * g : 128 * g + 128]
            num = dot_nn(pqg, st)
            den = dot_nn(pqg, tot_high) + dot_nn(pqg, tot_low)
            mixes.append(jnp.where(valid, num / den, 0.0))
        mix = jnp.where(pos < 0, mixed[w, :].astype(F32), jnp.concatenate(mixes, 1))
        mixed[w, :] = mix.astype(BF16)
        return 0

    lax.fori_loop(0, mols // 2, attend, 0)
    tick()
    lax.fori_loop(mols // 2, mols, attend, 0)
    need(5)
    tick()
    spill.wait()

    def project(i, _):
        r = rows(i, 208)
        lines = mixed[r, :]
        branch = jnp.concatenate([dot_nn(lines, block(9 + g)) for g in range(3)], 1)
        middle = xb[r, :].astype(F32) + branch
        acc[r, :] = middle
        hat, inverse = norm(middle)
        hat2[r, :] = hat.astype(BF16)
        inv2[r, :] = jnp.broadcast_to(inverse, (208, 128))
        second[r, :] = (hat * prm[2:3, :] + prm[3:4, :]).astype(BF16)
        dsec[r, :] = jnp.zeros((208, 768), F32)
        return 0

    lax.fori_loop(0, padded // 416, project, 0)
    tick()
    lax.fori_loop(padded // 416, padded // 208, project, 0)

    def turn(src):
        for j in range(6):
            tb[128 * j : 128 * j + 128, :] = src[:, 128 * j : 128 * j + 128].T

    spill_mixed = pltpu.make_async_copy(mixed.at[here], out_hbm, local.at[2])
    spill_mixed.start()
    load_dy.start()
    turn(second)
    load_dy.wait()
    spill_mixed.wait()
    while state["tick"] <= last[0] + lags[0]:
        tick()
    need(6)
    need(7)

    def pair_of(q):
        up, down = 6 + 2 * q, 7 + 2 * q
        return (
            Gather(at, wu.at[6 + q], ag_send.at[up], ag_recv.at[up], True),
            Gather(at, wd.at[q], ag_send.at[down], ag_recv.at[down], False),
        )

    def gather_on(q, phase):
        @pl.when(q < 6)
        def _():
            for unit in pair_of(q):
                if phase:
                    unit.arrived(phase - 1)
                unit.start(phase)

    su, sd = wu.at[6, 0], wu.at[6, 1]
    s2u, s2d = wu.at[7, 0, :, 0], wu.at[7, 0, :, 1]
    s3u, s3d = wu.at[7, 1, :, 0, 0], wu.at[7, 1, :, 0, 1]
    lane_u = Reduce(at, (ru, b1u, su, b2u, s2u, b3u, s3u, b4u), us, ur, True)
    lane_d = Reduce(at, (rd, b1d, sd, b2d, s2d, b3d, s3d, b4d), ds_, dr, False)

    def post(flat, par, unit):
        return remote(
            flat.at[par, 1 - at.c], res_u.at[unit, at.c], qs.at[unit], qr.at[unit], at.sib
        )

    def emit_pair(flat, total, par, unit):
        flat[par] = total.reshape(flat.shape[1:])
        res_u[unit, at.c] = flat[par, at.c]
        post(flat, par, unit).start()

    def emit_own(total, unit):
        for b in range(3):
            r = pl.ds(pl.multiple_of(16 * unit, 16), 16)
            down_out[r, 256 * b : 256 * b + 256] = total[16 * b : 16 * b + 16]

    def keep(lane, half, grad):
        lane.R[half] = grad.astype(BF16).reshape(4, 2, 2, 48, 256)

    slope = 0.7978845608028654
    bend = 0.044715

    def chunk(ch, _):
        def inner(i, _):
            r = rows(i, 416)
            lines, cot = second[r, :], xb[r, :]
            for h in range(2):
                pre = dot_nn(lines, wu[6 + ch, h].reshape(768, 256))
                dh = dot_nt(cot, wd[ch, h].reshape(256, 768))
                square = pre * pre
                t = jnp.tanh(pre * (slope + slope * bend * square))
                half = 0.5 + 0.5 * t
                col = slice(256 * h, 256 * h + 256)
                hid[r, col] = (pre * half).astype(BF16)
                bent = slope + 3.0 * slope * bend * square
                grad = half + 0.5 * pre * (1.0 - t * t) * bent
                dpre[r, col] = (dh * grad).astype(BF16)
            return 0

        @pl.when(ch >= 1)
        def _():
            for unit in pair_of(ch):
                unit.arrived(3)

        lax.fori_loop(0, padded // 416, inner, 0)
        gather_on(ch + 1, 3)
        gather_on(ch + 2, 2)
        gather_on(ch + 3, 1)
        gather_on(ch + 4, 0)
        par = lax.rem(ch, 2)
        for k in (1, 2):

            @pl.when(ch == k)
            def _():
                units[4 + 2 * k].sent()

        for phase in (4, 3, 2, 1):
            j = ch - phase

            @pl.when(j >= 0)
            def _():
                old = lax.rem(j + 8, 2)
                if phase == 4:

                    @pl.when(j >= 2)
                    def _():
                        post(flu, old, j - 2).wait_send()

                up_total = lane_u.step(phase, old, before=j >= 1)
                down_total = lane_d.step(phase, old, before=j >= 1)
                if phase == 4:
                    emit_pair(flu, up_total, old, j)
                    emit_own(down_total, j)

        @pl.when(ch >= 1)
        def _():
            lane_u.wait_sent(0, 1 - par)
            lane_d.wait_sent(0, 1 - par)

        for h in range(2):
            col = slice(256 * h, 256 * h + 256)
            keep(lane_u, h, dot_nn(tb[:768, :], dpre[:, col]))
            grad = dot_tn(hid[:, col], xb[...]).astype(BF16)
            for b in range(3):
                part = grad[:, 256 * b : 256 * b + 256].reshape(4, 2, 2, 16, 256)
                rd[h, :, :, :, 16 * b : 16 * b + 16, :] = part
        lane_u.start(0, par)
        lane_d.start(0, par)

        def outer(i, _):
            r = rows(i, 416)
            acc[r, :] += dot_nn(hid[r, 0:512], wd[ch].reshape(512, 768))
            dp = dpre[r, :]
            dsec[r, :] += dot_nt(dp[:, :256], wu[6 + ch, 0].reshape(768, 256)) + dot_nt(
                dp[:, 256:], wu[6 + ch, 1].reshape(768, 256)
            )
            return 0

        lax.fori_loop(0, padded // 416, outer, 0)
        return 0

    lax.fori_loop(0, 6, chunk, 0)
    fetch_mixed = pltpu.make_async_copy(out_hbm, mixed.at[here], local.at[2])
    fetch_mixed.start()

    def drain(lane, phase, j):
        par = j % 2
        pairs = lane is lane_u or j >= 6
        flat = flu if lane is lane_u else fld
        unit = j if lane is lane_u else j + 3
        if phase == 4 and pairs and (lane is lane_u or j >= 8):
            post(flat, par, unit - 2).wait_send()
        total = lane.step(phase, par)
        if phase == 4:
            if pairs:
                emit_pair(flat, total, par, unit)
            else:
                emit_own(total, j)

    def both(*steps):
        for phase, j in steps:
            drain(lane_u, phase, j)
            drain(lane_d, phase, j)

    both((4, 2), (3, 3), (2, 4), (1, 5))

    def second_back(i, _):
        r = rows(i, 208)
        e = dsec[r, :]
        hat = hat2[r, :].astype(F32)
        inverse = inv2[r, :][:, :1]
        lng[2:3, :] += jnp.sum(e * hat, 0, keepdims=True)
        lng[3:4, :] += jnp.sum(e, 0, keepdims=True)
        eg = e * prm[2:3, :]
        m1 = jnp.mean(eg, -1, keepdims=True)
        m2 = jnp.mean(eg * hat, -1, keepdims=True)
        dmid = xb[r, :].astype(F32) + inverse * (eg - m1 - hat * m2)
        dsec[r, :] = dmid
        low = dmid.astype(BF16)
        second[r, :] = low
        hat2[r, :] = acc[r, :].astype(BF16)
        grad = dot_nt(low[:, :256], block(9))
        grad = grad + dot_nt(low[:, 256:512], block(10))
        acc[r, :] = grad + dot_nt(low[:, 512:], block(11))
        return 0

    lax.fori_loop(0, padded // 416, second_back, 0)
    both((4, 3), (3, 4), (2, 5))
    lax.fori_loop(padded // 416, padded // 208, second_back, 0)
    store_out = pltpu.make_async_copy(hat2.at[pl.ds(0, tokens_here)], out_hbm, local.at[0])
    fetch_mixed.wait()
    store_out.start()
    load_x = pltpu.make_async_copy(x_hbm, xb.at[pl.ds(0, tokens_here)], local.at[2])
    load_x.start()

    def weight_grad(lane, j, parts):
        lane.wait_sent(0, 1 - j % 2)
        for h, (ref, col, base) in enumerate(parts):
            keep(lane, h, grad_of(ref, col, base))
        lane.start(0, j % 2)

    def grad_of(ref, col, base):
        lines = ref[:, 256 * col : 256 * col + 256]
        if base is None:
            return dot_nn(tb[:768, :], lines)
        both_of = dot_nn(tb[...], lines)
        grad, sums = both_of[:768], both_of[768:769]
        weight = block(base + col).astype(F32)
        share = weight * grad
        gain_col[...] += share[:, :128] + share[:, 128:]
        share = weight * sums
        shift_col[...] += share[:, :128] + share[:, 128:]
        return grad

    gain_col, shift_col = inv2.at[0:768], inv2.at[768:1536]
    inv2[0:1536, :] = jnp.zeros((1536, 128), F32)
    turn(mixed)
    fetch = pltpu.make_async_copy(dx_hbm, mixed.at[here], local.at[1])
    fetch.start()
    both((4, 4), (3, 5))
    weight_grad(lane_u, 6, ((second, 0, None), (second, 1, None)))

    def attend_back(s, _):
        w, pos, valid, live = places(s)
        olds = [acc[w, 128 * j : 128 * j + 128] for j in range(6)]
        vals = [vv[w, 256 * g : 256 * g + 256] for g in range(3)]
        dq_parts, dk_parts, dv_parts = [], [], []
        for g in range(3):
            thin = slice(128 * g, 128 * g + 128)
            diag = diagonal[...]
            pk32 = masked_keys(g, w, live)
            pkm = pk32.astype(BF16)
            st, tot_high, tot_low = state_of(g, w, live, pkm)
            tot = jnp.sum(pk32, 0, keepdims=True)
            pqg = pq[w, thin]
            pq32 = jnp.where(valid, pqg.astype(F32), 0.0)
            num = dot_nn(pqg, st)
            den = dot_nn(pqg, tot_high) + dot_nn(pqg, tot_low)
            share = 1.0 / den
            part = jnp.concatenate([olds[2 * g], olds[2 * g + 1]], 1) * share
            dnum = jnp.where(valid, part, 0.0).astype(BF16)
            e_high, e_low = split_low(jnp.where(valid, -part * (num * share), 0.0))
            dden = dot_nn(e_high, ones_val[...]) + dot_nn(e_low, ones_val[...])
            dpq = dot_nt(dnum, st) + dden * tot
            dst = (dot_tn(pqg, dnum) * diag).astype(BF16)
            dtot = jnp.sum(dden * pq32, 0, keepdims=True)
            dpk = dot_nt(vals[g], dst) + dtot
            dv_parts.append(dot_nn(pkm, dst))
            dq_parts.append(dpq * pq32)
            dk_parts.append(dpk * pk32)
        for j, new in enumerate(dq_parts + dk_parts):
            acc[w, 128 * j : 128 * j + 128] = jnp.where(valid, new, olds[j])
        for g in range(3):
            new = jnp.where(valid, dv_parts[g], vals[g].astype(F32))
            vv[w, 256 * g : 256 * g + 256] = new.astype(BF16)
        return 0

    lax.fori_loop(0, mols // 2, attend_back, 0)
    both((4, 5))
    drain(lane_u, 1, 6)
    lax.fori_loop(mols // 2, mols, attend_back, 0)
    vv[tail, :] = jnp.zeros((spare, 768), BF16)
    drain(lane_u, 2, 6)
    lane_d.wait_sent(0, 1)
    keep(lane_d, 0, grad_of(second, 2, None))
    fetch.wait()
    turn(mixed)
    keep(lane_d, 1, grad_of(vv, 0, 3))
    lane_d.start(0, 0)
    weight_grad(lane_u, 7, ((vv, 1, 3), (vv, 2, 3)))
    drain(lane_u, 3, 6)

    def unpick(lines, pick):
        high, rest = lines.astype(BF16), lines
        parts = [high]
        for _ in range(2):
            rest = rest - parts[-1].astype(F32)
            parts.append(rest.astype(BF16))
        count = lines.shape[0]
        wide = jnp.concatenate([part.astype(F32) for part in parts], 0).astype(BF16)
        out = pick(wide)
        return out[:count] + out[count : 2 * count] + out[2 * count :]

    def features_back(i, _):
        r = rows(i, 416)
        ct, sn = cosine[r, :], sine[r, :]
        for rot_ref, base in ((rotk, 384), (rotq, 0)):
            for g in range(3):
                wide = slice(256 * g, 256 * g + 256)
                high, low = split_low(acc[r, base + 128 * g : base + 128 * g + 128])
                rot = rot_ref[r, wide].astype(F32)
                total = dot_nt(high, ones_rot[...]) + dot_nt(low, ones_rot[...])
                back = dot_nt(jnp.concatenate([high, high], 1), feats[g])
                back = back + dot_nt(low, feats[g, :, :128]) - rot * total
                a, b = back[:, :128], back[:, 128:]
                turned = jnp.concatenate([a * ct + b * sn, b * ct - a * sn], 1)
                rot_ref[r, wide] = turned.astype(BF16)
        return 0

    lax.fori_loop(0, padded // 832, features_back, 0)
    drain(lane_d, 1, 6)
    drain(lane_u, 4, 6)
    drain(lane_u, 1, 7)
    lax.fori_loop(padded // 832, padded // 416, features_back, 0)
    for unit in range(6):
        post(flu, 0, unit).wait_recv()
    lines = []
    for i in range(4):
        cols = slice(64 * i, 64 * i + 64)
        lines.append(jnp.concatenate([res_u[ch, h, :, cols] for ch in range(6) for h in range(2)], 1))
    hidden_pick()

    def hidden_back(wide):
        out = dot_nt(wide[:, :256], picks[0][...])
        out = out + dot_nt(wide[:, 256:512], picks[1][...])
        return out + dot_nt(wide[:, 512:], picks[2][...])

    back = unpick(jnp.concatenate(lines, 0), hidden_back)
    for i in range(4):
        up_out[:, 768 * i : 768 * i + 768] = back[24 * i : 24 * i + 24]
    drain(lane_d, 2, 6)
    drain(lane_u, 2, 7)
    weight_grad(lane_d, 7, ((rotk, 0, 0), (rotk, 1, 0)))
    drain(lane_d, 3, 6)
    drain(lane_u, 3, 7)
    weight_grad(lane_u, 8, ((rotk, 2, 0), (rotq, 0, 6)))
    drain(lane_d, 4, 6)
    drain(lane_u, 4, 7)
    drain(lane_d, 1, 7)
    weight_grad(lane_d, 8, ((rotq, 1, 6), (rotq, 2, 6)))
    shift_row = jnp.sum(shift_col[...].T, 0, keepdims=True)
    gain_row = jnp.sum(gain_col[...].T, 0, keepdims=True)
    gain_row = (gain_row - prm[1:2, :] * shift_row) / prm[0:1, :]
    ends = jnp.concatenate([gain_row, shift_row, lng[2:8, :]], 0)
    ends = jnp.concatenate([ends, jnp.zeros((8, 128), F32)], 1)
    for i in range(32):
        k, shift = (24 * i) // 128, (24 * i) % 128
        pair = ends[:, 128 * k : 128 * k + 256]
        if shift:
            pair = pltpu.roll(pair, 256 - shift, 1)
        rp[i % 2, i // 8, (i // 4) % 2, (i // 2) % 2] = pair[:, :128]
    lane_p = Reduce(at, (rp, b1p, sp, b2p, s2p, b3p, s3p, b4p), ps, pr, True)
    lane_p.start(0, 0)
    drain(lane_d, 2, 7)
    drain(lane_u, 1, 8)

    def first_back(i, _):
        r = rows(i, 208)
        dn = jnp.zeros((208, 768), F32)
        for base, ref in ((0, rotk), (3, vv), (6, rotq)):
            lines = ref[r, :]
            for g in range(3):
                dn = dn + dot_nt(lines[:, 256 * g : 256 * g + 256], block(base + g))
        hat, inverse = norm(xb[r, :].astype(F32))
        eg = dn * prm[0:1, :]
        m1 = jnp.mean(eg, -1, keepdims=True)
        m2 = jnp.mean(eg * hat, -1, keepdims=True)
        mixed[r, :] = (dsec[r, :] + inverse * (eg - m1 - hat * m2)).astype(BF16)
        return 0

    load_x.wait()
    tiles = padded // 208
    quarter = tiles // 4
    lax.fori_loop(0, quarter, first_back, 0)
    drain(lane_d, 3, 7)
    drain(lane_u, 2, 8)
    drain(lane_d, 1, 8)
    lane_p.step(1, 0, before=False)
    lax.fori_loop(quarter, 2 * quarter, first_back, 0)
    drain(lane_d, 4, 7)
    drain(lane_u, 3, 8)
    drain(lane_d, 2, 8)
    lane_p.step(2, 0, before=False)
    lax.fori_loop(2 * quarter, 3 * quarter, first_back, 0)
    drain(lane_u, 4, 8)
    drain(lane_d, 3, 8)
    lane_p.step(3, 0, before=False)
    lax.fori_loop(3 * quarter, tiles, first_back, 0)
    store_dx = pltpu.make_async_copy(mixed.at[here], dx_hbm, local.at[1])
    store_dx.start()

    drain(lane_d, 4, 8)
    params_out[...] = lane_p.step(4, 0)
    for phase in range(4):
        lane_p.wait_sent(phase, 0)
        lane_u.wait_sent(phase, 0)
        lane_d.wait_sent(phase, 0)
    for flat, par, unit in ((flu, 1, 7), (flu, 0, 8), (fld, 1, 10), (fld, 0, 11)):
        post(flat, par, unit).wait_send()
    for unit in range(6, 12):
        post(flu, 0, unit).wait_recv()
    for u, unit in enumerate(units):
        if u not in (6, 8):
            unit.sent()
    params.sent()
    turned = unpick(
        jnp.concatenate(
            [res_u[u, h] for u, h in ((10, 0), (10, 1), (8, 0), (8, 1), (11, 0), (11, 1))], 0
        ),
        lambda wide: dot_nt(wide, halves_pick()),
    )
    for g in range(3):
        col = slice(256 * g, 256 * g + 256)
        key_out[:, col] = turned[24 * g : 24 * g + 24]
        query_out[:, col] = turned[72 + 24 * g : 96 + 24 * g]
        u, h = ((9, 1), (7, 0), (7, 1))[g]
        value_out[:, col] = res_u[u, h]
        u, h = ((6, 0), (6, 1), (9, 0))[g]
        mix_out[:, col] = res_u[u, h]
    store_out.wait()
    store_dx.wait()


def fused_device(
    tokens,
    lengths,
    feature_directions,
    first_gain,
    first_shift,
    query_weight,
    key_weight,
    value_weight,
    out_weight,
    second_gain,
    second_shift,
    up_weight,
    down_weight,
    out_cotangent,
):
    tokens_here, width = tokens.shape
    mols = lengths.shape[0]
    length = tokens_here // mols
    padded = -(-tokens_here // 416) * 416
    share = first_gain.shape[0]

    vectors = jnp.stack([first_gain, first_shift, second_gain, second_shift]).astype(F32)
    params = jnp.pad(vectors, ((0, 4), (0, 128 - share)))

    frequency = np.float32(10000.0) ** (-np.arange(32, dtype=np.float32) * np.float32(2.0 / 64))
    angles = (np.arange(padded) % length).astype(np.float32)[:, None] * frequency[None, :]
    scale = 64.0**-0.25
    cosine = jnp.asarray(np.tile(np.cos(angles) * scale, (1, 4)), F32)
    sine = jnp.asarray(np.tile(np.sin(angles) * scale, (1, 4)), F32)
    lane_head = np.arange(128) // 32
    ones_rot = jnp.asarray(np.tile(lane_head, 2)[:, None] == lane_head[None, :], BF16)
    value_head = np.arange(256) // 64
    ones_val = jnp.asarray(value_head[:, None] == lane_head[None, :], BF16)
    diagonal = jnp.asarray(lane_head[:, None] == value_head[None, :], F32)

    def vm(shape, kind):
        return pltpu.VMEM(shape, kind)

    def lane(block, kind, sums):
        shapes = [(2, 4, 2, 2), (2, 4, 2, 2), (2, 4, 2), (2, 4), (2, 3)]
        if sums:
            shapes = [(2, 4, 2, 2), (2, 4, 2, 2), (4, 2, 2), (2, 4, 2), (4, 2), (2, 4), (4,), (2, 3)]
        return [vm(shape + block, kind) for shape in shapes]

    rows16 = (padded, width)
    scratch = [
        vm((12, 2, 4, 2, 2, 48, 256), BF16),
        vm((6, 2, 4, 2, 2, 16, 768), BF16),
        vm((2, 4, 2, 2, 8, 128), F32),
        vm((12, 24, 256), F32),
        vm(rows16, BF16),
        vm(rows16, BF16),
        vm(rows16, BF16),
        vm(rows16, BF16),
        vm(rows16, BF16),
        vm((padded, 384), BF16),
        vm((padded, 384), BF16),
        vm(rows16, BF16),
        vm(rows16, BF16),
        vm((padded, 128), F32),
        vm(rows16, F32),
        vm(rows16, F32),
        vm((padded, 512), BF16),
        vm((width + 16, padded), BF16),
        vm((8, width), F32),
        vm((8, width), F32),
    ]
    scratch += lane((48, 256), BF16, False) + [vm((2, 2, 24, 256), F32)] * 2
    scratch += lane((48, 256), BF16, False) + lane((8, 128), F32, True)
    scratch += [
        vm((12, 2, 24, 256), F32),
        pltpu.SemaphoreType.DMA((19, 6)),
        pltpu.SemaphoreType.DMA((19, 6)),
        pltpu.SemaphoreType.DMA((2,)),
        pltpu.SemaphoreType.DMA((2,)),
    ]
    scratch += [pltpu.SemaphoreType.DMA((2, 6))] * 6 + [pltpu.SemaphoreType.DMA((12,))] * 2
    scratch += [vm((padded, 128), F32)] * 2 + [vm((3, 256, 256), BF16)]
    scratch += [pltpu.SemaphoreType.DMA((4,))]
    spaces = [pl.ANY, pl.ANY, pltpu.SMEM] + [pltpu.VMEM] * 8 + [pl.ANY] * 2 + [pltpu.VMEM] * 3
    square = jax.ShapeDtypeStruct((share, width), F32)
    kernel = functools.partial(layer_kernel, (tokens_here, padded, length, mols))
    outs = pl.pallas_call(
        kernel,
        out_shape=[
            jax.ShapeDtypeStruct(tokens.shape, BF16),
            jax.ShapeDtypeStruct(tokens.shape, BF16),
            square,
            square,
            square,
            square,
            jax.ShapeDtypeStruct(up_weight.shape, F32),
            jax.ShapeDtypeStruct(down_weight.shape, F32),
            jax.ShapeDtypeStruct((8, 128), F32),
        ],
        in_specs=[pl.BlockSpec(memory_space=s) for s in spaces],
        out_specs=[pl.BlockSpec(memory_space=s) for s in [pl.ANY] * 2 + [pltpu.VMEM] * 7],
        scratch_shapes=scratch,
        compiler_params=pltpu.CompilerParams(
            collective_id=0, has_side_effects=True, vmem_limit_bytes=VMEM_BYTES
        ),
        name="encoder_layer",
    )(
        tokens,
        out_cotangent,
        lengths,
        params,
        key_weight,
        value_weight,
        query_weight,
        out_weight,
        up_weight,
        down_weight,
        feature_directions.reshape(-1, feature_directions.shape[2]),
        cosine,
        sine,
        ones_rot,
        ones_val,
        diagonal,
    )
    output, input_grad, keys, values, queries, mixes, ups, downs, vector_grad = outs
    vectors = [vector_grad[row, :share] for row in range(4)]
    return (
        output,
        input_grad,
        vectors[0],
        vectors[1],
        queries,
        keys,
        values,
        mixes,
        vectors[2],
        vectors[3],
        ups,
        downs,
    )


LAGS = (0, 1, 2, 4)
VMEM_BYTES = 64 * 1024 * 1024


def solution(mesh):
    placed = (
        P("fsdp", None),
        P("fsdp"),
        P(),
        P("fsdp"),
        P("fsdp"),
        P("fsdp", None),
        P("fsdp", None),
        P("fsdp", None),
        P("fsdp", None),
        P("fsdp"),
        P("fsdp"),
        P("fsdp", None),
        P("fsdp", None),
        P("fsdp", None),
    )
    fused = mesh.shape["fsdp"] == 32
    return jax.shard_map(
        fused_device if fused else per_device,
        mesh=mesh,
        in_specs=placed,
        out_specs=(
            P("fsdp", None),
            P("fsdp", None),
            P("fsdp"),
            P("fsdp"),
            P("fsdp", None),
            P("fsdp", None),
            P("fsdp", None),
            P("fsdp", None),
            P("fsdp"),
            P("fsdp"),
            P("fsdp", None),
            P("fsdp", None),
        ),
        check_vma=False,
    )
```

```python
import functools

import jax
import jax.numpy as jnp
import numpy as np
from jax import lax
from jax.experimental import pallas as pl
from jax.experimental.pallas import tpu as pltpu
from jax.sharding import PartitionSpec as P

F32 = jnp.float32
BF16 = jnp.bfloat16


def rotate_scale(vectors):
    half_size = vectors.shape[-1] // 2
    positions = jnp.arange(vectors.shape[1], dtype=jnp.float32)
    frequency = 10000.0 ** (-jnp.arange(half_size, dtype=jnp.float32) * 2.0 / vectors.shape[-1])
    angles = positions[:, None] * frequency[None, :]
    cosine_table = jnp.cos(angles)[None, :, None, :]
    sine_table = jnp.sin(angles)[None, :, None, :]
    first_half = vectors[..., :half_size]
    second_half = vectors[..., half_size:]
    turned = jnp.concatenate(
        [
            first_half * cosine_table - second_half * sine_table,
            first_half * sine_table + second_half * cosine_table,
        ],
        -1,
    )
    return turned * vectors.shape[-1] ** (-0.25)


def feature_map(vectors, directions):
    turned = rotate_scale(vectors)
    logits = jnp.einsum("slhd,hdm->slhm", turned, directions, precision=lax.Precision.HIGHEST)
    logits = logits - 0.5 * jnp.sum(turned * turned, -1, keepdims=True)
    return jnp.exp(logits) * directions.shape[-1] ** (-0.5)


def smooth_gelu(values):
    return jax.nn.gelu(values, approximate=True)


def norm_parts(inputs, gain_row, shift_row):
    row_mean = jnp.mean(inputs, -1, keepdims=True)
    centered = inputs - row_mean
    inverse = lax.rsqrt(jnp.mean(centered * centered, -1, keepdims=True) + 1e-05)
    hat_rows = centered * inverse
    return (
        hat_rows * gain_row.astype(jnp.float32) + shift_row.astype(jnp.float32),
        hat_rows,
        inverse,
    )


def norm_back(grad_rows, hat_rows, inverse, gain_row):
    scaled = grad_rows * gain_row.astype(jnp.float32)
    return inverse * (
        scaled
        - jnp.mean(scaled, -1, keepdims=True)
        - hat_rows * jnp.mean(scaled * hat_rows, -1, keepdims=True)
    )


def per_device(
    tokens,
    lengths,
    feature_directions,
    first_gain,
    first_shift,
    query_weight,
    key_weight,
    value_weight,
    out_weight,
    second_gain,
    second_shift,
    up_weight,
    down_weight,
    out_cotangent,
):
    model_width = tokens.shape[1]
    head_count = feature_directions.shape[0]
    head_size = model_width // head_count
    seqs_here = lengths.shape[0]
    length = tokens.shape[0] // seqs_here
    inputs = tokens.astype(jnp.float32)

    def feature_of(row_block):
        return feature_map(
            row_block.reshape(seqs_here, length, head_count, head_size), feature_directions
        )

    gain_one, shift_one, query_full, key_full, value_full, out_full = (
        lax.all_gather(first_gain, "fsdp", axis=0, tiled=True),
        lax.all_gather(first_shift, "fsdp", axis=0, tiled=True),
        lax.all_gather(query_weight, "fsdp", axis=0, tiled=True),
        lax.all_gather(key_weight, "fsdp", axis=0, tiled=True),
        lax.all_gather(value_weight, "fsdp", axis=0, tiled=True),
        lax.all_gather(out_weight, "fsdp", axis=0, tiled=True),
    )
    normed_wide, hat_one, inverse_one = norm_parts(inputs, gain_one, shift_one)
    normed = normed_wide.astype(jnp.bfloat16)
    query_rows = jnp.dot(normed, query_full, preferred_element_type=jnp.float32)
    key_rows = jnp.dot(normed, key_full, preferred_element_type=jnp.float32)
    value_rows = jnp.dot(normed, value_full, preferred_element_type=jnp.float32)
    value_low = value_rows.astype(jnp.bfloat16).reshape(seqs_here, length, head_count, head_size)
    query_raw, query_back = jax.vjp(feature_of, query_rows)
    key_raw, key_back = jax.vjp(feature_of, key_rows)
    query_low = query_raw.astype(jnp.bfloat16)
    key_low = key_raw.astype(jnp.bfloat16)
    positions = jnp.arange(length, dtype=jnp.int32)
    key_live = positions[None, :] < lengths[:, None]
    masked = key_low * key_live.astype(jnp.bfloat16)[:, :, None, None]
    state_sum = jnp.einsum("slhm,slhd->shmd", masked, value_low, preferred_element_type=jnp.float32)
    state_low = state_sum.astype(jnp.bfloat16)
    totals = jnp.sum(masked.astype(jnp.float32), 1)
    numerator = jnp.einsum(
        "slhm,shmd->slhd", query_low, state_low, preferred_element_type=jnp.float32
    )
    query_wide = query_low.astype(jnp.float32)
    denominator = jnp.einsum("slhm,shm->slh", query_wide, totals, precision=lax.Precision.HIGHEST)
    mixed_rows = (numerator / denominator[..., None]).reshape(-1, model_width).astype(jnp.bfloat16)
    branch = jnp.dot(mixed_rows, out_full, preferred_element_type=jnp.float32)
    middle = inputs + branch
    gain_two, shift_two, up_full, down_full = (
        lax.all_gather(second_gain, "fsdp", axis=0, tiled=True),
        lax.all_gather(second_shift, "fsdp", axis=0, tiled=True),
        lax.all_gather(up_weight, "fsdp", axis=0, tiled=True),
        lax.all_gather(down_weight, "fsdp", axis=0, tiled=True),
    )
    second_wide, hat_two, inverse_two = norm_parts(middle, gain_two, shift_two)
    second = second_wide.astype(jnp.bfloat16)
    up_rows = jnp.dot(second, up_full, preferred_element_type=jnp.float32)
    gelu_rows, gelu_back = jax.vjp(smooth_gelu, up_rows)
    hidden = gelu_rows.astype(jnp.bfloat16)
    output = (middle + jnp.dot(hidden, down_full, preferred_element_type=jnp.float32)).astype(
        jnp.bfloat16
    )
    gain_two, shift_two, up_full, down_full = (
        lax.all_gather(second_gain, "fsdp", axis=0, tiled=True),
        lax.all_gather(second_shift, "fsdp", axis=0, tiled=True),
        lax.all_gather(up_weight, "fsdp", axis=0, tiled=True),
        lax.all_gather(down_weight, "fsdp", axis=0, tiled=True),
    )
    gain_one, shift_one, query_full, key_full, value_full, out_full = (
        lax.all_gather(first_gain, "fsdp", axis=0, tiled=True),
        lax.all_gather(first_shift, "fsdp", axis=0, tiled=True),
        lax.all_gather(query_weight, "fsdp", axis=0, tiled=True),
        lax.all_gather(key_weight, "fsdp", axis=0, tiled=True),
        lax.all_gather(value_weight, "fsdp", axis=0, tiled=True),
        lax.all_gather(out_weight, "fsdp", axis=0, tiled=True),
    )
    down_grad = jnp.einsum("tf,td->fd", hidden, out_cotangent, preferred_element_type=jnp.float32)
    hidden_grad = jnp.einsum(
        "td,fd->tf", out_cotangent, down_full, preferred_element_type=jnp.float32
    )
    pre_grad = gelu_back(hidden_grad)[0].astype(jnp.bfloat16)
    up_grad = jnp.einsum("td,tf->df", second, pre_grad, preferred_element_type=jnp.float32)
    second_grad = jnp.einsum("tf,df->td", pre_grad, up_full, preferred_element_type=jnp.float32)
    gain_two_grad = jnp.sum(second_grad * hat_two, 0)
    shift_two_grad = jnp.sum(second_grad, 0)
    middle_grad = out_cotangent.astype(jnp.float32) + norm_back(
        second_grad, hat_two, inverse_two, gain_two
    )
    ffn_shards = (
        lax.psum_scatter(gain_two_grad, "fsdp", scatter_dimension=0, tiled=True),
        lax.psum_scatter(shift_two_grad, "fsdp", scatter_dimension=0, tiled=True),
        lax.psum_scatter(up_grad, "fsdp", scatter_dimension=0, tiled=True),
        lax.psum_scatter(down_grad, "fsdp", scatter_dimension=0, tiled=True),
    )
    branch_grad = middle_grad.astype(jnp.bfloat16)
    out_grad = jnp.einsum("td,te->de", mixed_rows, branch_grad, preferred_element_type=jnp.float32)
    mixed_grad = jnp.einsum("te,de->td", branch_grad, out_full, preferred_element_type=jnp.float32)
    mixed_grad = mixed_grad.reshape(seqs_here, length, head_count, head_size)
    numer_grad = (mixed_grad / denominator[..., None]).astype(jnp.bfloat16)
    denom_grad = -jnp.sum(mixed_grad * numerator, -1) / (denominator * denominator)
    query_feat_grad = jnp.einsum(
        "slhd,shmd->slhm", numer_grad, state_low, preferred_element_type=jnp.float32
    )
    query_feat_grad = query_feat_grad + denom_grad[..., None] * totals[:, None]
    state_grad = jnp.einsum(
        "slhm,slhd->shmd", query_low, numer_grad, preferred_element_type=jnp.float32
    ).astype(jnp.bfloat16)
    totals_grad = jnp.einsum(
        "slh,slhm->shm", denom_grad, query_wide, precision=lax.Precision.HIGHEST
    )
    key_feat_grad = jnp.einsum(
        "slhd,shmd->slhm", value_low, state_grad, preferred_element_type=jnp.float32
    )
    key_feat_grad = (key_feat_grad + totals_grad[:, None]) * key_live.astype(jnp.float32)[
        :, :, None, None
    ]
    value_grad = jnp.einsum(
        "slhm,shmd->slhd", masked, state_grad, preferred_element_type=jnp.float32
    )
    value_grad = value_grad.reshape(-1, model_width).astype(jnp.bfloat16)
    query_grad = query_back(query_feat_grad)[0].astype(jnp.bfloat16)
    key_grad = key_back(key_feat_grad)[0].astype(jnp.bfloat16)
    normed_grad = jnp.einsum(
        "te,de->td", query_grad, query_full, preferred_element_type=jnp.float32
    )
    normed_grad = normed_grad + jnp.einsum(
        "te,de->td", key_grad, key_full, preferred_element_type=jnp.float32
    )
    normed_grad = normed_grad + jnp.einsum(
        "te,de->td", value_grad, value_full, preferred_element_type=jnp.float32
    )
    query_weight_grad = jnp.einsum(
        "td,te->de", normed, query_grad, preferred_element_type=jnp.float32
    )
    key_weight_grad = jnp.einsum("td,te->de", normed, key_grad, preferred_element_type=jnp.float32)
    value_weight_grad = jnp.einsum(
        "td,te->de", normed, value_grad, preferred_element_type=jnp.float32
    )
    gain_one_grad = jnp.sum(normed_grad * hat_one, 0)
    shift_one_grad = jnp.sum(normed_grad, 0)
    input_grad = middle_grad + norm_back(normed_grad, hat_one, inverse_one, gain_one)
    attn_shards = (
        lax.psum_scatter(gain_one_grad, "fsdp", scatter_dimension=0, tiled=True),
        lax.psum_scatter(shift_one_grad, "fsdp", scatter_dimension=0, tiled=True),
        lax.psum_scatter(query_weight_grad, "fsdp", scatter_dimension=0, tiled=True),
        lax.psum_scatter(key_weight_grad, "fsdp", scatter_dimension=0, tiled=True),
        lax.psum_scatter(value_weight_grad, "fsdp", scatter_dimension=0, tiled=True),
        lax.psum_scatter(out_grad, "fsdp", scatter_dimension=0, tiled=True),
    )
    shards = tuple(attn_shards) + tuple(ffn_shards)
    return (output, input_grad.astype(jnp.bfloat16)) + shards


def dot_nn(a, b):
    return lax.dot_general(a, b, (((1,), (0,)), ((), ())), preferred_element_type=F32)


def dot_nt(a, b):
    return lax.dot_general(a, b, (((1,), (1,)), ((), ())), preferred_element_type=F32)


def dot_tn(a, b):
    return lax.dot_general(a, b, (((0,), (0,)), ((), ())), preferred_element_type=F32)


def split_low(v):
    high = v.astype(BF16)
    return high, (v - high.astype(F32)).astype(BF16)


def remote(src, dst, send, recv, device):
    return pltpu.make_async_remote_copy(
        src_ref=src,
        dst_ref=dst,
        send_sem=send,
        recv_sem=recv,
        device_id=(device,),
        device_id_type=pl.DeviceIdType.MESH,
    )


class Place:
    def __init__(self):
        me = lax.axis_index("fsdp")
        self.c = lax.rem(me, 2)
        self.x = lax.rem(lax.div(me, 2), 2)
        self.y = lax.rem(lax.div(me, 4), 2)
        self.z = lax.div(me, 8)
        self.sib = me + 1 - 2 * self.c
        self.px = me + 2 - 4 * self.x
        self.py = me + 4 - 8 * self.y
        self.zs = [lax.rem(self.z + d, 4) for d in (1, 2, 3)]
        self.pz = [me + (zp - self.z) * 8 for zp in self.zs]

    def greet(self):
        barrier = pltpu.get_barrier_semaphore()
        for peer in [self.sib, self.px, self.py] + self.pz:
            pl.semaphore_signal(
                barrier, inc=1, device_id=(peer,), device_id_type=pl.DeviceIdType.MESH
            )

    def enter(self):
        pl.semaphore_wait(pltpu.get_barrier_semaphore(), 6)


class Gather:
    def __init__(self, at, buf, send, recv, y_first):
        self.buf, self.send, self.recv = buf, send, recv
        c, z, y, x = at.c, at.z, at.y, at.x
        mine = buf.at[c, z, y, x]
        line = buf.at[c, :, y, x]
        plane = buf.at[c, :, :, x] if y_first else buf.at[c, :, y]
        first, second = (at.py, at.px) if y_first else (at.px, at.py)
        self.copies = [
            [remote(mine, mine, send.at[d], recv.at[d], at.pz[d]) for d in range(3)],
            [remote(line, line, send.at[3], recv.at[3], first)],
            [remote(plane, plane, send.at[4], recv.at[4], second)],
            [remote(buf.at[c], buf.at[c], send.at[5], recv.at[5], at.sib)],
        ]

    def start(self, phase):
        for copy in self.copies[phase]:
            copy.start()

    def arrived(self, phase):
        for copy in self.copies[phase]:
            copy.wait_recv()

    def sent(self):
        for phase in self.copies:
            for copy in phase:
                copy.wait_send()


class Reduce:
    def __init__(self, at, refs, send, recv, y_first):
        self.at, self.y_first = at, y_first
        self.R, self.B1, self.S, self.B2, self.S2, self.B3, self.S3, self.B4 = refs
        self.send, self.recv = send, recv

    def copies(self, phase, par):
        at, s, r = self.at, self.send.at[par], self.recv.at[par]
        first, second = (at.py, at.px) if self.y_first else (at.px, at.py)
        if phase == 0:
            return [remote(self.R.at[1 - at.c], self.B1.at[par], s.at[0], r.at[0], at.sib)]
        if phase == 1:
            src = self.S.at[:, 1 - at.y] if self.y_first else self.S.at[:, :, 1 - at.x]
            return [remote(src, self.B2.at[par], s.at[1], r.at[1], first)]
        if phase == 2:
            src = self.S2.at[:, 1 - (at.x if self.y_first else at.y)]
            return [remote(src, self.B3.at[par], s.at[2], r.at[2], second)]
        return [
            remote(self.S3.at[at.zs[d]], self.B4.at[par, d], s.at[3 + d], r.at[3 + d], at.pz[d])
            for d in range(3)
        ]

    def start(self, phase, par):
        for copy in self.copies(phase, par):
            copy.start()

    def wait_sent(self, phase, par):
        for copy in self.copies(phase, par):
            copy.wait_send()

    def step(self, phase, par, before=True):
        at = self.at
        for copy in self.copies(phase - 1, par):
            copy.wait_recv()
        if phase == 4:
            total = self.S3[at.z].astype(F32)
            for d in range(3):
                total = total + self.B4[par, d].astype(F32)
            return total
        if before is True:
            self.wait_sent(phase, 1 - par)
        elif before is not False:

            @pl.when(before)
            def _():
                self.wait_sent(phase, 1 - par)

        kind = self.S.dtype

        def add(i, _):
            if phase == 1:
                own, other, out = self.R[at.c, i], self.B1[par, i], self.S
            elif phase == 2:
                own = self.S[i, at.y] if self.y_first else self.S[i, :, at.x]
                other, out = self.B2[par, i], self.S2
            else:
                own = self.S2[i, at.x if self.y_first else at.y]
                other, out = self.B3[par, i], self.S3
            out[i] = (own.astype(F32) + other.astype(F32)).astype(kind)
            return 0

        lax.fori_loop(0, 4, add, 0)
        self.start(phase, par)
        return None


def layer_kernel(
    sizes,
    x_hbm,
    dy_hbm,
    lengths,
    params_here,
    key_here,
    value_here,
    query_here,
    mix_here,
    up_here,
    down_here,
    directions,
    cosine_hbm,
    sine_hbm,
    ones_rot,
    ones_val,
    diagonal,
    out_hbm,
    dx_hbm,
    wide_out,
    up_out,
    down_out,
    params_out,
    wu,
    wd,
    pb,
    px32,
    xb,
    normed,
    rotq,
    rotk,
    vv,
    pq,
    pk,
    mixed,
    second,
    inv2,
    acc,
    dsec,
    dpre,
    tb,
    prm,
    lng,
    ru,
    b1u,
    b2u,
    b3u,
    b4u,
    flu,
    fld,
    rd,
    b1d,
    b2d,
    b3d,
    b4d,
    rp,
    b1p,
    sp,
    b2p,
    s2p,
    b3p,
    s3p,
    b4p,
    res_u,
    ag_send,
    ag_recv,
    pre_send,
    pre_recv,
    us,
    ur,
    ds_,
    dr,
    ps,
    pr,
    qs,
    qr,
    cosine,
    sine,
    feats,
    local,
):
    tokens_here, padded, length, mols = sizes
    spare = padded - tokens_here
    at = Place()
    at.greet()
    hid = mixed
    load_x = pltpu.make_async_copy(x_hbm, xb.at[pl.ds(0, tokens_here)], local.at[0])
    def load_dy(k):
        r = pl.ds(832 * k, 832 if k == 0 else tokens_here - 832)
        return pltpu.make_async_copy(dy_hbm.at[r], xb.at[r], local.at[4 + k])

    load_x.start()
    load_cos = pltpu.make_async_copy(cosine_hbm, cosine, local.at[2])
    load_sin = pltpu.make_async_copy(sine_hbm, sine, local.at[3])
    load_cos.start()
    load_sin.start()

    def halves_pick():
        t = lax.broadcasted_iota(jnp.int32, (1, 256), 1)
        source = ((t & 127) >> 5) * 64 + (t >> 7) * 32 + (t & 31)
        row = lax.broadcasted_iota(jnp.int32, (256, 256), 0)
        return jnp.where(row == source, 1.0, 0.0).astype(BF16)

    picks = [hid.at[0:768, 0:256], hid.at[0:768, 256:512], dpre.at[0:768, 0:256]]

    def hidden_pick():
        for b in range(3):
            t = lax.broadcasted_iota(jnp.int32, (1, 256), 1) + 256 * b
            owner = 2 * ((t & 63) >> 4) + ((t & 127) >> 6)
            source = 96 * owner + 16 * (t >> 7) + (t & 15)

            def fill(i, _):
                row = lax.broadcasted_iota(jnp.int32, (128, 256), 0) + 128 * i
                r = pl.ds(pl.multiple_of(128 * i, 128), 128)
                picks[b][r, :] = jnp.where(row == source, 1.0, 0.0).astype(BF16)
                return 0

            lax.fori_loop(0, 6, fill, 0)

    halves = halves_pick()
    for g in range(3):
        col = slice(256 * g, 256 * g + 256)
        for base, ref in ((0, key_here), (6, query_here)):
            res_u[(base + g) // 2, (base + g) % 2] = dot_nn(ref[:, col], halves)
        for base, ref in ((3, value_here), (9, mix_here)):
            res_u[(base + g) // 2, (base + g) % 2] = ref[:, col].astype(F32)
    pb[at.c, at.z, at.y, at.x] = params_here[...]
    for ch in range(6):
        wd[ch, at.c, at.z, at.y, at.x] = down_here[16 * ch : 16 * ch + 16, :]
    at.enter()

    def swap_of(k):
        half = pl.ds(6 * k, 6)
        src = res_u.at[half, 1 - at.c]
        return remote(src, px32.at[half], pre_send.at[k], pre_recv.at[k], at.sib)

    swaps = [swap_of(k) for k in range(2)]
    swaps[0].start()
    up32 = up_here[...].astype(F32)
    stacked = jnp.concatenate([up32[:, 768 * i : 768 * i + 768] for i in range(4)], 0)
    hidden_pick()
    stacked = stacked.astype(BF16)
    order = jnp.concatenate([dot_nn(stacked, pick[...]) for pick in picks], 1)
    for ch in range(6):
        for h in range(2):
            at_col = 128 * ch + 64 * h
            res_u[6 + ch, h] = jnp.concatenate(
                [order[24 * i : 24 * i + 24, at_col : at_col + 64] for i in range(4)], 1
            )
    swaps[1].start()
    swaps[0].wait()
    even = at.c == 0

    def build(u, _):
        mine = res_u[u, at.c]
        other = px32[u]
        top = jnp.where(even, mine, other)
        low = jnp.where(even, other, mine)
        wu[u, at.c, at.z, at.y, at.x] = jnp.concatenate([top, low], 0).astype(BF16)
        return 0

    lax.fori_loop(0, 6, build, 0)
    tail = pl.ds(tokens_here, spare)
    xb[tail, :] = jnp.zeros((spare, xb.shape[1]), BF16)
    mixed[tail, :] = jnp.zeros((spare, xb.shape[1]), BF16)
    lng[...] = jnp.zeros(lng.shape, F32)
    tb[768:784, :] = jnp.ones((16, padded), BF16)

    def gather_unit(u):
        if u < 6:
            buf = wu.at[u]
        else:
            buf = wu.at[6 + (u - 6) // 2] if u % 2 == 0 else wd.at[(u - 6) // 2]
        return Gather(at, buf, ag_send.at[u], ag_recv.at[u], u % 2 == 0)

    units = [gather_unit(u) for u in range(18)]
    params = Gather(at, pb, ag_send.at[18], ag_recv.at[18], True)
    state = {"tick": 0, "needed": set()}
    lags, last = LAGS, tuple(min(17, v + 2 * AHEAD) for v in (13, 11, 9, 7))

    def tick(count=1):
        for _ in range(count):
            t = state["tick"]
            state["tick"] += 1
            if t == 0:
                params.start(0)
            for k in range(4):
                u = t - lags[k]
                if 0 <= u <= last[k]:
                    if k:
                        if u == 0:
                            params.arrived(k - 1)
                            params.start(k)
                        units[u].arrived(k - 1)
                    units[u].start(k)

    def need(u):
        while state["tick"] <= u + lags[3]:
            tick()
        if u not in state["needed"]:
            state["needed"].add(u)
            units[u].arrived(3)

    tick(1)
    swaps[1].wait()
    lax.fori_loop(6, 12, build, 0)
    tick(1)
    for g in range(3):
        for half in range(2):
            lines = []
            for hh in range(4):
                piece = directions[4 * g + hh, :, 32 * half : 32 * half + 32].T
                gap = jnp.zeros((32, 32), F32)
                lines.append(jnp.concatenate([gap] * hh + [piece] + [gap] * (3 - hh), 1))
            high, low = split_low(jnp.concatenate(lines, 0))
            feats[g, 128 * half : 128 * half + 128, :] = jnp.concatenate([high, low], 1)

    def run(start, stop, body):
        if stop - start <= 4:
            for i in range(start, stop):
                body(i, 0)
        else:
            lax.fori_loop(start, stop, body, 0)

    def rows(i, count):
        return pl.ds(pl.multiple_of(i * count, 16), count)

    def norm(v):
        centered = v - jnp.mean(v, -1, keepdims=True)
        inverse = lax.rsqrt(jnp.mean(centered * centered, -1, keepdims=True) + 1e-05)
        return centered * inverse, inverse

    load_x.wait()
    load_cos.wait()
    load_sin.wait()

    def first_hat(i, _):
        r = rows(i, 208)
        acc[r, :] = norm(xb[r, :].astype(F32))[0]
        return 0

    lax.fori_loop(0, padded // 208, first_hat, 0)
    tick(lags[3] - 1)
    params.arrived(3)
    parts = [jnp.zeros((8, 128), F32) for _ in range(7)]
    for i in range(32):
        block = pb[i % 2, i // 8, (i // 4) % 2, (i // 2) % 2]
        k, shift = (24 * i) // 128, (24 * i) % 128
        pair = jnp.concatenate([block, jnp.zeros((8, 128), F32)], 1)
        if shift:
            pair = pltpu.roll(pair, shift, 1)
        parts[k] = parts[k] + pair[:, :128]
        parts[k + 1] = parts[k + 1] + pair[:, 128:]
    prm[...] = jnp.concatenate(parts[:6], 1)

    def first_norm(i, _):
        r = rows(i, 208)
        normed[r, :] = (acc[r, :] * prm[0:1, :] + prm[1:2, :]).astype(BF16)
        return 0

    lax.fori_loop(0, padded // 208, first_norm, 0)

    def block(b):
        return wu[b // 2, b % 2].reshape(768, 256)

    def blocks(base):
        return jnp.concatenate([block(base + g) for g in range(3)], 1)

    def features(base, rot_ref, feat_ref, groups):
        def body(i, _):
            r = rows(i, TILE_F)
            ct, st = cosine[r, :], sine[r, :]
            wide = jnp.concatenate([block(base + g) for g in groups], 1)
            us = dot_nn(normed[r, :], wide)
            for g in groups:
                u = us[:, 256 * (g - groups[0]) : 256 * (g - groups[0]) + 256]
                a, b = u[:, :128], u[:, 128:]
                rot = jnp.concatenate([a * ct - b * st, a * st + b * ct], 1)
                high, low = split_low(rot)
                sq_high, sq_low = split_low(rot * rot)
                two = dot_nn(high, feats[g])
                logits = two[:, :128] + two[:, 128:] + dot_nn(low, feats[g, :, :128])
                norms = dot_nn(sq_high, ones_rot[...]) + dot_nn(sq_low, ones_rot[...])
                p = jnp.exp(logits - 0.5 * norms) * (32**-0.5)
                rot_ref[r, 256 * g : 256 * g + 256] = high
                feat_ref[r, 128 * g : 128 * g + 128] = p.astype(BF16)
            return 0

        lax.fori_loop(0, padded // TILE_F, body, 0)

    def values(groups):
        def body(i, _):
            r = rows(i, 832)
            for g in groups:
                vv[r, 256 * g : 256 * g + 256] = dot_nn(normed[r, :], block(3 + g)).astype(BF16)
            return 0

        run(0, padded // 832, body)

    need(0)
    features(0, rotk, pk, (0, 1))
    tick()
    need(1)
    features(0, rotk, pk, (2,))
    values((0,))
    tick()
    need(2)
    values((1, 2))
    tick()
    need(3)
    features(6, rotq, pq, (0, 1))
    tick()
    need(4)
    features(6, rotq, pq, (2,))
    tick()
    here = pl.ds(0, tokens_here)
    spill = pltpu.make_async_copy(normed.at[here], dx_hbm, local.at[1])
    spill.start()
    hat2 = normed

    window = 224

    def places(s):
        begin = lax.div(s * length, 16) * 16
        pos = lax.broadcasted_iota(jnp.int32, (window, 1), 0) - (s * length - begin)
        valid = (pos >= 0) & (pos < length)
        live = valid & (pos < lengths[s])
        return pl.ds(pl.multiple_of(begin, 16), window), pos, valid, live

    def state_of(g, w, live, pkm):
        ones = jnp.ones((window, 256), BF16)
        diag = diagonal[...]
        st = (dot_tn(pkm, vv[w, 256 * g : 256 * g + 256]) * diag).astype(BF16)
        tot = dot_tn(pkm, ones) * diag
        tot_high, tot_low = split_low(tot)
        return st, tot_high, tot_low

    def masked_keys(g, w, live):
        keys = pk[w, 128 * g : 128 * g + 128].astype(F32)
        return jnp.where(live, keys, 0.0)

    def attend(s, _):
        w, pos, valid, live = places(s)
        mixes = []
        for g in range(3):
            pkm = masked_keys(g, w, live).astype(BF16)
            st, tot_high, tot_low = state_of(g, w, live, pkm)
            pqg = pq[w, 128 * g : 128 * g + 128]
            num = dot_nn(pqg, st)
            den = dot_nn(pqg, tot_high) + dot_nn(pqg, tot_low)
            mixes.append(jnp.where(valid, num / den, 0.0))
        mix = jnp.where(pos < 0, mixed[w, :].astype(F32), jnp.concatenate(mixes, 1))
        mixed[w, :] = mix.astype(BF16)
        return 0

    for k in range(4):
        lax.fori_loop(2 * k, 2 * k + 2, attend, 0, unroll=2)
        tick()
    need(5)
    spill.wait()

    spill_mixed = pltpu.make_async_copy(mixed.at[here], out_hbm, local.at[2])
    spill_mixed.start()

    def project(i, _):
        r = rows(i, TILE_P)
        branch = dot_nn(mixed[r, :], blocks(9))
        middle = xb[r, :].astype(F32) + branch
        acc[r, :] = middle
        hat, inverse = norm(middle)
        hat2[r, :] = hat.astype(BF16)
        inv2[r, :] = jnp.broadcast_to(inverse, (TILE_P, 128))
        second[r, :] = (hat * prm[2:3, :] + prm[3:4, :]).astype(BF16)
        dsec[r, :] = jnp.zeros((TILE_P, 768), F32)
        return 0

    half = padded // TILE_P // 2
    lax.fori_loop(0, half, project, 0)
    load_dy(0).start()
    tick()
    lax.fori_loop(half, 2 * half, project, 0)

    def turn(src):
        for j in range(6):
            tb[128 * j : 128 * j + 128, :] = src[:, 128 * j : 128 * j + 128].T

    load_dy(1).start()
    turn(second)
    load_dy(0).wait()
    load_dy(1).wait()
    spill_mixed.wait()
    while state["tick"] <= last[0] + lags[0]:
        tick()
    need(6)
    need(7)

    def pair_of(q):
        up, down = 6 + 2 * q, 7 + 2 * q
        return (
            Gather(at, wu.at[6 + q], ag_send.at[up], ag_recv.at[up], True),
            Gather(at, wd.at[q], ag_send.at[down], ag_recv.at[down], False),
        )

    def gather_on(q, phase):
        @pl.when(q < 6)
        def _():
            for unit in pair_of(q):
                if phase:
                    unit.arrived(phase - 1)
                unit.start(phase)

    su, sd = wu.at[6, 0], wu.at[6, 1]
    s2u, s2d = wu.at[7, 0, :, 0], wu.at[7, 0, :, 1]
    s3u, s3d = wu.at[7, 1, :, 0, 0], wu.at[7, 1, :, 0, 1]
    lane_u = Reduce(at, (ru, b1u, su, b2u, s2u, b3u, s3u, b4u), us, ur, True)
    lane_d = Reduce(at, (rd, b1d, sd, b2d, s2d, b3d, s3d, b4d), ds_, dr, False)

    def post(flat, par, unit):
        return remote(
            flat.at[par, 1 - at.c], res_u.at[unit, at.c], qs.at[unit], qr.at[unit], at.sib
        )

    def emit_pair(flat, total, par, unit):
        flat[par] = total.reshape(flat.shape[1:])
        res_u[unit, at.c] = flat[par, at.c]
        post(flat, par, unit).start()

    def emit_own(total, unit):
        for b in range(3):
            r = pl.ds(pl.multiple_of(16 * unit, 16), 16)
            down_out[r, 256 * b : 256 * b + 256] = total[16 * b : 16 * b + 16]

    def keep(lane, half, grad):
        lane.R[half] = grad.astype(BF16).reshape(4, 2, 2, 48, 256)

    slope = 0.7978845608028654
    bend = 0.044715

    def up_block(ch):
        return jnp.concatenate([wu[6 + ch, h].reshape(768, 256) for h in range(2)], 1)

    def chunk(ch, _):
        def inner(i, _):
            r = rows(i, 416)
            lines, cot = second[r, :], xb[r, :]
            pres = dot_nn(lines, up_block(ch))
            dhs = dot_nt(cot, wd[ch].reshape(512, 768))
            for h in range(2):
                pre = pres[:, 256 * h : 256 * h + 256]
                dh = dhs[:, 256 * h : 256 * h + 256]
                square = pre * pre
                t = jnp.tanh(pre * (slope + slope * bend * square))
                half = 0.5 + 0.5 * t
                col = slice(256 * h, 256 * h + 256)
                hid[r, col] = (pre * half).astype(BF16)
                bent = slope + 3.0 * slope * bend * square
                grad = half + 0.5 * pre * (1.0 - t * t) * bent
                dpre[r, col] = (dh * grad).astype(BF16)
            return 0

        @pl.when(ch >= 1)
        def _():
            for unit in pair_of(ch):
                unit.arrived(3)

        run(0, 4, inner)
        for phase in (3, 2, 1, 0):
            gather_on(ch + 4 + AHEAD - phase, phase)
        par = lax.rem(ch, 2)
        for k in (1, 2):

            @pl.when(ch == k)
            def _():
                units[4 + 2 * k].sent()

        for phase in (4, 3, 2, 1):
            j = ch - phase

            @pl.when(j >= 0)
            def _():
                old = lax.rem(j + 8, 2)
                if phase == 4:

                    @pl.when(j >= 2)
                    def _():
                        post(flu, old, j - 2).wait_send()

                up_total = lane_u.step(phase, old, before=j >= 1)
                down_total = lane_d.step(phase, old, before=j >= 1)
                if phase == 4:
                    emit_pair(flu, up_total, old, j)
                    emit_own(down_total, j)

        @pl.when(ch >= 1)
        def _():
            lane_u.wait_sent(0, 1 - par)
            lane_d.wait_sent(0, 1 - par)

        grads = dot_nn(tb[:768, :], dpre[...])
        keep(lane_u, 0, grads[:, :256])
        keep(lane_u, 1, grads[:, 256:])
        grads = dot_tn(hid[:, 0:512], xb[...]).astype(BF16)
        for h in range(2):
            for b in range(3):
                part = grads[256 * h : 256 * h + 256, 256 * b : 256 * b + 256]
                rd[h, :, :, :, 16 * b : 16 * b + 16, :] = part.reshape(4, 2, 2, 16, 256)
        lane_u.start(0, par)
        lane_d.start(0, par)

        def outer(i, _):
            r = rows(i, 832)
            acc[r, :] += dot_nn(hid[r, 0:512], wd[ch].reshape(512, 768))
            dsec[r, :] += dot_nt(dpre[r, :], up_block(ch))
            return 0

        run(0, 2, outer)
        return 0

    lax.fori_loop(0, 6, chunk, 0)
    fetch_mixed = pltpu.make_async_copy(out_hbm, mixed.at[here], local.at[2])
    fetch_mixed.start()

    def drain(lane, phase, j):
        par = j % 2
        pairs = lane is lane_u or j >= 6
        flat = flu if lane is lane_u else fld
        unit = j if lane is lane_u else j + 3
        if phase == 4 and pairs and (lane is lane_u or j >= 8):
            post(flat, par, unit - 2).wait_send()
        total = lane.step(phase, par)
        if phase == 4:
            if pairs:
                emit_pair(flat, total, par, unit)
            else:
                emit_own(total, j)

    def both(*steps):
        for phase, j in steps:
            drain(lane_u, phase, j)
            drain(lane_d, phase, j)

    both((4, 2), (3, 3), (2, 4), (1, 5))

    def second_back(i, _):
        r = rows(i, TILE_S)
        e = dsec[r, :]
        hat = hat2[r, :].astype(F32)
        inverse = inv2[r, :][:, :1]
        lng[2:3, :] += jnp.sum(e * hat, 0, keepdims=True)
        lng[3:4, :] += jnp.sum(e, 0, keepdims=True)
        eg = e * prm[2:3, :]
        m1 = jnp.mean(eg, -1, keepdims=True)
        m2 = jnp.mean(eg * hat, -1, keepdims=True)
        dmid = xb[r, :].astype(F32) + inverse * (eg - m1 - hat * m2)
        dsec[r, :] = dmid
        low = dmid.astype(BF16)
        second[r, :] = low
        hat2[r, :] = acc[r, :].astype(BF16)
        acc[r, :] = dot_nt(low, blocks(9))
        return 0

    half = padded // TILE_S // 2
    lax.fori_loop(0, half, second_back, 0)
    both((4, 3), (3, 4), (2, 5))
    lax.fori_loop(half, 2 * half, second_back, 0)
    store_out = pltpu.make_async_copy(hat2.at[pl.ds(0, tokens_here)], out_hbm, local.at[0])
    fetch_mixed.wait()
    store_out.start()
    load_x = pltpu.make_async_copy(x_hbm, xb.at[pl.ds(0, tokens_here)], local.at[2])
    load_x.start()

    def weight_grad(lane, j, parts):
        lane.wait_sent(0, 1 - j % 2)
        for h, (ref, col, base) in enumerate(parts):

            @pl.when(at.z >= 0)
            def _():
                keep(lane, h, grad_of(ref, col, base))

        lane.start(0, j % 2)

    def grad_of(ref, col, base):
        lines = ref[:, 256 * col : 256 * col + 256]
        if base is None:
            return dot_nn(tb[:768, :], lines)
        both_of = dot_nn(tb[...], lines)
        grad, sums = both_of[:768], both_of[768:769]
        weight = block(base + col).astype(F32)
        share = weight * grad
        gain_col[...] += share[:, :128] + share[:, 128:]
        share = weight * sums
        shift_col[...] += share[:, :128] + share[:, 128:]
        return grad

    gain_col, shift_col = inv2.at[0:768], inv2.at[768:1536]
    inv2[0:1536, :] = jnp.zeros((1536, 128), F32)
    turn(mixed)
    fetch = pltpu.make_async_copy(dx_hbm, mixed.at[here], local.at[1])
    fetch.start()
    both((4, 4), (3, 5))
    weight_grad(lane_u, 6, ((second, 0, None), (second, 1, None)))

    def attend_back(s, _):
        w, pos, valid, live = places(s)
        olds = [acc[w, 128 * j : 128 * j + 128] for j in range(6)]
        vals = [vv[w, 256 * g : 256 * g + 256] for g in range(3)]
        dq_parts, dk_parts, dv_parts = [], [], []
        for g in range(3):
            thin = slice(128 * g, 128 * g + 128)
            diag = diagonal[...]
            pk32 = masked_keys(g, w, live)
            pkm = pk32.astype(BF16)
            st, tot_high, tot_low = state_of(g, w, live, pkm)
            tot = jnp.sum(pk32, 0, keepdims=True)
            pqg = pq[w, thin]
            pq32 = jnp.where(valid, pqg.astype(F32), 0.0)
            num = dot_nn(pqg, st)
            den = dot_nn(pqg, tot_high) + dot_nn(pqg, tot_low)
            share = 1.0 / den
            part = jnp.concatenate([olds[2 * g], olds[2 * g + 1]], 1) * share
            dnum = jnp.where(valid, part, 0.0).astype(BF16)
            e_high, e_low = split_low(jnp.where(valid, -part * (num * share), 0.0))
            dden = dot_nn(e_high, ones_val[...]) + dot_nn(e_low, ones_val[...])
            dpq = dot_nt(dnum, st) + dden * tot
            dst = (dot_tn(pqg, dnum) * diag).astype(BF16)
            dtot = jnp.sum(dden * pq32, 0, keepdims=True)
            dpk = dot_nt(vals[g], dst) + dtot
            dv_parts.append(dot_nn(pkm, dst))
            dq_parts.append(dpq * pq32)
            dk_parts.append(dpk * pk32)
        for j, new in enumerate(dq_parts + dk_parts):
            acc[w, 128 * j : 128 * j + 128] = jnp.where(valid, new, olds[j])
        for g in range(3):
            new = jnp.where(valid, dv_parts[g], vals[g].astype(F32))
            vv[w, 256 * g : 256 * g + 256] = new.astype(BF16)
        return 0

    lax.fori_loop(0, mols // 2, attend_back, 0, unroll=2)
    both((4, 5))
    drain(lane_u, 1, 6)
    lax.fori_loop(mols // 2, mols, attend_back, 0, unroll=2)
    vv[tail, :] = jnp.zeros((spare, 768), BF16)
    drain(lane_u, 2, 6)
    lane_d.wait_sent(0, 1)
    keep(lane_d, 0, grad_of(second, 2, None))
    fetch.wait()
    turn(mixed)
    keep(lane_d, 1, grad_of(vv, 0, 3))
    lane_d.start(0, 0)
    weight_grad(lane_u, 7, ((vv, 1, 3), (vv, 2, 3)))
    drain(lane_u, 3, 6)

    def unpick(lines, pick):
        high, rest = lines.astype(BF16), lines
        parts = [high]
        for _ in range(2):
            rest = rest - parts[-1].astype(F32)
            parts.append(rest.astype(BF16))
        count = lines.shape[0]
        wide = jnp.concatenate([part.astype(F32) for part in parts], 0).astype(BF16)
        out = pick(wide)
        return out[:count] + out[count : 2 * count] + out[2 * count :]

    def features_back(rot_ref, base):
        def body(i, _):
            r = rows(i, TILE_FB)
            ct, sn = cosine[r, :], sine[r, :]
            for g in range(3):
                wide = slice(256 * g, 256 * g + 256)
                high, low = split_low(acc[r, base + 128 * g : base + 128 * g + 128])
                rot = rot_ref[r, wide].astype(F32)
                total = dot_nt(high, ones_rot[...]) + dot_nt(low, ones_rot[...])
                back = dot_nt(jnp.concatenate([high, high], 1), feats[g])
                back = back + dot_nt(low, feats[g, :, :128]) - rot * total
                a, b = back[:, :128], back[:, 128:]
                turned = jnp.concatenate([a * ct + b * sn, b * ct - a * sn], 1)
                rot_ref[r, wide] = turned.astype(BF16)
            return 0

        lax.fori_loop(0, padded // TILE_FB, body, 0)

    features_back(rotk, 384)
    drain(lane_d, 1, 6)
    drain(lane_u, 4, 6)
    drain(lane_u, 1, 7)
    weight_grad(lane_d, 7, ((rotk, 0, 0), (rotk, 1, 0)))
    features_back(rotq, 0)
    drain(lane_d, 2, 6)
    drain(lane_u, 2, 7)
    drain(lane_d, 1, 7)
    weight_grad(lane_u, 8, ((rotk, 2, 0), (rotq, 0, 6)))
    drain(lane_d, 3, 6)
    drain(lane_u, 3, 7)
    weight_grad(lane_d, 8, ((rotq, 1, 6), (rotq, 2, 6)))
    shift_row = jnp.sum(shift_col[...].T, 0, keepdims=True)
    gain_row = jnp.sum(gain_col[...].T, 0, keepdims=True)
    gain_row = (gain_row - prm[1:2, :] * shift_row) / prm[0:1, :]
    ends = jnp.concatenate([gain_row, shift_row, lng[2:8, :]], 0)
    ends = jnp.concatenate([ends, jnp.zeros((8, 128), F32)], 1)
    for i in range(32):
        k, shift = (24 * i) // 128, (24 * i) % 128
        pair = ends[:, 128 * k : 128 * k + 256]
        if shift:
            pair = pltpu.roll(pair, 256 - shift, 1)
        rp[i % 2, i // 8, (i // 4) % 2, (i // 2) % 2] = pair[:, :128]
    lane_p = Reduce(at, (rp, b1p, sp, b2p, s2p, b3p, s3p, b4p), ps, pr, True)
    lane_p.start(0, 0)
    drain(lane_d, 4, 6)
    drain(lane_u, 4, 7)
    drain(lane_d, 2, 7)
    drain(lane_u, 1, 8)
    for unit in range(6):
        post(flu, 0, unit).wait_recv()
    lines = []
    for i in range(4):
        cols = slice(64 * i, 64 * i + 64)
        lines.append(jnp.concatenate([res_u[ch, h, :, cols] for ch in range(6) for h in range(2)], 1))
    hidden_pick()

    def hidden_back(wide):
        out = dot_nt(wide[:, :256], picks[0][...])
        out = out + dot_nt(wide[:, 256:512], picks[1][...])
        return out + dot_nt(wide[:, 512:], picks[2][...])

    back = unpick(jnp.concatenate(lines, 0), hidden_back)
    for i in range(4):
        up_out[:, 768 * i : 768 * i + 768] = back[24 * i : 24 * i + 24]

    def first_back(i, _):
        r = rows(i, TILE_B)
        dn = jnp.zeros((TILE_B, 768), F32)
        for base, ref in ((0, rotk), (3, vv), (6, rotq)):
            for g in range(3):
                dn = dn + dot_nt(ref[r, 256 * g : 256 * g + 256], block(base + g))
        hat, inverse = norm(xb[r, :].astype(F32))
        eg = dn * prm[0:1, :]
        m1 = jnp.mean(eg, -1, keepdims=True)
        m2 = jnp.mean(eg * hat, -1, keepdims=True)
        mixed[r, :] = (dsec[r, :] + inverse * (eg - m1 - hat * m2)).astype(BF16)
        return 0

    load_x.wait()
    tiles = padded // TILE_B

    def store_dx(q):
        count = padded // 4
        r = pl.ds(count * q, count if q < 3 else tokens_here - 3 * count)
        return pltpu.make_async_copy(mixed.at[r], dx_hbm.at[r], local.at[4 + q])

    quarter = tiles // 4
    lax.fori_loop(0, quarter, first_back, 0)
    store_dx(0).start()
    drain(lane_d, 3, 7)
    drain(lane_u, 2, 8)
    drain(lane_d, 1, 8)
    lane_p.step(1, 0, before=False)
    lax.fori_loop(quarter, 2 * quarter, first_back, 0)
    store_dx(1).start()
    drain(lane_d, 4, 7)
    drain(lane_u, 3, 8)
    drain(lane_d, 2, 8)
    lane_p.step(2, 0, before=False)
    lax.fori_loop(2 * quarter, 3 * quarter, first_back, 0)
    store_dx(2).start()
    drain(lane_u, 4, 8)
    drain(lane_d, 3, 8)
    lane_p.step(3, 0, before=False)
    lax.fori_loop(3 * quarter, tiles, first_back, 0)
    store_dx(3).start()
    drain(lane_d, 4, 8)
    params_out[...] = lane_p.step(4, 0)
    for phase in range(4):
        lane_p.wait_sent(phase, 0)
        lane_u.wait_sent(phase, 0)
        lane_d.wait_sent(phase, 0)
    for flat, par, unit in ((flu, 1, 7), (flu, 0, 8), (fld, 1, 10), (fld, 0, 11)):
        post(flat, par, unit).wait_send()
    for unit in range(6, 12):
        post(flu, 0, unit).wait_recv()
    for u, unit in enumerate(units):
        if u not in (6, 8):
            unit.sent()
    params.sent()
    turned = unpick(
        jnp.concatenate(
            [res_u[u, h] for u, h in ((10, 0), (10, 1), (8, 0), (8, 1), (11, 0), (11, 1))], 0
        ),
        lambda wide: dot_nt(wide, halves_pick()),
    )
    for g in range(3):
        here_k, here_v, here_q, here_o = (slice(k + 256 * g, k + 256 * g + 256) for k in range(0, 3072, 768))
        wide_out[:, here_k] = turned[24 * g : 24 * g + 24]
        wide_out[:, here_q] = turned[72 + 24 * g : 96 + 24 * g]
        u, h = ((9, 1), (7, 0), (7, 1))[g]
        wide_out[:, here_v] = res_u[u, h]
        u, h = ((6, 0), (6, 1), (9, 0))[g]
        wide_out[:, here_o] = res_u[u, h]
    store_out.wait()
    for q in range(4):
        store_dx(q).wait()


def fused_device(
    tokens,
    lengths,
    feature_directions,
    first_gain,
    first_shift,
    query_weight,
    key_weight,
    value_weight,
    out_weight,
    second_gain,
    second_shift,
    up_weight,
    down_weight,
    out_cotangent,
):
    tokens_here, width = tokens.shape
    mols = lengths.shape[0]
    length = tokens_here // mols
    padded = -(-tokens_here // 416) * 416
    share = first_gain.shape[0]

    vectors = jnp.stack([first_gain, first_shift, second_gain, second_shift]).astype(F32)
    params = jnp.pad(vectors, ((0, 4), (0, 128 - share)))

    frequency = np.float32(10000.0) ** (-np.arange(32, dtype=np.float32) * np.float32(2.0 / 64))
    angles = (np.arange(padded) % length).astype(np.float32)[:, None] * frequency[None, :]
    scale = 64.0**-0.25
    cosine = jnp.asarray(np.tile(np.cos(angles) * scale, (1, 4)), F32)
    sine = jnp.asarray(np.tile(np.sin(angles) * scale, (1, 4)), F32)
    lane_head = np.arange(128) // 32
    ones_rot = jnp.asarray(np.tile(lane_head, 2)[:, None] == lane_head[None, :], BF16)
    value_head = np.arange(256) // 64
    ones_val = jnp.asarray(value_head[:, None] == lane_head[None, :], BF16)
    diagonal = jnp.asarray(lane_head[:, None] == value_head[None, :], F32)

    def vm(shape, kind):
        return pltpu.VMEM(shape, kind)

    def lane(block, kind, sums):
        shapes = [(2, 4, 2, 2), (2, 4, 2, 2), (2, 4, 2), (2, 4), (2, 3)]
        if sums:
            shapes = [(2, 4, 2, 2), (2, 4, 2, 2), (4, 2, 2), (2, 4, 2), (4, 2), (2, 4), (4,), (2, 3)]
        return [vm(shape + block, kind) for shape in shapes]

    rows16 = (padded, width)
    scratch = [
        vm((12, 2, 4, 2, 2, 48, 256), BF16),
        vm((6, 2, 4, 2, 2, 16, 768), BF16),
        vm((2, 4, 2, 2, 8, 128), F32),
        vm((12, 24, 256), F32),
        vm(rows16, BF16),
        vm(rows16, BF16),
        vm(rows16, BF16),
        vm(rows16, BF16),
        vm(rows16, BF16),
        vm((padded, 384), BF16),
        vm((padded, 384), BF16),
        vm(rows16, BF16),
        vm(rows16, BF16),
        vm((padded, 128), F32),
        vm(rows16, F32),
        vm(rows16, F32),
        vm((padded, 512), BF16),
        vm((width + 16, padded), BF16),
        vm((8, width), F32),
        vm((8, width), F32),
    ]
    scratch += lane((48, 256), BF16, False) + [vm((2, 2, 24, 256), F32)] * 2
    scratch += lane((48, 256), BF16, False) + lane((8, 128), F32, True)
    scratch += [
        vm((12, 2, 24, 256), F32),
        pltpu.SemaphoreType.DMA((19, 6)),
        pltpu.SemaphoreType.DMA((19, 6)),
        pltpu.SemaphoreType.DMA((2,)),
        pltpu.SemaphoreType.DMA((2,)),
    ]
    scratch += [pltpu.SemaphoreType.DMA((2, 6))] * 6 + [pltpu.SemaphoreType.DMA((12,))] * 2
    scratch += [vm((padded, 128), F32)] * 2 + [vm((3, 256, 256), BF16)]
    scratch += [pltpu.SemaphoreType.DMA((8,))]
    spaces = [pl.ANY, pl.ANY, pltpu.SMEM] + [pltpu.VMEM] * 8 + [pl.ANY] * 2 + [pltpu.VMEM] * 3
    kernel = functools.partial(layer_kernel, (tokens_here, padded, length, mols))
    outs = pl.pallas_call(
        kernel,
        out_shape=[
            jax.ShapeDtypeStruct(tokens.shape, BF16),
            jax.ShapeDtypeStruct(tokens.shape, BF16),
            jax.ShapeDtypeStruct((share, 4 * width), F32),
            jax.ShapeDtypeStruct(up_weight.shape, F32),
            jax.ShapeDtypeStruct(down_weight.shape, F32),
            jax.ShapeDtypeStruct((8, 128), F32),
        ],
        in_specs=[pl.BlockSpec(memory_space=s) for s in spaces],
        out_specs=[pl.BlockSpec(memory_space=s) for s in [pl.ANY] * 2 + [pltpu.VMEM] * 4],
        scratch_shapes=scratch,
        compiler_params=pltpu.CompilerParams(
            collective_id=0, has_side_effects=True, vmem_limit_bytes=VMEM_BYTES
        ),
        name="encoder_layer",
    )(
        tokens,
        out_cotangent,
        lengths,
        params,
        key_weight,
        value_weight,
        query_weight,
        out_weight,
        up_weight,
        down_weight,
        feature_directions.transpose(0, 2, 1),
        cosine,
        sine,
        ones_rot,
        ones_val,
        diagonal,
    )
    output, input_grad, wide_grad, ups, downs, vector_grad = outs
    keys, values, queries, mixes = (
        wide_grad[:, width * k : width * k + width] for k in range(4)
    )
    vectors = [vector_grad[row, :share] for row in range(4)]
    return (
        output,
        input_grad,
        vectors[0],
        vectors[1],
        queries,
        keys,
        values,
        mixes,
        vectors[2],
        vectors[3],
        ups,
        downs,
    )


LAGS = (0, 2, 4, 6)
AHEAD = 0
TILE_F = 832
TILE_P = 416
TILE_S = 416
TILE_B = 208
TILE_FB = 416
VMEM_BYTES = 62 * 1024 * 1024


def solution(mesh):
    placed = (
        P("fsdp", None),
        P("fsdp"),
        P(),
        P("fsdp"),
        P("fsdp"),
        P("fsdp", None),
        P("fsdp", None),
        P("fsdp", None),
        P("fsdp", None),
        P("fsdp"),
        P("fsdp"),
        P("fsdp", None),
        P("fsdp", None),
        P("fsdp", None),
    )
    fused = mesh.shape["fsdp"] == 32
    return jax.shard_map(
        fused_device if fused else per_device,
        mesh=mesh,
        in_specs=placed,
        out_specs=(
            P("fsdp", None),
            P("fsdp", None),
            P("fsdp"),
            P("fsdp"),
            P("fsdp", None),
            P("fsdp", None),
            P("fsdp", None),
            P("fsdp", None),
            P("fsdp"),
            P("fsdp"),
            P("fsdp", None),
            P("fsdp", None),
        ),
        check_vma=False,
    )
```

```python
import functools

import jax
import jax.numpy as jnp
import numpy as np
from jax import lax
from jax.experimental import pallas as pl
from jax.experimental.pallas import tpu as pltpu
from jax.sharding import PartitionSpec as P

F32 = jnp.float32
BF16 = jnp.bfloat16


def rotate_scale(vectors):
    half_size = vectors.shape[-1] // 2
    positions = jnp.arange(vectors.shape[1], dtype=jnp.float32)
    frequency = 10000.0 ** (-jnp.arange(half_size, dtype=jnp.float32) * 2.0 / vectors.shape[-1])
    angles = positions[:, None] * frequency[None, :]
    cosine_table = jnp.cos(angles)[None, :, None, :]
    sine_table = jnp.sin(angles)[None, :, None, :]
    first_half = vectors[..., :half_size]
    second_half = vectors[..., half_size:]
    turned = jnp.concatenate(
        [
            first_half * cosine_table - second_half * sine_table,
            first_half * sine_table + second_half * cosine_table,
        ],
        -1,
    )
    return turned * vectors.shape[-1] ** (-0.25)


def feature_map(vectors, directions):
    turned = rotate_scale(vectors)
    logits = jnp.einsum("slhd,hdm->slhm", turned, directions, precision=lax.Precision.HIGHEST)
    logits = logits - 0.5 * jnp.sum(turned * turned, -1, keepdims=True)
    return jnp.exp(logits) * directions.shape[-1] ** (-0.5)


def smooth_gelu(values):
    return jax.nn.gelu(values, approximate=True)


def norm_parts(inputs, gain_row, shift_row):
    row_mean = jnp.mean(inputs, -1, keepdims=True)
    centered = inputs - row_mean
    inverse = lax.rsqrt(jnp.mean(centered * centered, -1, keepdims=True) + 1e-05)
    hat_rows = centered * inverse
    return (
        hat_rows * gain_row.astype(jnp.float32) + shift_row.astype(jnp.float32),
        hat_rows,
        inverse,
    )


def norm_back(grad_rows, hat_rows, inverse, gain_row):
    scaled = grad_rows * gain_row.astype(jnp.float32)
    return inverse * (
        scaled
        - jnp.mean(scaled, -1, keepdims=True)
        - hat_rows * jnp.mean(scaled * hat_rows, -1, keepdims=True)
    )


def per_device(
    tokens,
    lengths,
    feature_directions,
    first_gain,
    first_shift,
    query_weight,
    key_weight,
    value_weight,
    out_weight,
    second_gain,
    second_shift,
    up_weight,
    down_weight,
    out_cotangent,
):
    model_width = tokens.shape[1]
    head_count = feature_directions.shape[0]
    head_size = model_width // head_count
    seqs_here = lengths.shape[0]
    length = tokens.shape[0] // seqs_here
    inputs = tokens.astype(jnp.float32)

    def feature_of(row_block):
        return feature_map(
            row_block.reshape(seqs_here, length, head_count, head_size), feature_directions
        )

    gain_one, shift_one, query_full, key_full, value_full, out_full = (
        lax.all_gather(first_gain, "fsdp", axis=0, tiled=True),
        lax.all_gather(first_shift, "fsdp", axis=0, tiled=True),
        lax.all_gather(query_weight, "fsdp", axis=0, tiled=True),
        lax.all_gather(key_weight, "fsdp", axis=0, tiled=True),
        lax.all_gather(value_weight, "fsdp", axis=0, tiled=True),
        lax.all_gather(out_weight, "fsdp", axis=0, tiled=True),
    )
    normed_wide, hat_one, inverse_one = norm_parts(inputs, gain_one, shift_one)
    normed = normed_wide.astype(jnp.bfloat16)
    query_rows = jnp.dot(normed, query_full, preferred_element_type=jnp.float32)
    key_rows = jnp.dot(normed, key_full, preferred_element_type=jnp.float32)
    value_rows = jnp.dot(normed, value_full, preferred_element_type=jnp.float32)
    value_low = value_rows.astype(jnp.bfloat16).reshape(seqs_here, length, head_count, head_size)
    query_raw, query_back = jax.vjp(feature_of, query_rows)
    key_raw, key_back = jax.vjp(feature_of, key_rows)
    query_low = query_raw.astype(jnp.bfloat16)
    key_low = key_raw.astype(jnp.bfloat16)
    positions = jnp.arange(length, dtype=jnp.int32)
    key_live = positions[None, :] < lengths[:, None]
    masked = key_low * key_live.astype(jnp.bfloat16)[:, :, None, None]
    state_sum = jnp.einsum("slhm,slhd->shmd", masked, value_low, preferred_element_type=jnp.float32)
    state_low = state_sum.astype(jnp.bfloat16)
    totals = jnp.sum(masked.astype(jnp.float32), 1)
    numerator = jnp.einsum(
        "slhm,shmd->slhd", query_low, state_low, preferred_element_type=jnp.float32
    )
    query_wide = query_low.astype(jnp.float32)
    denominator = jnp.einsum("slhm,shm->slh", query_wide, totals, precision=lax.Precision.HIGHEST)
    mixed_rows = (numerator / denominator[..., None]).reshape(-1, model_width).astype(jnp.bfloat16)
    branch = jnp.dot(mixed_rows, out_full, preferred_element_type=jnp.float32)
    middle = inputs + branch
    gain_two, shift_two, up_full, down_full = (
        lax.all_gather(second_gain, "fsdp", axis=0, tiled=True),
        lax.all_gather(second_shift, "fsdp", axis=0, tiled=True),
        lax.all_gather(up_weight, "fsdp", axis=0, tiled=True),
        lax.all_gather(down_weight, "fsdp", axis=0, tiled=True),
    )
    second_wide, hat_two, inverse_two = norm_parts(middle, gain_two, shift_two)
    second = second_wide.astype(jnp.bfloat16)
    up_rows = jnp.dot(second, up_full, preferred_element_type=jnp.float32)
    gelu_rows, gelu_back = jax.vjp(smooth_gelu, up_rows)
    hidden = gelu_rows.astype(jnp.bfloat16)
    output = (middle + jnp.dot(hidden, down_full, preferred_element_type=jnp.float32)).astype(
        jnp.bfloat16
    )
    gain_two, shift_two, up_full, down_full = (
        lax.all_gather(second_gain, "fsdp", axis=0, tiled=True),
        lax.all_gather(second_shift, "fsdp", axis=0, tiled=True),
        lax.all_gather(up_weight, "fsdp", axis=0, tiled=True),
        lax.all_gather(down_weight, "fsdp", axis=0, tiled=True),
    )
    gain_one, shift_one, query_full, key_full, value_full, out_full = (
        lax.all_gather(first_gain, "fsdp", axis=0, tiled=True),
        lax.all_gather(first_shift, "fsdp", axis=0, tiled=True),
        lax.all_gather(query_weight, "fsdp", axis=0, tiled=True),
        lax.all_gather(key_weight, "fsdp", axis=0, tiled=True),
        lax.all_gather(value_weight, "fsdp", axis=0, tiled=True),
        lax.all_gather(out_weight, "fsdp", axis=0, tiled=True),
    )
    down_grad = jnp.einsum("tf,td->fd", hidden, out_cotangent, preferred_element_type=jnp.float32)
    hidden_grad = jnp.einsum(
        "td,fd->tf", out_cotangent, down_full, preferred_element_type=jnp.float32
    )
    pre_grad = gelu_back(hidden_grad)[0].astype(jnp.bfloat16)
    up_grad = jnp.einsum("td,tf->df", second, pre_grad, preferred_element_type=jnp.float32)
    second_grad = jnp.einsum("tf,df->td", pre_grad, up_full, preferred_element_type=jnp.float32)
    gain_two_grad = jnp.sum(second_grad * hat_two, 0)
    shift_two_grad = jnp.sum(second_grad, 0)
    middle_grad = out_cotangent.astype(jnp.float32) + norm_back(
        second_grad, hat_two, inverse_two, gain_two
    )
    ffn_shards = (
        lax.psum_scatter(gain_two_grad, "fsdp", scatter_dimension=0, tiled=True),
        lax.psum_scatter(shift_two_grad, "fsdp", scatter_dimension=0, tiled=True),
        lax.psum_scatter(up_grad, "fsdp", scatter_dimension=0, tiled=True),
        lax.psum_scatter(down_grad, "fsdp", scatter_dimension=0, tiled=True),
    )
    branch_grad = middle_grad.astype(jnp.bfloat16)
    out_grad = jnp.einsum("td,te->de", mixed_rows, branch_grad, preferred_element_type=jnp.float32)
    mixed_grad = jnp.einsum("te,de->td", branch_grad, out_full, preferred_element_type=jnp.float32)
    mixed_grad = mixed_grad.reshape(seqs_here, length, head_count, head_size)
    numer_grad = (mixed_grad / denominator[..., None]).astype(jnp.bfloat16)
    denom_grad = -jnp.sum(mixed_grad * numerator, -1) / (denominator * denominator)
    query_feat_grad = jnp.einsum(
        "slhd,shmd->slhm", numer_grad, state_low, preferred_element_type=jnp.float32
    )
    query_feat_grad = query_feat_grad + denom_grad[..., None] * totals[:, None]
    state_grad = jnp.einsum(
        "slhm,slhd->shmd", query_low, numer_grad, preferred_element_type=jnp.float32
    ).astype(jnp.bfloat16)
    totals_grad = jnp.einsum(
        "slh,slhm->shm", denom_grad, query_wide, precision=lax.Precision.HIGHEST
    )
    key_feat_grad = jnp.einsum(
        "slhd,shmd->slhm", value_low, state_grad, preferred_element_type=jnp.float32
    )
    key_feat_grad = (key_feat_grad + totals_grad[:, None]) * key_live.astype(jnp.float32)[
        :, :, None, None
    ]
    value_grad = jnp.einsum(
        "slhm,shmd->slhd", masked, state_grad, preferred_element_type=jnp.float32
    )
    value_grad = value_grad.reshape(-1, model_width).astype(jnp.bfloat16)
    query_grad = query_back(query_feat_grad)[0].astype(jnp.bfloat16)
    key_grad = key_back(key_feat_grad)[0].astype(jnp.bfloat16)
    normed_grad = jnp.einsum(
        "te,de->td", query_grad, query_full, preferred_element_type=jnp.float32
    )
    normed_grad = normed_grad + jnp.einsum(
        "te,de->td", key_grad, key_full, preferred_element_type=jnp.float32
    )
    normed_grad = normed_grad + jnp.einsum(
        "te,de->td", value_grad, value_full, preferred_element_type=jnp.float32
    )
    query_weight_grad = jnp.einsum(
        "td,te->de", normed, query_grad, preferred_element_type=jnp.float32
    )
    key_weight_grad = jnp.einsum("td,te->de", normed, key_grad, preferred_element_type=jnp.float32)
    value_weight_grad = jnp.einsum(
        "td,te->de", normed, value_grad, preferred_element_type=jnp.float32
    )
    gain_one_grad = jnp.sum(normed_grad * hat_one, 0)
    shift_one_grad = jnp.sum(normed_grad, 0)
    input_grad = middle_grad + norm_back(normed_grad, hat_one, inverse_one, gain_one)
    attn_shards = (
        lax.psum_scatter(gain_one_grad, "fsdp", scatter_dimension=0, tiled=True),
        lax.psum_scatter(shift_one_grad, "fsdp", scatter_dimension=0, tiled=True),
        lax.psum_scatter(query_weight_grad, "fsdp", scatter_dimension=0, tiled=True),
        lax.psum_scatter(key_weight_grad, "fsdp", scatter_dimension=0, tiled=True),
        lax.psum_scatter(value_weight_grad, "fsdp", scatter_dimension=0, tiled=True),
        lax.psum_scatter(out_grad, "fsdp", scatter_dimension=0, tiled=True),
    )
    shards = tuple(attn_shards) + tuple(ffn_shards)
    return (output, input_grad.astype(jnp.bfloat16)) + shards


def dot_nn(a, b):
    return lax.dot_general(a, b, (((1,), (0,)), ((), ())), preferred_element_type=F32)


def dot_nt(a, b):
    return lax.dot_general(a, b, (((1,), (1,)), ((), ())), preferred_element_type=F32)


def dot_tn(a, b):
    return lax.dot_general(a, b, (((0,), (0,)), ((), ())), preferred_element_type=F32)


def split_low(v):
    high = v.astype(BF16)
    return high, (v - high.astype(F32)).astype(BF16)


def remote(src, dst, send, recv, device):
    return pltpu.make_async_remote_copy(
        src_ref=src,
        dst_ref=dst,
        send_sem=send,
        recv_sem=recv,
        device_id=(device,),
        device_id_type=pl.DeviceIdType.MESH,
    )


class Place:
    def __init__(self):
        me = lax.axis_index("fsdp")
        self.c = lax.rem(me, 2)
        self.x = lax.rem(lax.div(me, 2), 2)
        self.y = lax.rem(lax.div(me, 4), 2)
        self.z = lax.div(me, 8)
        self.sib = me + 1 - 2 * self.c
        self.px = me + 2 - 4 * self.x
        self.py = me + 4 - 8 * self.y
        self.zs = [lax.rem(self.z + d, 4) for d in (1, 2, 3)]
        self.pz = [me + (zp - self.z) * 8 for zp in self.zs]

    def greet(self):
        barrier = pltpu.get_barrier_semaphore()
        for peer in [self.sib, self.px, self.py] + self.pz:
            pl.semaphore_signal(
                barrier, inc=1, device_id=(peer,), device_id_type=pl.DeviceIdType.MESH
            )

    def enter(self):
        pl.semaphore_wait(pltpu.get_barrier_semaphore(), 6)


class Gather:
    def __init__(self, at, buf, send, recv):
        c, z, y, x = at.c, at.z, at.y, at.x
        mine = buf.at[c, z, y, x]
        low, high = pl.ds(0, 2), pl.ds(2, 2)

        def share(part, k, peer):
            return remote(part, part, send.at[k], recv.at[k], peer)

        self.copies = [
            [share(mine, d, at.pz[d]) for d in range(3)],
            [share(buf.at[c, low, y, x], 3, at.py), share(buf.at[c, high, y, x], 4, at.px)],
            [share(buf.at[c, low, :, x], 5, at.px), share(buf.at[c, high, y], 6, at.py)],
            [share(buf.at[c], 7, at.sib)],
        ]

    def start(self, phase):
        for copy in self.copies[phase]:
            copy.start()

    def arrived(self, phase):
        for copy in self.copies[phase]:
            copy.wait_recv()

    def sent(self):
        for phase in self.copies:
            for copy in phase:
                copy.wait_send()


class Reduce:
    def __init__(self, at, refs, send, recv):
        self.at = at
        self.R, self.B1, self.S, self.B2, self.S2, self.B3, self.S3, self.B4 = refs
        self.send, self.recv = send, recv

    def copies(self, phase, par):
        at, s, r = self.at, self.send.at[par], self.recv.at[par]
        low, high = pl.ds(0, 2), pl.ds(2, 2)

        def move(src, dst, k, peer):
            return remote(src, dst, s.at[k], r.at[k], peer)

        if phase == 0:
            return [move(self.R.at[1 - at.c], self.B1.at[par], 0, at.sib)]
        if phase == 1:
            return [
                move(self.S.at[low, 1 - at.y], self.B2.at[par, low], 1, at.py),
                move(self.S.at[high, :, 1 - at.x], self.B2.at[par, high], 2, at.px),
            ]
        if phase == 2:
            return [
                move(self.S2.at[low, 1 - at.x], self.B3.at[par, low], 3, at.px),
                move(self.S2.at[high, 1 - at.y], self.B3.at[par, high], 4, at.py),
            ]
        return [
            move(self.S3.at[at.zs[d]], self.B4.at[par, d], 5 + d, at.pz[d]) for d in range(3)
        ]

    def start(self, phase, par):
        for copy in self.copies(phase, par):
            copy.start()

    def wait_sent(self, phase, par):
        for copy in self.copies(phase, par):
            copy.wait_send()

    def step(self, phase, par, before=True):
        at = self.at
        for copy in self.copies(phase - 1, par):
            copy.wait_recv()
        if phase == 4:
            total = self.S3[at.z].astype(F32)
            for d in range(3):
                total = total + self.B4[par, d].astype(F32)
            return total
        if before is True:
            self.wait_sent(phase, 1 - par)
        elif before is not False:

            @pl.when(before)
            def _():
                self.wait_sent(phase, 1 - par)

        kind = self.S.dtype

        def add(i, _, upper):
            if phase == 1:
                own, other, out = self.R[at.c, i], self.B1[par, i], self.S
            elif phase == 2:
                own = self.S[i, :, at.x] if upper else self.S[i, at.y]
                other, out = self.B2[par, i], self.S2
            else:
                own = self.S2[i, at.y if upper else at.x]
                other, out = self.B3[par, i], self.S3
            out[i] = (own.astype(F32) + other.astype(F32)).astype(kind)
            return 0

        lax.fori_loop(0, 2, functools.partial(add, upper=False), 0)
        lax.fori_loop(2, 4, functools.partial(add, upper=True), 0)
        self.start(phase, par)
        return None


def layer_kernel(
    sizes,
    x_hbm,
    dy_hbm,
    lengths,
    params_here,
    key_here,
    value_here,
    query_here,
    mix_here,
    up_here,
    down_here,
    directions,
    cosine_hbm,
    sine_hbm,
    ones_rot,
    ones_val,
    diagonal,
    out_hbm,
    dx_hbm,
    wide_out,
    up_out,
    down_out,
    params_out,
    wu,
    wd,
    pb,
    px32,
    xb,
    normed,
    rotq,
    rotk,
    vv,
    pq,
    pk,
    mixed,
    second,
    inv2,
    acc,
    dsec,
    dpre,
    tb,
    prm,
    lng,
    ru,
    b1u,
    b2u,
    b3u,
    b4u,
    flu,
    fld,
    rd,
    b1d,
    b2d,
    b3d,
    b4d,
    rp,
    b1p,
    sp,
    b2p,
    s2p,
    b3p,
    s3p,
    b4p,
    res_u,
    ag_send,
    ag_recv,
    pre_send,
    pre_recv,
    us,
    ur,
    ds_,
    dr,
    ps,
    pr,
    qs,
    qr,
    cosine,
    sine,
    feats,
    local,
):
    tokens_here, padded, length, mols = sizes
    spare = padded - tokens_here
    at = Place()
    at.greet()
    hid = mixed
    load_x = pltpu.make_async_copy(x_hbm, xb.at[pl.ds(0, tokens_here)], local.at[0])
    def load_dy(k):
        r = pl.ds(832 * k, 832 if k == 0 else tokens_here - 832)
        return pltpu.make_async_copy(dy_hbm.at[r], xb.at[r], local.at[4 + k])

    load_x.start()
    load_cos = pltpu.make_async_copy(cosine_hbm, cosine, local.at[2])
    load_sin = pltpu.make_async_copy(sine_hbm, sine, local.at[3])
    load_cos.start()
    load_sin.start()

    def halves_pick():
        t = lax.broadcasted_iota(jnp.int32, (1, 256), 1)
        source = ((t & 127) >> 5) * 64 + (t >> 7) * 32 + (t & 31)
        row = lax.broadcasted_iota(jnp.int32, (256, 256), 0)
        return jnp.where(row == source, 1.0, 0.0).astype(BF16)

    picks = [hid.at[0:768, 0:256], hid.at[0:768, 256:512], dpre.at[0:768, 0:256]]

    def hidden_pick():
        for b in range(3):
            t = lax.broadcasted_iota(jnp.int32, (1, 256), 1) + 256 * b
            owner = 2 * ((t & 63) >> 4) + ((t & 127) >> 6)
            source = 96 * owner + 16 * (t >> 7) + (t & 15)

            def fill(i, _):
                row = lax.broadcasted_iota(jnp.int32, (128, 256), 0) + 128 * i
                r = pl.ds(pl.multiple_of(128 * i, 128), 128)
                picks[b][r, :] = jnp.where(row == source, 1.0, 0.0).astype(BF16)
                return 0

            lax.fori_loop(0, 6, fill, 0)

    halves = halves_pick()
    for g in range(3):
        col = slice(256 * g, 256 * g + 256)
        for base, ref in ((0, key_here), (6, query_here)):
            res_u[(base + g) // 2, (base + g) % 2] = dot_nn(ref[:, col], halves)
        for base, ref in ((3, value_here), (9, mix_here)):
            res_u[(base + g) // 2, (base + g) % 2] = ref[:, col].astype(F32)
    pb[at.c, at.z, at.y, at.x] = params_here[...]
    for ch in range(6):
        wd[ch, at.c, at.z, at.y, at.x] = down_here[16 * ch : 16 * ch + 16, :]
    at.enter()

    def swap_of(k):
        half = pl.ds(6 * k, 6)
        src = res_u.at[half, 1 - at.c]
        return remote(src, px32.at[half], pre_send.at[k], pre_recv.at[k], at.sib)

    swaps = [swap_of(k) for k in range(2)]
    swaps[0].start()
    up32 = up_here[...].astype(F32)
    stacked = jnp.concatenate([up32[:, 768 * i : 768 * i + 768] for i in range(4)], 0)
    hidden_pick()
    stacked = stacked.astype(BF16)
    order = jnp.concatenate([dot_nn(stacked, pick[...]) for pick in picks], 1)
    for ch in range(6):
        for h in range(2):
            at_col = 128 * ch + 64 * h
            res_u[6 + ch, h] = jnp.concatenate(
                [order[24 * i : 24 * i + 24, at_col : at_col + 64] for i in range(4)], 1
            )
    swaps[1].start()
    swaps[0].wait()
    even = at.c == 0

    def build(u, _):
        mine = res_u[u, at.c]
        other = px32[u]
        top = jnp.where(even, mine, other)
        low = jnp.where(even, other, mine)
        wu[u, at.c, at.z, at.y, at.x] = jnp.concatenate([top, low], 0).astype(BF16)
        return 0

    lax.fori_loop(0, 6, build, 0)
    tail = pl.ds(tokens_here, spare)
    xb[tail, :] = jnp.zeros((spare, xb.shape[1]), BF16)
    mixed[tail, :] = jnp.zeros((spare, xb.shape[1]), BF16)
    lng[...] = jnp.zeros(lng.shape, F32)
    tb[768:784, :] = jnp.ones((16, padded), BF16)

    def gather_unit(u):
        if u < 6:
            buf = wu.at[u]
        else:
            buf = wu.at[6 + (u - 6) // 2] if u % 2 == 0 else wd.at[(u - 6) // 2]
        return Gather(at, buf, ag_send.at[u], ag_recv.at[u])

    units = [gather_unit(u) for u in range(18)]
    params = Gather(at, pb, ag_send.at[18], ag_recv.at[18])
    state = {"tick": 0, "needed": set()}
    lags, last = LAGS, tuple(min(17, v + 2 * AHEAD) for v in (13, 11, 9, 7))

    def tick(count=1):
        for _ in range(count):
            t = state["tick"]
            state["tick"] += 1
            if t == 0:
                params.start(0)
            for k in range(4):
                u = t - lags[k]
                if 0 <= u <= last[k]:
                    if k:
                        if u == 0:
                            params.arrived(k - 1)
                            params.start(k)
                        units[u].arrived(k - 1)
                    units[u].start(k)

    def need(u):
        while state["tick"] <= u + lags[3]:
            tick()
        if u not in state["needed"]:
            state["needed"].add(u)
            units[u].arrived(3)

    tick(1)
    swaps[1].wait()
    lax.fori_loop(6, 12, build, 0)
    tick(1)
    for g in range(3):
        for half in range(2):
            lines = []
            for hh in range(4):
                piece = directions[4 * g + hh, :, 32 * half : 32 * half + 32].T
                gap = jnp.zeros((32, 32), F32)
                lines.append(jnp.concatenate([gap] * hh + [piece] + [gap] * (3 - hh), 1))
            high, low = split_low(jnp.concatenate(lines, 0))
            feats[g, 128 * half : 128 * half + 128, :] = jnp.concatenate([high, low], 1)

    def run(start, stop, body):
        if stop - start <= 4:
            for i in range(start, stop):
                body(i, 0)
        else:
            lax.fori_loop(start, stop, body, 0)

    def rows(i, count):
        return pl.ds(pl.multiple_of(i * count, 16), count)

    def norm(v):
        centered = v - jnp.mean(v, -1, keepdims=True)
        inverse = lax.rsqrt(jnp.mean(centered * centered, -1, keepdims=True) + 1e-05)
        return centered * inverse, inverse

    load_x.wait()
    load_cos.wait()
    load_sin.wait()

    def first_hat(i, _):
        r = rows(i, 208)
        acc[r, :] = norm(xb[r, :].astype(F32))[0]
        return 0

    lax.fori_loop(0, padded // 208, first_hat, 0)
    tick(lags[3] - 1)
    params.arrived(3)
    parts = [jnp.zeros((8, 128), F32) for _ in range(7)]
    for i in range(32):
        block = pb[i % 2, i // 8, (i // 4) % 2, (i // 2) % 2]
        k, shift = (24 * i) // 128, (24 * i) % 128
        pair = jnp.concatenate([block, jnp.zeros((8, 128), F32)], 1)
        if shift:
            pair = pltpu.roll(pair, shift, 1)
        parts[k] = parts[k] + pair[:, :128]
        parts[k + 1] = parts[k + 1] + pair[:, 128:]
    prm[...] = jnp.concatenate(parts[:6], 1)

    def first_norm(i, _):
        r = rows(i, 208)
        normed[r, :] = (acc[r, :] * prm[0:1, :] + prm[1:2, :]).astype(BF16)
        return 0

    lax.fori_loop(0, padded // 208, first_norm, 0)

    def block(b):
        return wu[b // 2, b % 2].reshape(768, 256)

    def blocks(base):
        return jnp.concatenate([block(base + g) for g in range(3)], 1)

    def features(base, rot_ref, feat_ref, groups):
        def body(i, _):
            r = rows(i, TILE_F)
            ct, st = cosine[r, :], sine[r, :]
            wide = jnp.concatenate([block(base + g) for g in groups], 1)
            us = dot_nn(normed[r, :], wide)
            for g in groups:
                u = us[:, 256 * (g - groups[0]) : 256 * (g - groups[0]) + 256]
                a, b = u[:, :128], u[:, 128:]
                rot = jnp.concatenate([a * ct - b * st, a * st + b * ct], 1)
                high, low = split_low(rot)
                sq_high, sq_low = split_low(rot * rot)
                two = dot_nn(high, feats[g])
                logits = two[:, :128] + two[:, 128:] + dot_nn(low, feats[g, :, :128])
                norms = dot_nn(sq_high, ones_rot[...]) + dot_nn(sq_low, ones_rot[...])
                p = jnp.exp(logits - 0.5 * norms) * (32**-0.5)
                rot_ref[r, 256 * g : 256 * g + 256] = high
                feat_ref[r, 128 * g : 128 * g + 128] = p.astype(BF16)
            return 0

        lax.fori_loop(0, padded // TILE_F, body, 0)

    def values(groups):
        def body(i, _):
            r = rows(i, 832)
            for g in groups:
                vv[r, 256 * g : 256 * g + 256] = dot_nn(normed[r, :], block(3 + g)).astype(BF16)
            return 0

        run(0, padded // 832, body)

    need(0)
    features(0, rotk, pk, (0, 1))
    tick()
    need(1)
    features(0, rotk, pk, (2,))
    values((0,))
    tick()
    need(2)
    values((1, 2))
    tick()
    need(3)
    features(6, rotq, pq, (0, 1))
    tick()
    need(4)
    features(6, rotq, pq, (2,))
    tick()
    here = pl.ds(0, tokens_here)
    spill = pltpu.make_async_copy(normed.at[here], dx_hbm, local.at[1])
    spill.start()
    hat2 = normed

    window = 224

    def places(s):
        begin = lax.div(s * length, 16) * 16
        pos = lax.broadcasted_iota(jnp.int32, (window, 1), 0) - (s * length - begin)
        valid = (pos >= 0) & (pos < length)
        live = valid & (pos < lengths[s])
        return pl.ds(pl.multiple_of(begin, 16), window), pos, valid, live

    def state_of(g, w, live, pkm):
        ones = jnp.ones((window, 256), BF16)
        diag = diagonal[...]
        st = (dot_tn(pkm, vv[w, 256 * g : 256 * g + 256]) * diag).astype(BF16)
        tot = dot_tn(pkm, ones) * diag
        tot_high, tot_low = split_low(tot)
        return st, tot_high, tot_low

    def masked_keys(g, w, live):
        keys = pk[w, 128 * g : 128 * g + 128].astype(F32)
        return jnp.where(live, keys, 0.0)

    def attend(s, _):
        w, pos, valid, live = places(s)
        mixes = []
        for g in range(3):
            pkm = masked_keys(g, w, live).astype(BF16)
            st, tot_high, tot_low = state_of(g, w, live, pkm)
            pqg = pq[w, 128 * g : 128 * g + 128]
            num = dot_nn(pqg, st)
            den = dot_nn(pqg, tot_high) + dot_nn(pqg, tot_low)
            mixes.append(jnp.where(valid, num / den, 0.0))
        mix = jnp.where(pos < 0, mixed[w, :].astype(F32), jnp.concatenate(mixes, 1))
        mixed[w, :] = mix.astype(BF16)
        return 0

    for k in range(4):
        lax.fori_loop(2 * k, 2 * k + 2, attend, 0, unroll=2)
        tick()
    need(5)
    spill.wait()

    spill_mixed = pltpu.make_async_copy(mixed.at[here], out_hbm, local.at[2])
    spill_mixed.start()

    def project(i, _):
        r = rows(i, TILE_P)
        branch = dot_nn(mixed[r, :], blocks(9))
        middle = xb[r, :].astype(F32) + branch
        acc[r, :] = middle
        hat, inverse = norm(middle)
        hat2[r, :] = hat.astype(BF16)
        inv2[r, :] = jnp.broadcast_to(inverse, (TILE_P, 128))
        second[r, :] = (hat * prm[2:3, :] + prm[3:4, :]).astype(BF16)
        dsec[r, :] = jnp.zeros((TILE_P, 768), F32)
        return 0

    half = padded // TILE_P // 2
    lax.fori_loop(0, half, project, 0)
    load_dy(0).start()
    tick()
    lax.fori_loop(half, 2 * half, project, 0)

    def turn(src):
        for j in range(6):
            tb[128 * j : 128 * j + 128, :] = src[:, 128 * j : 128 * j + 128].T

    load_dy(1).start()
    turn(second)
    load_dy(0).wait()
    load_dy(1).wait()
    spill_mixed.wait()
    while state["tick"] <= last[0] + lags[0]:
        tick()
    need(6)
    need(7)

    def pair_of(q):
        up, down = 6 + 2 * q, 7 + 2 * q
        return (
            Gather(at, wu.at[6 + q], ag_send.at[up], ag_recv.at[up]),
            Gather(at, wd.at[q], ag_send.at[down], ag_recv.at[down]),
        )

    def gather_on(q, phase):
        @pl.when(q < 6)
        def _():
            for unit in pair_of(q):
                if phase:
                    unit.arrived(phase - 1)
                unit.start(phase)

    su, sd = wu.at[6, 0], wu.at[6, 1]
    s2u, s2d = wu.at[7, 0, :, 0], wu.at[7, 0, :, 1]
    s3u, s3d = wu.at[7, 1, :, 0, 0], wu.at[7, 1, :, 0, 1]
    lane_u = Reduce(at, (ru, b1u, su, b2u, s2u, b3u, s3u, b4u), us, ur)
    lane_d = Reduce(at, (rd, b1d, sd, b2d, s2d, b3d, s3d, b4d), ds_, dr)

    def post(flat, par, unit):
        return remote(
            flat.at[par, 1 - at.c], res_u.at[unit, at.c], qs.at[unit], qr.at[unit], at.sib
        )

    def emit_pair(flat, total, par, unit):
        flat[par] = total.reshape(flat.shape[1:])
        res_u[unit, at.c] = flat[par, at.c]
        post(flat, par, unit).start()

    def emit_own(total, unit):
        for b in range(3):
            r = pl.ds(pl.multiple_of(16 * unit, 16), 16)
            down_out[r, 256 * b : 256 * b + 256] = total[16 * b : 16 * b + 16]

    def keep(lane, half, grad):
        lane.R[half] = grad.astype(BF16).reshape(4, 2, 2, 48, 256)

    slope = 0.7978845608028654
    bend = 0.044715

    def up_block(ch):
        return jnp.concatenate([wu[6 + ch, h].reshape(768, 256) for h in range(2)], 1)

    def chunk(ch, _):
        def inner(i, _):
            r = rows(i, 416)
            lines, cot = second[r, :], xb[r, :]
            pres = dot_nn(lines, up_block(ch))
            dhs = dot_nt(cot, wd[ch].reshape(512, 768))
            for h in range(2):
                pre = pres[:, 256 * h : 256 * h + 256]
                dh = dhs[:, 256 * h : 256 * h + 256]
                square = pre * pre
                t = jnp.tanh(pre * (slope + slope * bend * square))
                half = 0.5 + 0.5 * t
                col = slice(256 * h, 256 * h + 256)
                hid[r, col] = (pre * half).astype(BF16)
                bent = slope + 3.0 * slope * bend * square
                grad = half + 0.5 * pre * (1.0 - t * t) * bent
                dpre[r, col] = (dh * grad).astype(BF16)
            return 0

        @pl.when(ch >= 1)
        def _():
            for unit in pair_of(ch):
                unit.arrived(3)

        run(0, 4, inner)
        for phase in (3, 2, 1, 0):
            gather_on(ch + 4 + AHEAD - phase, phase)
        par = lax.rem(ch, 2)
        for k in (1, 2):

            @pl.when(ch == k)
            def _():
                units[4 + 2 * k].sent()

        for phase in (4, 3, 2, 1):
            j = ch - phase

            @pl.when(j >= 0)
            def _():
                old = lax.rem(j + 8, 2)
                if phase == 4:

                    @pl.when(j >= 2)
                    def _():
                        post(flu, old, j - 2).wait_send()

                up_total = lane_u.step(phase, old, before=j >= 1)
                down_total = lane_d.step(phase, old, before=j >= 1)
                if phase == 4:
                    emit_pair(flu, up_total, old, j)
                    emit_own(down_total, j)

        @pl.when(ch >= 1)
        def _():
            lane_u.wait_sent(0, 1 - par)
            lane_d.wait_sent(0, 1 - par)

        grads = dot_nn(tb[:768, :], dpre[...])
        keep(lane_u, 0, grads[:, :256])
        keep(lane_u, 1, grads[:, 256:])
        grads = dot_tn(hid[:, 0:512], xb[...]).astype(BF16)
        for h in range(2):
            for b in range(3):
                part = grads[256 * h : 256 * h + 256, 256 * b : 256 * b + 256]
                rd[h, :, :, :, 16 * b : 16 * b + 16, :] = part.reshape(4, 2, 2, 16, 256)
        lane_u.start(0, par)
        lane_d.start(0, par)

        def outer(i, _):
            r = rows(i, 832)
            acc[r, :] += dot_nn(hid[r, 0:512], wd[ch].reshape(512, 768))
            dsec[r, :] += dot_nt(dpre[r, :], up_block(ch))
            return 0

        run(0, 2, outer)
        return 0

    lax.fori_loop(0, 6, chunk, 0)
    fetch_mixed = pltpu.make_async_copy(out_hbm, mixed.at[here], local.at[2])
    fetch_mixed.start()

    def drain(lane, phase, j):
        par = j % 2
        pairs = lane is lane_u or j >= 6
        flat = flu if lane is lane_u else fld
        unit = j if lane is lane_u else j + 3
        if phase == 4 and pairs and (lane is lane_u or j >= 8):
            post(flat, par, unit - 2).wait_send()
        total = lane.step(phase, par)
        if phase == 4:
            if pairs:
                emit_pair(flat, total, par, unit)
            else:
                emit_own(total, j)

    def both(*steps):
        for phase, j in steps:
            drain(lane_u, phase, j)
            drain(lane_d, phase, j)

    both((4, 2), (3, 3), (2, 4), (1, 5))

    def second_back(i, _):
        r = rows(i, TILE_S)
        e = dsec[r, :]
        hat = hat2[r, :].astype(F32)
        inverse = inv2[r, :][:, :1]
        lng[2:3, :] += jnp.sum(e * hat, 0, keepdims=True)
        lng[3:4, :] += jnp.sum(e, 0, keepdims=True)
        eg = e * prm[2:3, :]
        m1 = jnp.mean(eg, -1, keepdims=True)
        m2 = jnp.mean(eg * hat, -1, keepdims=True)
        dmid = xb[r, :].astype(F32) + inverse * (eg - m1 - hat * m2)
        dsec[r, :] = dmid
        low = dmid.astype(BF16)
        second[r, :] = low
        hat2[r, :] = acc[r, :].astype(BF16)
        acc[r, :] = dot_nt(low, blocks(9))
        return 0

    half = padded // TILE_S // 2
    lax.fori_loop(0, half, second_back, 0)
    both((4, 3), (3, 4), (2, 5))
    lax.fori_loop(half, 2 * half, second_back, 0)
    store_out = pltpu.make_async_copy(hat2.at[pl.ds(0, tokens_here)], out_hbm, local.at[0])
    fetch_mixed.wait()
    store_out.start()
    load_x = pltpu.make_async_copy(x_hbm, xb.at[pl.ds(0, tokens_here)], local.at[2])
    load_x.start()

    def weight_grad(lane, j, parts):
        lane.wait_sent(0, 1 - j % 2)
        for h, (ref, col, base) in enumerate(parts):

            @pl.when(at.z >= 0)
            def _():
                keep(lane, h, grad_of(ref, col, base))

        lane.start(0, j % 2)

    def grad_of(ref, col, base):
        lines = ref[:, 256 * col : 256 * col + 256]
        if base is None:
            return dot_nn(tb[:768, :], lines)
        both_of = dot_nn(tb[...], lines)
        grad, sums = both_of[:768], both_of[768:769]
        weight = block(base + col).astype(F32)
        share = weight * grad
        gain_col[...] += share[:, :128] + share[:, 128:]
        share = weight * sums
        shift_col[...] += share[:, :128] + share[:, 128:]
        return grad

    gain_col, shift_col = inv2.at[0:768], inv2.at[768:1536]
    inv2[0:1536, :] = jnp.zeros((1536, 128), F32)
    turn(mixed)
    fetch = pltpu.make_async_copy(dx_hbm, mixed.at[here], local.at[1])
    fetch.start()
    both((4, 4), (3, 5))
    weight_grad(lane_u, 6, ((second, 0, None), (second, 1, None)))

    def attend_back(s, _):
        w, pos, valid, live = places(s)
        olds = [acc[w, 128 * j : 128 * j + 128] for j in range(6)]
        vals = [vv[w, 256 * g : 256 * g + 256] for g in range(3)]
        dq_parts, dk_parts, dv_parts = [], [], []
        for g in range(3):
            thin = slice(128 * g, 128 * g + 128)
            diag = diagonal[...]
            pk32 = masked_keys(g, w, live)
            pkm = pk32.astype(BF16)
            st, tot_high, tot_low = state_of(g, w, live, pkm)
            tot = jnp.sum(pk32, 0, keepdims=True)
            pqg = pq[w, thin]
            pq32 = jnp.where(valid, pqg.astype(F32), 0.0)
            num = dot_nn(pqg, st)
            den = dot_nn(pqg, tot_high) + dot_nn(pqg, tot_low)
            share = 1.0 / den
            part = jnp.concatenate([olds[2 * g], olds[2 * g + 1]], 1) * share
            dnum = jnp.where(valid, part, 0.0).astype(BF16)
            e_high, e_low = split_low(jnp.where(valid, -part * (num * share), 0.0))
            dden = dot_nn(e_high, ones_val[...]) + dot_nn(e_low, ones_val[...])
            dpq = dot_nt(dnum, st) + dden * tot
            dst = (dot_tn(pqg, dnum) * diag).astype(BF16)
            dtot = jnp.sum(dden * pq32, 0, keepdims=True)
            dpk = dot_nt(vals[g], dst) + dtot
            dv_parts.append(dot_nn(pkm, dst))
            dq_parts.append(dpq * pq32)
            dk_parts.append(dpk * pk32)
        for j, new in enumerate(dq_parts + dk_parts):
            acc[w, 128 * j : 128 * j + 128] = jnp.where(valid, new, olds[j])
        for g in range(3):
            new = jnp.where(valid, dv_parts[g], vals[g].astype(F32))
            vv[w, 256 * g : 256 * g + 256] = new.astype(BF16)
        return 0

    lax.fori_loop(0, mols // 2, attend_back, 0, unroll=2)
    both((4, 5))
    drain(lane_u, 1, 6)
    lax.fori_loop(mols // 2, mols, attend_back, 0, unroll=2)
    vv[tail, :] = jnp.zeros((spare, 768), BF16)
    drain(lane_u, 2, 6)
    lane_d.wait_sent(0, 1)
    keep(lane_d, 0, grad_of(second, 2, None))
    fetch.wait()
    turn(mixed)
    keep(lane_d, 1, grad_of(vv, 0, 3))
    lane_d.start(0, 0)
    weight_grad(lane_u, 7, ((vv, 1, 3), (vv, 2, 3)))
    drain(lane_u, 3, 6)

    def unpick(lines, pick):
        high, rest = lines.astype(BF16), lines
        parts = [high]
        for _ in range(2):
            rest = rest - parts[-1].astype(F32)
            parts.append(rest.astype(BF16))
        count = lines.shape[0]
        wide = jnp.concatenate([part.astype(F32) for part in parts], 0).astype(BF16)
        out = pick(wide)
        return out[:count] + out[count : 2 * count] + out[2 * count :]

    def features_back(rot_ref, base):
        def body(i, _):
            r = rows(i, TILE_FB)
            ct, sn = cosine[r, :], sine[r, :]
            for g in range(3):
                wide = slice(256 * g, 256 * g + 256)
                high, low = split_low(acc[r, base + 128 * g : base + 128 * g + 128])
                rot = rot_ref[r, wide].astype(F32)
                total = dot_nt(high, ones_rot[...]) + dot_nt(low, ones_rot[...])
                back = dot_nt(jnp.concatenate([high, high], 1), feats[g])
                back = back + dot_nt(low, feats[g, :, :128]) - rot * total
                a, b = back[:, :128], back[:, 128:]
                turned = jnp.concatenate([a * ct + b * sn, b * ct - a * sn], 1)
                rot_ref[r, wide] = turned.astype(BF16)
            return 0

        lax.fori_loop(0, padded // TILE_FB, body, 0)

    features_back(rotk, 384)
    drain(lane_d, 1, 6)
    drain(lane_u, 4, 6)
    drain(lane_u, 1, 7)
    weight_grad(lane_d, 7, ((rotk, 0, 0), (rotk, 1, 0)))
    features_back(rotq, 0)
    drain(lane_d, 2, 6)
    drain(lane_u, 2, 7)
    drain(lane_d, 1, 7)
    weight_grad(lane_u, 8, ((rotk, 2, 0), (rotq, 0, 6)))
    drain(lane_d, 3, 6)
    drain(lane_u, 3, 7)
    weight_grad(lane_d, 8, ((rotq, 1, 6), (rotq, 2, 6)))
    shift_row = jnp.sum(shift_col[...].T, 0, keepdims=True)
    gain_row = jnp.sum(gain_col[...].T, 0, keepdims=True)
    gain_row = (gain_row - prm[1:2, :] * shift_row) / prm[0:1, :]
    ends = jnp.concatenate([gain_row, shift_row, lng[2:8, :]], 0)
    ends = jnp.concatenate([ends, jnp.zeros((8, 128), F32)], 1)
    for i in range(32):
        k, shift = (24 * i) // 128, (24 * i) % 128
        pair = ends[:, 128 * k : 128 * k + 256]
        if shift:
            pair = pltpu.roll(pair, 256 - shift, 1)
        rp[i % 2, i // 8, (i // 4) % 2, (i // 2) % 2] = pair[:, :128]
    lane_p = Reduce(at, (rp, b1p, sp, b2p, s2p, b3p, s3p, b4p), ps, pr)
    lane_p.start(0, 0)
    drain(lane_d, 4, 6)
    drain(lane_u, 4, 7)
    drain(lane_d, 2, 7)
    drain(lane_u, 1, 8)
    for unit in range(6):
        post(flu, 0, unit).wait_recv()
    lines = []
    for i in range(4):
        cols = slice(64 * i, 64 * i + 64)
        lines.append(jnp.concatenate([res_u[ch, h, :, cols] for ch in range(6) for h in range(2)], 1))
    hidden_pick()

    def hidden_back(wide):
        out = dot_nt(wide[:, :256], picks[0][...])
        out = out + dot_nt(wide[:, 256:512], picks[1][...])
        return out + dot_nt(wide[:, 512:], picks[2][...])

    back = unpick(jnp.concatenate(lines, 0), hidden_back)
    for i in range(4):
        up_out[:, 768 * i : 768 * i + 768] = back[24 * i : 24 * i + 24]

    def first_back(i, _):
        r = rows(i, TILE_B)
        dn = jnp.zeros((TILE_B, 768), F32)
        for base, ref in ((0, rotk), (3, vv), (6, rotq)):
            for g in range(3):
                dn = dn + dot_nt(ref[r, 256 * g : 256 * g + 256], block(base + g))
        hat, inverse = norm(xb[r, :].astype(F32))
        eg = dn * prm[0:1, :]
        m1 = jnp.mean(eg, -1, keepdims=True)
        m2 = jnp.mean(eg * hat, -1, keepdims=True)
        mixed[r, :] = (dsec[r, :] + inverse * (eg - m1 - hat * m2)).astype(BF16)
        return 0

    load_x.wait()
    tiles = padded // TILE_B

    def store_dx(q):
        count = padded // 4
        r = pl.ds(count * q, count if q < 3 else tokens_here - 3 * count)
        return pltpu.make_async_copy(mixed.at[r], dx_hbm.at[r], local.at[4 + q])

    quarter = tiles // 4
    lax.fori_loop(0, quarter, first_back, 0)
    store_dx(0).start()
    drain(lane_d, 3, 7)
    drain(lane_u, 2, 8)
    drain(lane_d, 1, 8)
    lane_p.step(1, 0, before=False)
    lax.fori_loop(quarter, 2 * quarter, first_back, 0)
    store_dx(1).start()
    drain(lane_d, 4, 7)
    drain(lane_u, 3, 8)
    drain(lane_d, 2, 8)
    lane_p.step(2, 0, before=False)
    lax.fori_loop(2 * quarter, 3 * quarter, first_back, 0)
    store_dx(2).start()
    drain(lane_u, 4, 8)
    drain(lane_d, 3, 8)
    lane_p.step(3, 0, before=False)
    lax.fori_loop(3 * quarter, tiles, first_back, 0)
    store_dx(3).start()
    drain(lane_d, 4, 8)
    params_out[...] = lane_p.step(4, 0)
    for phase in range(4):
        lane_p.wait_sent(phase, 0)
        lane_u.wait_sent(phase, 0)
        lane_d.wait_sent(phase, 0)
    for flat, par, unit in ((flu, 1, 7), (flu, 0, 8), (fld, 1, 10), (fld, 0, 11)):
        post(flat, par, unit).wait_send()
    for unit in range(6, 12):
        post(flu, 0, unit).wait_recv()
    for u, unit in enumerate(units):
        if u not in (6, 8):
            unit.sent()
    params.sent()
    turned = unpick(
        jnp.concatenate(
            [res_u[u, h] for u, h in ((10, 0), (10, 1), (8, 0), (8, 1), (11, 0), (11, 1))], 0
        ),
        lambda wide: dot_nt(wide, halves_pick()),
    )
    for g in range(3):
        here_k, here_v, here_q, here_o = (slice(k + 256 * g, k + 256 * g + 256) for k in range(0, 3072, 768))
        wide_out[:, here_k] = turned[24 * g : 24 * g + 24]
        wide_out[:, here_q] = turned[72 + 24 * g : 96 + 24 * g]
        u, h = ((9, 1), (7, 0), (7, 1))[g]
        wide_out[:, here_v] = res_u[u, h]
        u, h = ((6, 0), (6, 1), (9, 0))[g]
        wide_out[:, here_o] = res_u[u, h]
    store_out.wait()
    for q in range(4):
        store_dx(q).wait()


def fused_device(
    tokens,
    lengths,
    feature_directions,
    first_gain,
    first_shift,
    query_weight,
    key_weight,
    value_weight,
    out_weight,
    second_gain,
    second_shift,
    up_weight,
    down_weight,
    out_cotangent,
):
    tokens_here, width = tokens.shape
    mols = lengths.shape[0]
    length = tokens_here // mols
    padded = -(-tokens_here // 416) * 416
    share = first_gain.shape[0]

    vectors = jnp.stack([first_gain, first_shift, second_gain, second_shift]).astype(F32)
    params = jnp.pad(vectors, ((0, 4), (0, 128 - share)))

    frequency = np.float32(10000.0) ** (-np.arange(32, dtype=np.float32) * np.float32(2.0 / 64))
    angles = (np.arange(padded) % length).astype(np.float32)[:, None] * frequency[None, :]
    scale = 64.0**-0.25
    cosine = jnp.asarray(np.tile(np.cos(angles) * scale, (1, 4)), F32)
    sine = jnp.asarray(np.tile(np.sin(angles) * scale, (1, 4)), F32)
    lane_head = np.arange(128) // 32
    ones_rot = jnp.asarray(np.tile(lane_head, 2)[:, None] == lane_head[None, :], BF16)
    value_head = np.arange(256) // 64
    ones_val = jnp.asarray(value_head[:, None] == lane_head[None, :], BF16)
    diagonal = jnp.asarray(lane_head[:, None] == value_head[None, :], F32)

    def vm(shape, kind):
        return pltpu.VMEM(shape, kind)

    def lane(block, kind, sums):
        shapes = [(2, 4, 2, 2), (2, 4, 2, 2), (2, 4, 2), (2, 4), (2, 3)]
        if sums:
            shapes = [(2, 4, 2, 2), (2, 4, 2, 2), (4, 2, 2), (2, 4, 2), (4, 2), (2, 4), (4,), (2, 3)]
        return [vm(shape + block, kind) for shape in shapes]

    rows16 = (padded, width)
    scratch = [
        vm((12, 2, 4, 2, 2, 48, 256), BF16),
        vm((6, 2, 4, 2, 2, 16, 768), BF16),
        vm((2, 4, 2, 2, 8, 128), F32),
        vm((12, 24, 256), F32),
        vm(rows16, BF16),
        vm(rows16, BF16),
        vm(rows16, BF16),
        vm(rows16, BF16),
        vm(rows16, BF16),
        vm((padded, 384), BF16),
        vm((padded, 384), BF16),
        vm(rows16, BF16),
        vm(rows16, BF16),
        vm((padded, 128), F32),
        vm(rows16, F32),
        vm(rows16, F32),
        vm((padded, 512), BF16),
        vm((width + 16, padded), BF16),
        vm((8, width), F32),
        vm((8, width), F32),
    ]
    scratch += lane((48, 256), BF16, False) + [vm((2, 2, 24, 256), F32)] * 2
    scratch += lane((48, 256), BF16, False) + lane((8, 128), F32, True)
    scratch += [
        vm((12, 2, 24, 256), F32),
        pltpu.SemaphoreType.DMA((19, 8)),
        pltpu.SemaphoreType.DMA((19, 8)),
        pltpu.SemaphoreType.DMA((2,)),
        pltpu.SemaphoreType.DMA((2,)),
    ]
    scratch += [pltpu.SemaphoreType.DMA((2, 8))] * 6 + [pltpu.SemaphoreType.DMA((12,))] * 2
    scratch += [vm((padded, 128), F32)] * 2 + [vm((3, 256, 256), BF16)]
    scratch += [pltpu.SemaphoreType.DMA((8,))]
    spaces = [pl.ANY, pl.ANY, pltpu.SMEM] + [pltpu.VMEM] * 8 + [pl.ANY] * 2 + [pltpu.VMEM] * 3
    kernel = functools.partial(layer_kernel, (tokens_here, padded, length, mols))
    outs = pl.pallas_call(
        kernel,
        out_shape=[
            jax.ShapeDtypeStruct(tokens.shape, BF16),
            jax.ShapeDtypeStruct(tokens.shape, BF16),
            jax.ShapeDtypeStruct((share, 4 * width), F32),
            jax.ShapeDtypeStruct(up_weight.shape, F32),
            jax.ShapeDtypeStruct(down_weight.shape, F32),
            jax.ShapeDtypeStruct((8, 128), F32),
        ],
        in_specs=[pl.BlockSpec(memory_space=s) for s in spaces],
        out_specs=[pl.BlockSpec(memory_space=s) for s in [pl.ANY] * 2 + [pltpu.VMEM] * 4],
        scratch_shapes=scratch,
        compiler_params=pltpu.CompilerParams(
            collective_id=0, has_side_effects=True, vmem_limit_bytes=VMEM_BYTES
        ),
        name="encoder_layer",
    )(
        tokens,
        out_cotangent,
        lengths,
        params,
        key_weight,
        value_weight,
        query_weight,
        out_weight,
        up_weight,
        down_weight,
        feature_directions.transpose(0, 2, 1),
        cosine,
        sine,
        ones_rot,
        ones_val,
        diagonal,
    )
    output, input_grad, wide_grad, ups, downs, vector_grad = outs
    keys, values, queries, mixes = (
        wide_grad[:, width * k : width * k + width] for k in range(4)
    )
    vectors = [vector_grad[row, :share] for row in range(4)]
    return (
        output,
        input_grad,
        vectors[0],
        vectors[1],
        queries,
        keys,
        values,
        mixes,
        vectors[2],
        vectors[3],
        ups,
        downs,
    )


LAGS = (0, 2, 4, 6)
AHEAD = 0
TILE_F = 832
TILE_P = 416
TILE_S = 416
TILE_B = 208
TILE_FB = 416
VMEM_BYTES = 62 * 1024 * 1024


def solution(mesh):
    placed = (
        P("fsdp", None),
        P("fsdp"),
        P(),
        P("fsdp"),
        P("fsdp"),
        P("fsdp", None),
        P("fsdp", None),
        P("fsdp", None),
        P("fsdp", None),
        P("fsdp"),
        P("fsdp"),
        P("fsdp", None),
        P("fsdp", None),
        P("fsdp", None),
    )
    fused = mesh.shape["fsdp"] == 32
    return jax.shard_map(
        fused_device if fused else per_device,
        mesh=mesh,
        in_specs=placed,
        out_specs=(
            P("fsdp", None),
            P("fsdp", None),
            P("fsdp"),
            P("fsdp"),
            P("fsdp", None),
            P("fsdp", None),
            P("fsdp", None),
            P("fsdp", None),
            P("fsdp"),
            P("fsdp"),
            P("fsdp", None),
            P("fsdp", None),
        ),
        check_vma=False,
    )
```

```python
import functools

import jax
import jax.numpy as jnp
import numpy as np
from jax import lax
from jax.experimental import pallas as pl
from jax.experimental.pallas import tpu as pltpu
from jax.sharding import PartitionSpec as P

F32 = jnp.float32
BF16 = jnp.bfloat16


def rotate_scale(vectors):
    half_size = vectors.shape[-1] // 2
    positions = jnp.arange(vectors.shape[1], dtype=jnp.float32)
    frequency = 10000.0 ** (-jnp.arange(half_size, dtype=jnp.float32) * 2.0 / vectors.shape[-1])
    angles = positions[:, None] * frequency[None, :]
    cosine_table = jnp.cos(angles)[None, :, None, :]
    sine_table = jnp.sin(angles)[None, :, None, :]
    first_half = vectors[..., :half_size]
    second_half = vectors[..., half_size:]
    turned = jnp.concatenate(
        [
            first_half * cosine_table - second_half * sine_table,
            first_half * sine_table + second_half * cosine_table,
        ],
        -1,
    )
    return turned * vectors.shape[-1] ** (-0.25)


def feature_map(vectors, directions):
    turned = rotate_scale(vectors)
    logits = jnp.einsum("slhd,hdm->slhm", turned, directions, precision=lax.Precision.HIGHEST)
    logits = logits - 0.5 * jnp.sum(turned * turned, -1, keepdims=True)
    return jnp.exp(logits) * directions.shape[-1] ** (-0.5)


def smooth_gelu(values):
    return jax.nn.gelu(values, approximate=True)


def norm_parts(inputs, gain_row, shift_row):
    row_mean = jnp.mean(inputs, -1, keepdims=True)
    centered = inputs - row_mean
    inverse = lax.rsqrt(jnp.mean(centered * centered, -1, keepdims=True) + 1e-05)
    hat_rows = centered * inverse
    return (
        hat_rows * gain_row.astype(jnp.float32) + shift_row.astype(jnp.float32),
        hat_rows,
        inverse,
    )


def norm_back(grad_rows, hat_rows, inverse, gain_row):
    scaled = grad_rows * gain_row.astype(jnp.float32)
    return inverse * (
        scaled
        - jnp.mean(scaled, -1, keepdims=True)
        - hat_rows * jnp.mean(scaled * hat_rows, -1, keepdims=True)
    )


def per_device(
    tokens,
    lengths,
    feature_directions,
    first_gain,
    first_shift,
    query_weight,
    key_weight,
    value_weight,
    out_weight,
    second_gain,
    second_shift,
    up_weight,
    down_weight,
    out_cotangent,
):
    model_width = tokens.shape[1]
    head_count = feature_directions.shape[0]
    head_size = model_width // head_count
    seqs_here = lengths.shape[0]
    length = tokens.shape[0] // seqs_here
    inputs = tokens.astype(jnp.float32)

    def feature_of(row_block):
        return feature_map(
            row_block.reshape(seqs_here, length, head_count, head_size), feature_directions
        )

    gain_one, shift_one, query_full, key_full, value_full, out_full = (
        lax.all_gather(first_gain, "fsdp", axis=0, tiled=True),
        lax.all_gather(first_shift, "fsdp", axis=0, tiled=True),
        lax.all_gather(query_weight, "fsdp", axis=0, tiled=True),
        lax.all_gather(key_weight, "fsdp", axis=0, tiled=True),
        lax.all_gather(value_weight, "fsdp", axis=0, tiled=True),
        lax.all_gather(out_weight, "fsdp", axis=0, tiled=True),
    )
    normed_wide, hat_one, inverse_one = norm_parts(inputs, gain_one, shift_one)
    normed = normed_wide.astype(jnp.bfloat16)
    query_rows = jnp.dot(normed, query_full, preferred_element_type=jnp.float32)
    key_rows = jnp.dot(normed, key_full, preferred_element_type=jnp.float32)
    value_rows = jnp.dot(normed, value_full, preferred_element_type=jnp.float32)
    value_low = value_rows.astype(jnp.bfloat16).reshape(seqs_here, length, head_count, head_size)
    query_raw, query_back = jax.vjp(feature_of, query_rows)
    key_raw, key_back = jax.vjp(feature_of, key_rows)
    query_low = query_raw.astype(jnp.bfloat16)
    key_low = key_raw.astype(jnp.bfloat16)
    positions = jnp.arange(length, dtype=jnp.int32)
    key_live = positions[None, :] < lengths[:, None]
    masked = key_low * key_live.astype(jnp.bfloat16)[:, :, None, None]
    state_sum = jnp.einsum("slhm,slhd->shmd", masked, value_low, preferred_element_type=jnp.float32)
    state_low = state_sum.astype(jnp.bfloat16)
    totals = jnp.sum(masked.astype(jnp.float32), 1)
    numerator = jnp.einsum(
        "slhm,shmd->slhd", query_low, state_low, preferred_element_type=jnp.float32
    )
    query_wide = query_low.astype(jnp.float32)
    denominator = jnp.einsum("slhm,shm->slh", query_wide, totals, precision=lax.Precision.HIGHEST)
    mixed_rows = (numerator / denominator[..., None]).reshape(-1, model_width).astype(jnp.bfloat16)
    branch = jnp.dot(mixed_rows, out_full, preferred_element_type=jnp.float32)
    middle = inputs + branch
    gain_two, shift_two, up_full, down_full = (
        lax.all_gather(second_gain, "fsdp", axis=0, tiled=True),
        lax.all_gather(second_shift, "fsdp", axis=0, tiled=True),
        lax.all_gather(up_weight, "fsdp", axis=0, tiled=True),
        lax.all_gather(down_weight, "fsdp", axis=0, tiled=True),
    )
    second_wide, hat_two, inverse_two = norm_parts(middle, gain_two, shift_two)
    second = second_wide.astype(jnp.bfloat16)
    up_rows = jnp.dot(second, up_full, preferred_element_type=jnp.float32)
    gelu_rows, gelu_back = jax.vjp(smooth_gelu, up_rows)
    hidden = gelu_rows.astype(jnp.bfloat16)
    output = (middle + jnp.dot(hidden, down_full, preferred_element_type=jnp.float32)).astype(
        jnp.bfloat16
    )
    gain_two, shift_two, up_full, down_full = (
        lax.all_gather(second_gain, "fsdp", axis=0, tiled=True),
        lax.all_gather(second_shift, "fsdp", axis=0, tiled=True),
        lax.all_gather(up_weight, "fsdp", axis=0, tiled=True),
        lax.all_gather(down_weight, "fsdp", axis=0, tiled=True),
    )
    gain_one, shift_one, query_full, key_full, value_full, out_full = (
        lax.all_gather(first_gain, "fsdp", axis=0, tiled=True),
        lax.all_gather(first_shift, "fsdp", axis=0, tiled=True),
        lax.all_gather(query_weight, "fsdp", axis=0, tiled=True),
        lax.all_gather(key_weight, "fsdp", axis=0, tiled=True),
        lax.all_gather(value_weight, "fsdp", axis=0, tiled=True),
        lax.all_gather(out_weight, "fsdp", axis=0, tiled=True),
    )
    down_grad = jnp.einsum("tf,td->fd", hidden, out_cotangent, preferred_element_type=jnp.float32)
    hidden_grad = jnp.einsum(
        "td,fd->tf", out_cotangent, down_full, preferred_element_type=jnp.float32
    )
    pre_grad = gelu_back(hidden_grad)[0].astype(jnp.bfloat16)
    up_grad = jnp.einsum("td,tf->df", second, pre_grad, preferred_element_type=jnp.float32)
    second_grad = jnp.einsum("tf,df->td", pre_grad, up_full, preferred_element_type=jnp.float32)
    gain_two_grad = jnp.sum(second_grad * hat_two, 0)
    shift_two_grad = jnp.sum(second_grad, 0)
    middle_grad = out_cotangent.astype(jnp.float32) + norm_back(
        second_grad, hat_two, inverse_two, gain_two
    )
    ffn_shards = (
        lax.psum_scatter(gain_two_grad, "fsdp", scatter_dimension=0, tiled=True),
        lax.psum_scatter(shift_two_grad, "fsdp", scatter_dimension=0, tiled=True),
        lax.psum_scatter(up_grad, "fsdp", scatter_dimension=0, tiled=True),
        lax.psum_scatter(down_grad, "fsdp", scatter_dimension=0, tiled=True),
    )
    branch_grad = middle_grad.astype(jnp.bfloat16)
    out_grad = jnp.einsum("td,te->de", mixed_rows, branch_grad, preferred_element_type=jnp.float32)
    mixed_grad = jnp.einsum("te,de->td", branch_grad, out_full, preferred_element_type=jnp.float32)
    mixed_grad = mixed_grad.reshape(seqs_here, length, head_count, head_size)
    numer_grad = (mixed_grad / denominator[..., None]).astype(jnp.bfloat16)
    denom_grad = -jnp.sum(mixed_grad * numerator, -1) / (denominator * denominator)
    query_feat_grad = jnp.einsum(
        "slhd,shmd->slhm", numer_grad, state_low, preferred_element_type=jnp.float32
    )
    query_feat_grad = query_feat_grad + denom_grad[..., None] * totals[:, None]
    state_grad = jnp.einsum(
        "slhm,slhd->shmd", query_low, numer_grad, preferred_element_type=jnp.float32
    ).astype(jnp.bfloat16)
    totals_grad = jnp.einsum(
        "slh,slhm->shm", denom_grad, query_wide, precision=lax.Precision.HIGHEST
    )
    key_feat_grad = jnp.einsum(
        "slhd,shmd->slhm", value_low, state_grad, preferred_element_type=jnp.float32
    )
    key_feat_grad = (key_feat_grad + totals_grad[:, None]) * key_live.astype(jnp.float32)[
        :, :, None, None
    ]
    value_grad = jnp.einsum(
        "slhm,shmd->slhd", masked, state_grad, preferred_element_type=jnp.float32
    )
    value_grad = value_grad.reshape(-1, model_width).astype(jnp.bfloat16)
    query_grad = query_back(query_feat_grad)[0].astype(jnp.bfloat16)
    key_grad = key_back(key_feat_grad)[0].astype(jnp.bfloat16)
    normed_grad = jnp.einsum(
        "te,de->td", query_grad, query_full, preferred_element_type=jnp.float32
    )
    normed_grad = normed_grad + jnp.einsum(
        "te,de->td", key_grad, key_full, preferred_element_type=jnp.float32
    )
    normed_grad = normed_grad + jnp.einsum(
        "te,de->td", value_grad, value_full, preferred_element_type=jnp.float32
    )
    query_weight_grad = jnp.einsum(
        "td,te->de", normed, query_grad, preferred_element_type=jnp.float32
    )
    key_weight_grad = jnp.einsum("td,te->de", normed, key_grad, preferred_element_type=jnp.float32)
    value_weight_grad = jnp.einsum(
        "td,te->de", normed, value_grad, preferred_element_type=jnp.float32
    )
    gain_one_grad = jnp.sum(normed_grad * hat_one, 0)
    shift_one_grad = jnp.sum(normed_grad, 0)
    input_grad = middle_grad + norm_back(normed_grad, hat_one, inverse_one, gain_one)
    attn_shards = (
        lax.psum_scatter(gain_one_grad, "fsdp", scatter_dimension=0, tiled=True),
        lax.psum_scatter(shift_one_grad, "fsdp", scatter_dimension=0, tiled=True),
        lax.psum_scatter(query_weight_grad, "fsdp", scatter_dimension=0, tiled=True),
        lax.psum_scatter(key_weight_grad, "fsdp", scatter_dimension=0, tiled=True),
        lax.psum_scatter(value_weight_grad, "fsdp", scatter_dimension=0, tiled=True),
        lax.psum_scatter(out_grad, "fsdp", scatter_dimension=0, tiled=True),
    )
    shards = tuple(attn_shards) + tuple(ffn_shards)
    return (output, input_grad.astype(jnp.bfloat16)) + shards


def dot_nn(a, b):
    return lax.dot_general(a, b, (((1,), (0,)), ((), ())), preferred_element_type=F32)


def dot_nt(a, b):
    return lax.dot_general(a, b, (((1,), (1,)), ((), ())), preferred_element_type=F32)


def dot_tn(a, b):
    return lax.dot_general(a, b, (((0,), (0,)), ((), ())), preferred_element_type=F32)


def split_low(v):
    high = v.astype(BF16)
    return high, (v - high.astype(F32)).astype(BF16)


def remote(src, dst, send, recv, device):
    return pltpu.make_async_remote_copy(
        src_ref=src,
        dst_ref=dst,
        send_sem=send,
        recv_sem=recv,
        device_id=(device,),
        device_id_type=pl.DeviceIdType.MESH,
    )


class Place:
    def __init__(self):
        me = lax.axis_index("fsdp")
        self.c = lax.rem(me, 2)
        self.x = lax.rem(lax.div(me, 2), 2)
        self.y = lax.rem(lax.div(me, 4), 2)
        self.z = lax.div(me, 8)
        self.sib = me + 1 - 2 * self.c
        self.px = me + 2 - 4 * self.x
        self.py = me + 4 - 8 * self.y
        self.zs = [lax.rem(self.z + d, 4) for d in (1, 2, 3)]
        self.pz = [me + (zp - self.z) * 8 for zp in self.zs]

    def greet(self):
        barrier = pltpu.get_barrier_semaphore()
        for peer in [self.sib, self.px, self.py] + self.pz:
            pl.semaphore_signal(
                barrier, inc=1, device_id=(peer,), device_id_type=pl.DeviceIdType.MESH
            )

    def enter(self):
        pl.semaphore_wait(pltpu.get_barrier_semaphore(), 6)


class Gather:
    def __init__(self, at, buf, send, recv):
        c, z, y, x = at.c, at.z, at.y, at.x
        mine = buf.at[c, z, y, x]
        low, high = pl.ds(0, 2), pl.ds(2, 2)

        def share(part, k, peer):
            return remote(part, part, send.at[k], recv.at[k], peer)

        self.copies = [
            [share(mine, d, at.pz[d]) for d in range(3)],
            [share(buf.at[c, low, y, x], 3, at.py), share(buf.at[c, high, y, x], 4, at.px)],
            [share(buf.at[c, low, :, x], 5, at.px), share(buf.at[c, high, y], 6, at.py)],
            [share(buf.at[c], 7, at.sib)],
        ]

    def start(self, phase):
        for copy in self.copies[phase]:
            copy.start()

    def arrived(self, phase):
        for copy in self.copies[phase]:
            copy.wait_recv()

    def sent(self):
        for phase in self.copies:
            for copy in phase:
                copy.wait_send()


class Reduce:
    def __init__(self, at, refs, send, recv):
        self.at = at
        self.R, self.B1, self.S, self.B2, self.S2, self.B3, self.S3, self.B4 = refs
        self.send, self.recv = send, recv

    def copies(self, phase, par):
        at, s, r = self.at, self.send.at[par], self.recv.at[par]
        low, high = pl.ds(0, 2), pl.ds(2, 2)

        def move(src, dst, k, peer):
            return remote(src, dst, s.at[k], r.at[k], peer)

        if phase == 0:
            return [move(self.R.at[1 - at.c], self.B1.at[par], 0, at.sib)]
        if phase == 1:
            return [
                move(self.S.at[low, 1 - at.y], self.B2.at[par, low], 1, at.py),
                move(self.S.at[high, :, 1 - at.x], self.B2.at[par, high], 2, at.px),
            ]
        if phase == 2:
            return [
                move(self.S2.at[low, 1 - at.x], self.B3.at[par, low], 3, at.px),
                move(self.S2.at[high, 1 - at.y], self.B3.at[par, high], 4, at.py),
            ]
        return [
            move(self.S3.at[at.zs[d]], self.B4.at[par, d], 5 + d, at.pz[d]) for d in range(3)
        ]

    def start(self, phase, par):
        for copy in self.copies(phase, par):
            copy.start()

    def wait_sent(self, phase, par):
        for copy in self.copies(phase, par):
            copy.wait_send()

    def step(self, phase, par, before=True):
        at = self.at
        for copy in self.copies(phase - 1, par):
            copy.wait_recv()
        if phase == 4:
            total = self.S3[at.z].astype(F32)
            for d in range(3):
                total = total + self.B4[par, d].astype(F32)
            return total
        if before is True:
            self.wait_sent(phase, 1 - par)
        elif before is not False:

            @pl.when(before)
            def _():
                self.wait_sent(phase, 1 - par)

        kind = self.S.dtype

        def add(i, _, upper):
            if phase == 1:
                own, other, out = self.R[at.c, i], self.B1[par, i], self.S
            elif phase == 2:
                own = self.S[i, :, at.x] if upper else self.S[i, at.y]
                other, out = self.B2[par, i], self.S2
            else:
                own = self.S2[i, at.y if upper else at.x]
                other, out = self.B3[par, i], self.S3
            out[i] = (own.astype(F32) + other.astype(F32)).astype(kind)
            return 0

        lax.fori_loop(0, 2, functools.partial(add, upper=False), 0)
        lax.fori_loop(2, 4, functools.partial(add, upper=True), 0)
        self.start(phase, par)
        return None


def layer_kernel(
    sizes,
    x_hbm,
    dy_hbm,
    lengths,
    params_here,
    key_here,
    value_here,
    query_here,
    mix_here,
    up_here,
    down_here,
    directions,
    cosine_hbm,
    sine_hbm,
    ones_rot,
    ones_val,
    diagonal,
    out_hbm,
    dx_hbm,
    wide_out,
    up_out,
    down_out,
    params_out,
    wu,
    wd,
    pb,
    px32,
    xb,
    normed,
    rotq,
    rotk,
    vv,
    pq,
    pk,
    mixed,
    second,
    inv2,
    acc,
    dsec,
    dpre,
    tb,
    prm,
    lng,
    ru,
    b1u,
    b2u,
    b3u,
    b4u,
    flu,
    fld,
    rd,
    b1d,
    b2d,
    b3d,
    b4d,
    rp,
    b1p,
    sp,
    b2p,
    s2p,
    b3p,
    s3p,
    b4p,
    res_u,
    ag_send,
    ag_recv,
    pre_send,
    pre_recv,
    us,
    ur,
    ds_,
    dr,
    ps,
    pr,
    qs,
    qr,
    cosine,
    sine,
    feats,
    local,
):
    tokens_here, padded, length, mols = sizes
    spare = padded - tokens_here
    at = Place()
    at.greet()
    hid = mixed
    load_x = pltpu.make_async_copy(x_hbm, xb.at[pl.ds(0, tokens_here)], local.at[0])
    def load_dy(k):
        r = pl.ds(832 * k, 832 if k == 0 else tokens_here - 832)
        return pltpu.make_async_copy(dy_hbm.at[r], xb.at[r], local.at[4 + k])

    load_x.start()
    load_cos = pltpu.make_async_copy(cosine_hbm, cosine, local.at[2])
    load_sin = pltpu.make_async_copy(sine_hbm, sine, local.at[3])
    load_cos.start()
    load_sin.start()

    def halves_pick():
        t = lax.broadcasted_iota(jnp.int32, (1, 256), 1)
        source = ((t & 127) >> 5) * 64 + (t >> 7) * 32 + (t & 31)
        row = lax.broadcasted_iota(jnp.int32, (256, 256), 0)
        return jnp.where(row == source, 1.0, 0.0).astype(BF16)

    picks = [hid.at[0:768, 0:256], hid.at[0:768, 256:512], dpre.at[0:768, 0:256]]

    def hidden_pick():
        for b in range(3):
            t = lax.broadcasted_iota(jnp.int32, (1, 256), 1) + 256 * b
            owner = 2 * ((t & 63) >> 4) + ((t & 127) >> 6)
            source = 96 * owner + 16 * (t >> 7) + (t & 15)

            def fill(i, _):
                row = lax.broadcasted_iota(jnp.int32, (128, 256), 0) + 128 * i
                r = pl.ds(pl.multiple_of(128 * i, 128), 128)
                picks[b][r, :] = jnp.where(row == source, 1.0, 0.0).astype(BF16)
                return 0

            lax.fori_loop(0, 6, fill, 0)

    halves = halves_pick()
    for g in range(3):
        col = slice(256 * g, 256 * g + 256)
        for base, ref in ((0, key_here), (6, query_here)):
            res_u[(base + g) // 2, (base + g) % 2] = dot_nn(ref[:, col], halves)
        for base, ref in ((3, value_here), (9, mix_here)):
            res_u[(base + g) // 2, (base + g) % 2] = ref[:, col].astype(F32)
    pb[at.c, at.z, at.y, at.x] = params_here[...]
    for ch in range(6):
        wd[ch, at.c, at.z, at.y, at.x] = down_here[16 * ch : 16 * ch + 16, :]
    at.enter()

    def swap_of(k):
        half = pl.ds(6 * k, 6)
        src = res_u.at[half, 1 - at.c]
        return remote(src, px32.at[half], pre_send.at[k], pre_recv.at[k], at.sib)

    swaps = [swap_of(k) for k in range(2)]
    swaps[0].start()
    up32 = up_here[...].astype(F32)
    stacked = jnp.concatenate([up32[:, 768 * i : 768 * i + 768] for i in range(4)], 0)
    hidden_pick()
    stacked = stacked.astype(BF16)
    order = jnp.concatenate([dot_nn(stacked, pick[...]) for pick in picks], 1)
    for ch in range(6):
        for h in range(2):
            at_col = 128 * ch + 64 * h
            res_u[6 + ch, h] = jnp.concatenate(
                [order[24 * i : 24 * i + 24, at_col : at_col + 64] for i in range(4)], 1
            )
    swaps[1].start()
    swaps[0].wait()
    even = at.c == 0

    def build(u, _):
        mine = res_u[u, at.c]
        other = px32[u]
        top = jnp.where(even, mine, other)
        low = jnp.where(even, other, mine)
        wu[u, at.c, at.z, at.y, at.x] = jnp.concatenate([top, low], 0).astype(BF16)
        return 0

    lax.fori_loop(0, 6, build, 0)
    tail = pl.ds(tokens_here, spare)
    xb[tail, :] = jnp.zeros((spare, xb.shape[1]), BF16)
    mixed[tail, :] = jnp.zeros((spare, xb.shape[1]), BF16)
    lng[...] = jnp.zeros(lng.shape, F32)
    tb[768:784, :] = jnp.ones((16, padded), BF16)

    def gather_unit(u):
        if u < 6:
            buf = wu.at[u]
        else:
            buf = wu.at[6 + (u - 6) // 2] if u % 2 == 0 else wd.at[(u - 6) // 2]
        return Gather(at, buf, ag_send.at[u], ag_recv.at[u])

    units = [gather_unit(u) for u in range(18)]
    params = Gather(at, pb, ag_send.at[18], ag_recv.at[18])
    state = {"tick": 0, "needed": set()}
    lags, last = LAGS, tuple(min(17, v + 2 * AHEAD) for v in (13, 11, 9, 7))

    def tick(count=1):
        for _ in range(count):
            t = state["tick"]
            state["tick"] += 1
            if t == 0:
                params.start(0)
            for k in range(4):
                u = t - lags[k]
                if 0 <= u <= last[k]:
                    if k:
                        if u == 0:
                            params.arrived(k - 1)
                            params.start(k)
                        units[u].arrived(k - 1)
                    units[u].start(k)

    def need(u):
        while state["tick"] <= u + lags[3]:
            tick()
        if u not in state["needed"]:
            state["needed"].add(u)
            units[u].arrived(3)

    tick(1)
    swaps[1].wait()
    lax.fori_loop(6, 12, build, 0)
    tick(1)
    for g in range(3):
        for half in range(2):
            lines = []
            for hh in range(4):
                piece = directions[4 * g + hh, :, 32 * half : 32 * half + 32].T
                gap = jnp.zeros((32, 32), F32)
                lines.append(jnp.concatenate([gap] * hh + [piece] + [gap] * (3 - hh), 1))
            high, low = split_low(jnp.concatenate(lines, 0))
            feats[g, 128 * half : 128 * half + 128, :] = jnp.concatenate([high, low], 1)

    def run(start, stop, body):
        if stop - start <= 4:
            for i in range(start, stop):
                body(i, 0)
        else:
            lax.fori_loop(start, stop, body, 0)

    def rows(i, count):
        return pl.ds(pl.multiple_of(i * count, 16), count)

    def norm(v):
        centered = v - jnp.mean(v, -1, keepdims=True)
        inverse = lax.rsqrt(jnp.mean(centered * centered, -1, keepdims=True) + 1e-05)
        return centered * inverse, inverse

    load_x.wait()
    load_cos.wait()
    load_sin.wait()

    def first_hat(i, _):
        r = rows(i, 208)
        acc[r, :] = norm(xb[r, :].astype(F32))[0]
        return 0

    lax.fori_loop(0, padded // 208, first_hat, 0)
    tick(lags[3] - 1)
    params.arrived(3)
    parts = [jnp.zeros((8, 128), F32) for _ in range(7)]
    for i in range(32):
        block = pb[i % 2, i // 8, (i // 4) % 2, (i // 2) % 2]
        k, shift = (24 * i) // 128, (24 * i) % 128
        pair = jnp.concatenate([block, jnp.zeros((8, 128), F32)], 1)
        if shift:
            pair = pltpu.roll(pair, shift, 1)
        parts[k] = parts[k] + pair[:, :128]
        parts[k + 1] = parts[k + 1] + pair[:, 128:]
    prm[...] = jnp.concatenate(parts[:6], 1)

    def first_norm(i, _):
        r = rows(i, 208)
        normed[r, :] = (acc[r, :] * prm[0:1, :] + prm[1:2, :]).astype(BF16)
        return 0

    lax.fori_loop(0, padded // 208, first_norm, 0)

    def block(b):
        return wu[b // 2, b % 2].reshape(768, 256)

    def blocks(base):
        return jnp.concatenate([block(base + g) for g in range(3)], 1)

    def features(base, rot_ref, feat_ref, groups):
        def body(i, _):
            r = rows(i, TILE_F)
            ct, st = cosine[r, :], sine[r, :]
            wide = jnp.concatenate([block(base + g) for g in groups], 1)
            us = dot_nn(normed[r, :], wide)
            for g in groups:
                u = us[:, 256 * (g - groups[0]) : 256 * (g - groups[0]) + 256]
                a, b = u[:, :128], u[:, 128:]
                rot = jnp.concatenate([a * ct - b * st, a * st + b * ct], 1)
                high, low = split_low(rot)
                sq_high, sq_low = split_low(rot * rot)
                two = dot_nn(high, feats[g])
                logits = two[:, :128] + two[:, 128:] + dot_nn(low, feats[g, :, :128])
                norms = dot_nn(sq_high, ones_rot[...]) + dot_nn(sq_low, ones_rot[...])
                p = jnp.exp(logits - 0.5 * norms) * (32**-0.5)
                rot_ref[r, 256 * g : 256 * g + 256] = high
                feat_ref[r, 128 * g : 128 * g + 128] = p.astype(BF16)
            return 0

        lax.fori_loop(0, padded // TILE_F, body, 0)

    def values(groups):
        def body(i, _):
            r = rows(i, 832)
            for g in groups:
                vv[r, 256 * g : 256 * g + 256] = dot_nn(normed[r, :], block(3 + g)).astype(BF16)
            return 0

        run(0, padded // 832, body)

    need(0)
    features(0, rotk, pk, (0, 1))
    tick()
    need(1)
    features(0, rotk, pk, (2,))
    values((0,))
    tick()
    need(2)
    values((1, 2))
    tick()
    need(3)
    features(6, rotq, pq, (0, 1))
    tick()
    need(4)
    features(6, rotq, pq, (2,))
    tick()
    here = pl.ds(0, tokens_here)
    spill = pltpu.make_async_copy(normed.at[here], dx_hbm, local.at[1])
    spill.start()
    hat2 = normed

    window = 224

    def places(s):
        begin = lax.div(s * length, 16) * 16
        pos = lax.broadcasted_iota(jnp.int32, (window, 1), 0) - (s * length - begin)
        valid = (pos >= 0) & (pos < length)
        live = valid & (pos < lengths[s])
        return pl.ds(pl.multiple_of(begin, 16), window), pos, valid, live

    def state_of(g, w, live, pkm):
        ones = jnp.ones((window, 256), BF16)
        diag = diagonal[...]
        st = (dot_tn(pkm, vv[w, 256 * g : 256 * g + 256]) * diag).astype(BF16)
        tot = dot_tn(pkm, ones) * diag
        tot_high, tot_low = split_low(tot)
        return st, tot_high, tot_low

    def masked_keys(g, w, live):
        keys = pk[w, 128 * g : 128 * g + 128].astype(F32)
        return jnp.where(live, keys, 0.0)

    def attend(s, _):
        w, pos, valid, live = places(s)
        mixes = []
        for g in range(3):
            pkm = masked_keys(g, w, live).astype(BF16)
            st, tot_high, tot_low = state_of(g, w, live, pkm)
            pqg = pq[w, 128 * g : 128 * g + 128]
            num = dot_nn(pqg, st)
            den = dot_nn(pqg, tot_high) + dot_nn(pqg, tot_low)
            mixes.append(jnp.where(valid, num / den, 0.0))
        mix = jnp.where(pos < 0, mixed[w, :].astype(F32), jnp.concatenate(mixes, 1))
        mixed[w, :] = mix.astype(BF16)
        return 0

    for k in range(4):
        lax.fori_loop(2 * k, 2 * k + 2, attend, 0, unroll=2)
        tick()
    need(5)
    spill.wait()

    spill_mixed = pltpu.make_async_copy(mixed.at[here], out_hbm, local.at[2])
    spill_mixed.start()

    def project(i, _):
        r = rows(i, TILE_P)
        branch = dot_nn(mixed[r, :], blocks(9))
        middle = xb[r, :].astype(F32) + branch
        acc[r, :] = middle
        hat, inverse = norm(middle)
        hat2[r, :] = hat.astype(BF16)
        inv2[r, :] = jnp.broadcast_to(inverse, (TILE_P, 128))
        second[r, :] = (hat * prm[2:3, :] + prm[3:4, :]).astype(BF16)
        dsec[r, :] = jnp.zeros((TILE_P, 768), F32)
        return 0

    half = padded // TILE_P // 2
    lax.fori_loop(0, half, project, 0)
    load_dy(0).start()
    tick()
    lax.fori_loop(half, 2 * half, project, 0)

    def turn(src):
        for j in range(6):
            tb[128 * j : 128 * j + 128, :] = src[:, 128 * j : 128 * j + 128].T

    load_dy(1).start()
    turn(second)
    load_dy(0).wait()
    load_dy(1).wait()
    spill_mixed.wait()
    while state["tick"] <= last[0] + lags[0]:
        tick()
    need(6)
    need(7)

    def pair_of(q):
        up, down = 6 + 2 * q, 7 + 2 * q
        return (
            Gather(at, wu.at[6 + q], ag_send.at[up], ag_recv.at[up]),
            Gather(at, wd.at[q], ag_send.at[down], ag_recv.at[down]),
        )

    def gather_on(q, phase):
        @pl.when(q < 6)
        def _():
            for unit in pair_of(q):
                if phase:
                    unit.arrived(phase - 1)
                unit.start(phase)

    su, sd = wu.at[6, 0], wu.at[6, 1]
    s2u, s2d = wu.at[7, 0, :, 0], wu.at[7, 0, :, 1]
    s3u, s3d = wu.at[7, 1, :, 0, 0], wu.at[7, 1, :, 0, 1]
    lane_u = Reduce(at, (ru, b1u, su, b2u, s2u, b3u, s3u, b4u), us, ur)
    lane_d = Reduce(at, (rd, b1d, sd, b2d, s2d, b3d, s3d, b4d), ds_, dr)

    def post(flat, par, unit):
        return remote(
            flat.at[par, 1 - at.c], res_u.at[unit, at.c], qs.at[unit], qr.at[unit], at.sib
        )

    def emit_pair(flat, total, par, unit):
        flat[par] = total.reshape(flat.shape[1:])
        res_u[unit, at.c] = flat[par, at.c]
        post(flat, par, unit).start()

    def emit_own(total, unit):
        for b in range(3):
            r = pl.ds(pl.multiple_of(16 * unit, 16), 16)
            down_out[r, 256 * b : 256 * b + 256] = total[16 * b : 16 * b + 16]

    def keep(lane, half, grad):
        lane.R[half] = grad.astype(BF16).reshape(4, 2, 2, 48, 256)

    slope = 0.7978845608028654
    bend = 0.044715

    def up_block(ch):
        return jnp.concatenate([wu[6 + ch, h].reshape(768, 256) for h in range(2)], 1)

    def chunk(ch, _):
        def inner(i, _):
            r = rows(i, 416)
            lines, cot = second[r, :], xb[r, :]
            pres = dot_nn(lines, up_block(ch))
            dhs = dot_nt(cot, wd[ch].reshape(512, 768))
            for h in range(2):
                pre = pres[:, 256 * h : 256 * h + 256]
                dh = dhs[:, 256 * h : 256 * h + 256]
                square = pre * pre
                t = jnp.tanh(pre * (slope + slope * bend * square))
                half = 0.5 + 0.5 * t
                col = slice(256 * h, 256 * h + 256)
                hid[r, col] = (pre * half).astype(BF16)
                bent = slope + 3.0 * slope * bend * square
                grad = half + 0.5 * pre * (1.0 - t * t) * bent
                dpre[r, col] = (dh * grad).astype(BF16)
            return 0

        @pl.when(ch >= 1)
        def _():
            for unit in pair_of(ch):
                unit.arrived(3)

        run(0, 4, inner)
        for phase in (3, 2, 1, 0):
            gather_on(ch + 4 + AHEAD - phase, phase)
        par = lax.rem(ch, 2)
        for k in (1, 2):

            @pl.when(ch == k)
            def _():
                units[4 + 2 * k].sent()

        for phase in (4, 3, 2, 1):
            j = ch - phase

            @pl.when(j >= 0)
            def _():
                old = lax.rem(j + 8, 2)
                if phase == 4:

                    @pl.when(j >= 2)
                    def _():
                        post(flu, old, j - 2).wait_send()

                up_total = lane_u.step(phase, old, before=j >= 1)
                down_total = lane_d.step(phase, old, before=j >= 1)
                if phase == 4:
                    emit_pair(flu, up_total, old, j)
                    emit_own(down_total, j)

        @pl.when(ch >= 1)
        def _():
            lane_u.wait_sent(0, 1 - par)
            lane_d.wait_sent(0, 1 - par)

        grads = dot_nn(tb[:768, :], dpre[...])
        keep(lane_u, 0, grads[:, :256])
        keep(lane_u, 1, grads[:, 256:])
        grads = dot_tn(hid[:, 0:512], xb[...]).astype(BF16)
        for h in range(2):
            for b in range(3):
                part = grads[256 * h : 256 * h + 256, 256 * b : 256 * b + 256]
                rd[h, :, :, :, 16 * b : 16 * b + 16, :] = part.reshape(4, 2, 2, 16, 256)
        lane_u.start(0, par)
        lane_d.start(0, par)

        def outer(i, _):
            r = rows(i, 832)
            acc[r, :] += dot_nn(hid[r, 0:512], wd[ch].reshape(512, 768))
            dsec[r, :] += dot_nt(dpre[r, :], up_block(ch))
            return 0

        run(0, 2, outer)
        return 0

    lax.fori_loop(0, 6, chunk, 0)
    fetch_mixed = pltpu.make_async_copy(out_hbm, mixed.at[here], local.at[2])
    fetch_mixed.start()

    def drain(lane, phase, j):
        par = j % 2
        pairs = lane is lane_u or j >= 6
        flat = flu if lane is lane_u else fld
        unit = j if lane is lane_u else j + 3
        if phase == 4 and pairs and (lane is lane_u or j >= 8):
            post(flat, par, unit - 2).wait_send()
        total = lane.step(phase, par)
        if phase == 4:
            if pairs:
                emit_pair(flat, total, par, unit)
            else:
                emit_own(total, j)

    def both(*steps):
        for phase, j in steps:
            drain(lane_u, phase, j)
            drain(lane_d, phase, j)

    both((4, 2), (3, 3), (2, 4), (1, 5))

    def second_back(i, _):
        r = rows(i, TILE_S)
        e = dsec[r, :]
        hat = hat2[r, :].astype(F32)
        inverse = inv2[r, :][:, :1]
        lng[2:3, :] += jnp.sum(e * hat, 0, keepdims=True)
        lng[3:4, :] += jnp.sum(e, 0, keepdims=True)
        eg = e * prm[2:3, :]
        m1 = jnp.mean(eg, -1, keepdims=True)
        m2 = jnp.mean(eg * hat, -1, keepdims=True)
        dmid = xb[r, :].astype(F32) + inverse * (eg - m1 - hat * m2)
        dsec[r, :] = dmid
        low = dmid.astype(BF16)
        second[r, :] = low
        hat2[r, :] = acc[r, :].astype(BF16)
        acc[r, :] = dot_nt(low, blocks(9))
        return 0

    half = padded // TILE_S // 2
    lax.fori_loop(0, half, second_back, 0)
    both((4, 3), (3, 4), (2, 5))
    lax.fori_loop(half, 2 * half, second_back, 0)
    store_out = pltpu.make_async_copy(hat2.at[pl.ds(0, tokens_here)], out_hbm, local.at[0])
    fetch_mixed.wait()
    store_out.start()
    load_x = pltpu.make_async_copy(x_hbm, xb.at[pl.ds(0, tokens_here)], local.at[2])
    load_x.start()

    def weight_grad(lane, j, parts):
        lane.wait_sent(0, 1 - j % 2)
        for h, (ref, col, base) in enumerate(parts):

            @pl.when(at.z >= 0)
            def _():
                keep(lane, h, grad_of(ref, col, base))

        lane.start(0, j % 2)

    def grad_of(ref, col, base):
        lines = ref[:, 256 * col : 256 * col + 256]
        if base is None:
            return dot_nn(tb[:768, :], lines)
        both_of = dot_nn(tb[...], lines)
        grad, sums = both_of[:768], both_of[768:769]
        weight = block(base + col).astype(F32)
        share = weight * grad
        gain_col[...] += share[:, :128] + share[:, 128:]
        share = weight * sums
        shift_col[...] += share[:, :128] + share[:, 128:]
        return grad

    gain_col, shift_col = inv2.at[0:768], inv2.at[768:1536]
    inv2[0:1536, :] = jnp.zeros((1536, 128), F32)
    turn(mixed)
    fetch = pltpu.make_async_copy(dx_hbm, mixed.at[here], local.at[1])
    fetch.start()
    both((4, 4), (3, 5))
    weight_grad(lane_u, 6, ((second, 0, None), (second, 1, None)))

    def attend_back(s, _):
        w, pos, valid, live = places(s)
        olds = [acc[w, 128 * j : 128 * j + 128] for j in range(6)]
        vals = [vv[w, 256 * g : 256 * g + 256] for g in range(3)]
        dq_parts, dk_parts, dv_parts = [], [], []
        for g in range(3):
            thin = slice(128 * g, 128 * g + 128)
            diag = diagonal[...]
            pk32 = masked_keys(g, w, live)
            pkm = pk32.astype(BF16)
            st, tot_high, tot_low = state_of(g, w, live, pkm)
            tot = jnp.sum(pk32, 0, keepdims=True)
            pqg = pq[w, thin]
            pq32 = jnp.where(valid, pqg.astype(F32), 0.0)
            num = dot_nn(pqg, st)
            den = dot_nn(pqg, tot_high) + dot_nn(pqg, tot_low)
            share = 1.0 / den
            part = jnp.concatenate([olds[2 * g], olds[2 * g + 1]], 1) * share
            dnum = jnp.where(valid, part, 0.0).astype(BF16)
            e_high, e_low = split_low(jnp.where(valid, -part * (num * share), 0.0))
            dden = dot_nn(e_high, ones_val[...]) + dot_nn(e_low, ones_val[...])
            dpq = dot_nt(dnum, st) + dden * tot
            dst = (dot_tn(pqg, dnum) * diag).astype(BF16)
            dtot = jnp.sum(dden * pq32, 0, keepdims=True)
            dpk = dot_nt(vals[g], dst) + dtot
            dv_parts.append(dot_nn(pkm, dst))
            dq_parts.append(dpq * pq32)
            dk_parts.append(dpk * pk32)
        for j, new in enumerate(dq_parts + dk_parts):
            acc[w, 128 * j : 128 * j + 128] = jnp.where(valid, new, olds[j])
        for g in range(3):
            new = jnp.where(valid, dv_parts[g], vals[g].astype(F32))
            vv[w, 256 * g : 256 * g + 256] = new.astype(BF16)
        return 0

    lax.fori_loop(0, mols // 2, attend_back, 0, unroll=2)
    both((4, 5))
    drain(lane_u, 1, 6)
    lax.fori_loop(mols // 2, mols, attend_back, 0, unroll=2)
    vv[tail, :] = jnp.zeros((spare, 768), BF16)
    drain(lane_u, 2, 6)
    lane_d.wait_sent(0, 1)
    keep(lane_d, 0, grad_of(second, 2, None))
    fetch.wait()
    turn(mixed)
    keep(lane_d, 1, grad_of(vv, 0, 3))
    lane_d.start(0, 0)
    weight_grad(lane_u, 7, ((vv, 1, 3), (vv, 2, 3)))
    drain(lane_u, 3, 6)

    def unpick(lines, pick):
        high, rest = lines.astype(BF16), lines
        parts = [high]
        for _ in range(2):
            rest = rest - parts[-1].astype(F32)
            parts.append(rest.astype(BF16))
        count = lines.shape[0]
        wide = jnp.concatenate([part.astype(F32) for part in parts], 0).astype(BF16)
        out = pick(wide)
        return out[:count] + out[count : 2 * count] + out[2 * count :]

    def features_back(rot_ref, base):
        def body(i, _):
            r = rows(i, TILE_FB)
            ct, sn = cosine[r, :], sine[r, :]
            for g in range(3):
                wide = slice(256 * g, 256 * g + 256)
                high, low = split_low(acc[r, base + 128 * g : base + 128 * g + 128])
                rot = rot_ref[r, wide].astype(F32)
                total = dot_nt(high, ones_rot[...]) + dot_nt(low, ones_rot[...])
                back = dot_nt(jnp.concatenate([high, high], 1), feats[g])
                back = back + dot_nt(low, feats[g, :, :128]) - rot * total
                a, b = back[:, :128], back[:, 128:]
                turned = jnp.concatenate([a * ct + b * sn, b * ct - a * sn], 1)
                rot_ref[r, wide] = turned.astype(BF16)
            return 0

        lax.fori_loop(0, padded // TILE_FB, body, 0)

    features_back(rotk, 384)
    drain(lane_d, 1, 6)
    drain(lane_u, 4, 6)
    drain(lane_u, 1, 7)
    weight_grad(lane_d, 7, ((rotk, 0, 0), (rotk, 1, 0)))
    features_back(rotq, 0)
    drain(lane_d, 2, 6)
    drain(lane_u, 2, 7)
    drain(lane_d, 1, 7)
    weight_grad(lane_u, 8, ((rotk, 2, 0), (rotq, 0, 6)))
    drain(lane_d, 3, 6)
    drain(lane_u, 3, 7)
    weight_grad(lane_d, 8, ((rotq, 1, 6), (rotq, 2, 6)))
    shift_row = jnp.sum(shift_col[...].T, 0, keepdims=True)
    gain_row = jnp.sum(gain_col[...].T, 0, keepdims=True)
    gain_row = (gain_row - prm[1:2, :] * shift_row) / prm[0:1, :]
    ends = jnp.concatenate([gain_row, shift_row, lng[2:8, :]], 0)
    ends = jnp.concatenate([ends, jnp.zeros((8, 128), F32)], 1)
    for i in range(32):
        k, shift = (24 * i) // 128, (24 * i) % 128
        pair = ends[:, 128 * k : 128 * k + 256]
        if shift:
            pair = pltpu.roll(pair, 256 - shift, 1)
        rp[i % 2, i // 8, (i // 4) % 2, (i // 2) % 2] = pair[:, :128]
    lane_p = Reduce(at, (rp, b1p, sp, b2p, s2p, b3p, s3p, b4p), ps, pr)
    lane_p.start(0, 0)
    drain(lane_d, 4, 6)
    drain(lane_u, 4, 7)
    drain(lane_d, 2, 7)
    drain(lane_u, 1, 8)
    for unit in range(6):
        post(flu, 0, unit).wait_recv()
    lines = []
    for i in range(4):
        cols = slice(64 * i, 64 * i + 64)
        lines.append(jnp.concatenate([res_u[ch, h, :, cols] for ch in range(6) for h in range(2)], 1))
    hidden_pick()

    def hidden_back(wide):
        out = dot_nt(wide[:, :256], picks[0][...])
        out = out + dot_nt(wide[:, 256:512], picks[1][...])
        return out + dot_nt(wide[:, 512:], picks[2][...])

    back = unpick(jnp.concatenate(lines, 0), hidden_back)
    for i in range(4):
        up_out[:, 768 * i : 768 * i + 768] = back[24 * i : 24 * i + 24]

    def first_back(i, _):
        r = rows(i, TILE_B)
        dn = jnp.zeros((TILE_B, 768), F32)
        for base, ref in ((0, rotk), (3, vv), (6, rotq)):
            for g in range(3):
                dn = dn + dot_nt(ref[r, 256 * g : 256 * g + 256], block(base + g))
        hat, inverse = norm(xb[r, :].astype(F32))
        eg = dn * prm[0:1, :]
        m1 = jnp.mean(eg, -1, keepdims=True)
        m2 = jnp.mean(eg * hat, -1, keepdims=True)
        mixed[r, :] = (dsec[r, :] + inverse * (eg - m1 - hat * m2)).astype(BF16)
        return 0

    load_x.wait()
    tiles = padded // TILE_B

    def store_dx(q):
        count = padded // 4
        r = pl.ds(count * q, count if q < 3 else tokens_here - 3 * count)
        return pltpu.make_async_copy(mixed.at[r], dx_hbm.at[r], local.at[4 + q])

    quarter = tiles // 4
    lax.fori_loop(0, quarter, first_back, 0)
    store_dx(0).start()
    drain(lane_d, 3, 7)
    drain(lane_u, 2, 8)
    drain(lane_d, 1, 8)
    lane_p.step(1, 0, before=False)
    lax.fori_loop(quarter, 2 * quarter, first_back, 0)
    store_dx(1).start()
    drain(lane_d, 4, 7)
    drain(lane_u, 3, 8)
    drain(lane_d, 2, 8)
    lane_p.step(2, 0, before=False)
    lax.fori_loop(2 * quarter, 3 * quarter, first_back, 0)
    store_dx(2).start()
    drain(lane_u, 4, 8)
    drain(lane_d, 3, 8)
    lane_p.step(3, 0, before=False)
    lax.fori_loop(3 * quarter, tiles, first_back, 0)
    store_dx(3).start()
    drain(lane_d, 4, 8)
    params_out[...] = lane_p.step(4, 0)
    for phase in range(4):
        lane_p.wait_sent(phase, 0)
        lane_u.wait_sent(phase, 0)
        lane_d.wait_sent(phase, 0)
    for flat, par, unit in ((flu, 1, 7), (flu, 0, 8), (fld, 1, 10), (fld, 0, 11)):
        post(flat, par, unit).wait_send()
    for unit in range(6, 12):
        post(flu, 0, unit).wait_recv()
    for u, unit in enumerate(units):
        if u not in (6, 8):
            unit.sent()
    params.sent()
    turned = unpick(
        jnp.concatenate(
            [res_u[u, h] for u, h in ((10, 0), (10, 1), (8, 0), (8, 1), (11, 0), (11, 1))], 0
        ),
        lambda wide: dot_nt(wide, halves_pick()),
    )
    for g in range(3):
        here_k, here_v, here_q, here_o = (slice(k + 256 * g, k + 256 * g + 256) for k in range(0, 3072, 768))
        wide_out[:, here_k] = turned[24 * g : 24 * g + 24]
        wide_out[:, here_q] = turned[72 + 24 * g : 96 + 24 * g]
        u, h = ((9, 1), (7, 0), (7, 1))[g]
        wide_out[:, here_v] = res_u[u, h]
        u, h = ((6, 0), (6, 1), (9, 0))[g]
        wide_out[:, here_o] = res_u[u, h]
    store_out.wait()
    for q in range(4):
        store_dx(q).wait()


def fused_device(
    tokens,
    lengths,
    feature_directions,
    first_gain,
    first_shift,
    query_weight,
    key_weight,
    value_weight,
    out_weight,
    second_gain,
    second_shift,
    up_weight,
    down_weight,
    out_cotangent,
):
    tokens_here, width = tokens.shape
    mols = lengths.shape[0]
    length = tokens_here // mols
    padded = -(-tokens_here // 416) * 416
    share = first_gain.shape[0]

    vectors = jnp.stack([first_gain, first_shift, second_gain, second_shift]).astype(F32)
    params = jnp.pad(vectors, ((0, 4), (0, 128 - share)))

    frequency = np.float32(10000.0) ** (-np.arange(32, dtype=np.float32) * np.float32(2.0 / 64))
    angles = (np.arange(padded) % length).astype(np.float32)[:, None] * frequency[None, :]
    scale = 64.0**-0.25
    cosine = jnp.asarray(np.tile(np.cos(angles) * scale, (1, 4)), F32)
    sine = jnp.asarray(np.tile(np.sin(angles) * scale, (1, 4)), F32)
    lane_head = np.arange(128) // 32
    ones_rot = jnp.asarray(np.tile(lane_head, 2)[:, None] == lane_head[None, :], BF16)
    value_head = np.arange(256) // 64
    ones_val = jnp.asarray(value_head[:, None] == lane_head[None, :], BF16)
    diagonal = jnp.asarray(lane_head[:, None] == value_head[None, :], F32)

    def vm(shape, kind):
        return pltpu.VMEM(shape, kind)

    def lane(block, kind, sums):
        shapes = [(2, 4, 2, 2), (2, 4, 2, 2), (2, 4, 2), (2, 4), (2, 3)]
        if sums:
            shapes = [(2, 4, 2, 2), (2, 4, 2, 2), (4, 2, 2), (2, 4, 2), (4, 2), (2, 4), (4,), (2, 3)]
        return [vm(shape + block, kind) for shape in shapes]

    rows16 = (padded, width)
    scratch = [
        vm((12, 2, 4, 2, 2, 48, 256), BF16),
        vm((6, 2, 4, 2, 2, 16, 768), BF16),
        vm((2, 4, 2, 2, 8, 128), F32),
        vm((12, 24, 256), F32),
        vm(rows16, BF16),
        vm(rows16, BF16),
        vm(rows16, BF16),
        vm(rows16, BF16),
        vm(rows16, BF16),
        vm((padded, 384), BF16),
        vm((padded, 384), BF16),
        vm(rows16, BF16),
        vm(rows16, BF16),
        vm((padded, 128), F32),
        vm(rows16, F32),
        vm(rows16, F32),
        vm((padded, 512), BF16),
        vm((width + 16, padded), BF16),
        vm((8, width), F32),
        vm((8, width), F32),
    ]
    scratch += lane((48, 256), BF16, False) + [vm((2, 2, 24, 256), F32)] * 2
    scratch += lane((48, 256), BF16, False) + lane((8, 128), F32, True)
    scratch += [
        vm((12, 2, 24, 256), F32),
        pltpu.SemaphoreType.DMA((19, 8)),
        pltpu.SemaphoreType.DMA((19, 8)),
        pltpu.SemaphoreType.DMA((2,)),
        pltpu.SemaphoreType.DMA((2,)),
    ]
    scratch += [pltpu.SemaphoreType.DMA((2, 8))] * 6 + [pltpu.SemaphoreType.DMA((12,))] * 2
    scratch += [vm((padded, 128), F32)] * 2 + [vm((3, 256, 256), BF16)]
    scratch += [pltpu.SemaphoreType.DMA((8,))]
    spaces = [pl.ANY, pl.ANY, pltpu.SMEM] + [pltpu.VMEM] * 8 + [pl.ANY] * 2 + [pltpu.VMEM] * 3
    kernel = functools.partial(layer_kernel, (tokens_here, padded, length, mols))
    outs = pl.pallas_call(
        kernel,
        out_shape=[
            jax.ShapeDtypeStruct(tokens.shape, BF16),
            jax.ShapeDtypeStruct(tokens.shape, BF16),
            jax.ShapeDtypeStruct((share, 4 * width), F32),
            jax.ShapeDtypeStruct(up_weight.shape, F32),
            jax.ShapeDtypeStruct(down_weight.shape, F32),
            jax.ShapeDtypeStruct((8, 128), F32),
        ],
        in_specs=[pl.BlockSpec(memory_space=s) for s in spaces],
        out_specs=[pl.BlockSpec(memory_space=s) for s in [pl.ANY] * 2 + [pltpu.VMEM] * 4],
        scratch_shapes=scratch,
        compiler_params=pltpu.CompilerParams(
            collective_id=0, has_side_effects=True, vmem_limit_bytes=VMEM_BYTES
        ),
        name="encoder_layer",
    )(
        tokens,
        out_cotangent,
        lengths,
        params,
        key_weight,
        value_weight,
        query_weight,
        out_weight,
        up_weight,
        down_weight,
        feature_directions.transpose(0, 2, 1),
        cosine,
        sine,
        ones_rot,
        ones_val,
        diagonal,
    )
    output, input_grad, wide_grad, ups, downs, vector_grad = outs
    keys, values, queries, mixes = (
        wide_grad[:, width * k : width * k + width] for k in range(4)
    )
    vectors = [vector_grad[row, :share] for row in range(4)]
    return (
        output,
        input_grad,
        vectors[0],
        vectors[1],
        queries,
        keys,
        values,
        mixes,
        vectors[2],
        vectors[3],
        ups,
        downs,
    )


LAGS = (0, 2, 4, 6)
AHEAD = 1
TILE_F = 832
TILE_P = 416
TILE_S = 416
TILE_B = 208
TILE_FB = 416
VMEM_BYTES = 62 * 1024 * 1024


def solution(mesh):
    placed = (
        P("fsdp", None),
        P("fsdp"),
        P(),
        P("fsdp"),
        P("fsdp"),
        P("fsdp", None),
        P("fsdp", None),
        P("fsdp", None),
        P("fsdp", None),
        P("fsdp"),
        P("fsdp"),
        P("fsdp", None),
        P("fsdp", None),
        P("fsdp", None),
    )
    fused = mesh.shape["fsdp"] == 32
    return jax.shard_map(
        fused_device if fused else per_device,
        mesh=mesh,
        in_specs=placed,
        out_specs=(
            P("fsdp", None),
            P("fsdp", None),
            P("fsdp"),
            P("fsdp"),
            P("fsdp", None),
            P("fsdp", None),
            P("fsdp", None),
            P("fsdp", None),
            P("fsdp"),
            P("fsdp"),
            P("fsdp", None),
            P("fsdp", None),
        ),
        check_vma=False,
    )
```
